32 devices in a mesh: wide: 4 (over y, x), narrow: 8 (over z, core).
Axes of the slice: x: 2, y: 2, z: 4, core: 2. Of those that a mesh axis runs over, the one named last changes fastest.
Arguments:
- inputs: bfloat16 [32768, 1024], P(('wide', 'narrow')), may hold values from -6 to 6
- seg_ids: int32 [16, 2048], P('wide'), may hold values from 0 to 7, never falling along the last dimension, each value on 1 to 1024 neighbouring positions
- buckets: int32 [2048], replicated, may hold values from 0 to 31, as said below
- norm1_gain: float32 [1024], replicated, may hold values from 0.5 to 1.5
- norm1_shift: float32 [1024], replicated, may hold values from -1 to 1
- w_query: bfloat16 [1024, 1024], P('narrow'), may hold values from -0.1875 to 0.1875
- w_key: bfloat16 [1024, 1024], P('narrow'), may hold values from -0.1875 to 0.1875
- w_value: bfloat16 [1024, 1024], P('narrow'), may hold values from -0.1875 to 0.1875
- w_out: bfloat16 [1024, 1024], P('narrow'), may hold values from -1 to 1
- norm2_gain: float32 [1024], replicated, may hold values from 0.5 to 1.5
- norm2_shift: float32 [1024], replicated, may hold values from -1 to 1
- w_up: bfloat16 [1024, 4096], P(None, 'narrow'), may hold values from -0.1875 to 0.1875
- w_down: bfloat16 [4096, 1024], P('narrow'), may hold values from -0.09375 to 0.09375
- rel_table: float32 [32, 16], P(None, 'narrow'), may hold values from -5 to 5
- out_grad: bfloat16 [32768, 1024], P(('wide', 'narrow')), may hold values from -6 to 6
Outputs:
- out: bfloat16 [32768, 1024], P(('wide', 'narrow'))
- input_grad: float32 [32768, 1024], P(('wide', 'narrow'))
- grad_norm1_gain: float32 [1024], replicated
- grad_norm1_shift: float32 [1024], replicated
- grad_query: float32 [1024, 1024], P('narrow')
- grad_key: float32 [1024, 1024], P('narrow')
- grad_value: float32 [1024, 1024], P('narrow')
- grad_out: float32 [1024, 1024], P('narrow')
- grad_norm2_gain: float32 [1024], replicated
- grad_norm2_shift: float32 [1024], replicated
- grad_up: float32 [1024, 4096], P(None, 'narrow')
- grad_down: float32 [4096, 1024], P('narrow')
- grad_table: float32 [32, 16], P(None, 'narrow')
The draws below stay inside these ranges and needn't reach their ends.
Inputs may be any that keep to these rules, and one draw needn't show every extreme that they name: `seg_ids`: ids never fall along a row; each clip holds 1 to 1024 tokens and some clip exactly that many. `buckets`: never falls with the distance; equals the distance below 16.
All inputs are finite; a program needn't handle non-finite values.
Results may differ from the reference program's by a relative error of at most 0.015.
Values may be sent and summed in bfloat16 or wider, within the bound.
No kernel may reach another device: no remote copies, remote signals or barrier semaphores. Data moves between devices by JAX's collectives and lax.ppermute only.
A program may use at most 384 MiB of HBM per device.

```python
import math
import jax
import jax.numpy as jnp
import numpy as np
from jax import lax

D = 1024
HEADS = 16
HD = 64
FF = 4096
BUCKETS = 32
LEN = 2048
BLOCK = 512
CLIPS = 8
ROWS_DEV = 4
ROWS = 16
TOKENS = 32768


def draw_buckets(key, part):
    key = jax.random.fold_in(key, 11)
    half = BUCKETS // 2
    edge_count = BUCKETS - half - 1
    order = jax.random.permutation(key, LEN - half - 1)
    edges = jnp.sort(order[:edge_count]) + half + 1
    distance = jnp.arange(LEN)
    far_bucket = half + jnp.sum((edges[None, :] <= distance[:, None]).astype(jnp.int32), axis=1)
    return jnp.where(distance < half, distance, far_bucket).astype(jnp.int32)


def shard_levels(key, shape, split, smallest, largest):
    loudness = 1.0
    for dim, parts in split:
        draws = jax.random.uniform(jax.random.fold_in(jax.random.fold_in(key, 6), dim), (parts,), jnp.float32, smallest / len(split), largest / len(split))
        loudness = loudness * jnp.repeat(jnp.exp(draws), shape[dim] // parts).reshape((-1,) + (1,) * (len(shape) - 1 - dim))
    return loudness


def split_up(amount, total, limit, lean):
    loads = [(1 << 20) // math.isqrt(grade ** lean) + 1 for grade in range(2, amount + 1)]
    surplus, counts = total - limit - (amount - 1), [1] * (amount - 1)
    while surplus > 0:
        free = [i for i in range(amount - 1) if counts[i] < limit]
        pool, budget = sum([loads[i] for i in free]), surplus
        for i in free:
            addition = min(limit - counts[i], max(1, budget * loads[i] // pool), surplus)
            counts[i] = counts[i] + addition
            surplus = surplus - addition
    return np.array([limit] + counts)


def uneven(rng, amount, total, reach, slope):
    if amount == 2:
        one = jax.random.randint(rng, (), max(1, total - reach), min(reach, total - 1) + 1)
        return jnp.stack([one, total - one])
    tallies = jnp.asarray(split_up(amount, total, reach, slope), jnp.int32)
    couples = (amount - 1) // 2
    donor, receiver = tallies[1:1 + 2 * couples:2], tallies[2:2 + 2 * couples:2]
    margin = jnp.minimum(donor - 1, reach - receiver)
    shifted = jax.random.randint(jax.random.fold_in(rng, 1), (couples,), 0, 1 << 20) % (margin + 1)
    tallies = tallies.at[1:1 + 2 * couples:2].set(donor - shifted).at[2:2 + 2 * couples:2].set(receiver + shifted)
    return tallies[jax.random.permutation(jax.random.fold_in(rng, 2), amount)]


def normal_values(rng, shape, deviation, most, cuts=(), dtype=jnp.bfloat16):
    level = shard_levels(rng, shape, cuts, -0.22, 0.18) if cuts else 1.0
    array = jax.random.normal(rng, shape, jnp.float32) * deviation * level
    return jnp.minimum(jnp.maximum(array, -most), most).astype(dtype)


def setup_inputs(seed: int = 0) -> dict:
    splits = jax.random.split(jax.random.key(seed), 16)
    return {
        "inputs": normal_values(splits[0], (TOKENS, D), 1.0, 6.0, ((0, 32),)),
        "seg_ids": jax.vmap(lambda own: jnp.searchsorted(jnp.cumsum(uneven(own, CLIPS, LEN, LEN // 2, 1)), jnp.arange(LEN), side="right"))(jax.random.split(splits[1], ROWS)).reshape((ROWS, LEN)).astype(jnp.int32),
        "buckets": draw_buckets(jax.random.fold_in(splits[15], 71), 0),
        "norm1_gain": jnp.clip(1.0 + 0.1 * jax.random.normal(splits[3], (D,), jnp.float32), 0.5, 1.5),
        "norm1_shift": normal_values(splits[4], (D,), 0.2, 1.0, (), jnp.float32),
        "w_query": normal_values(splits[5], (D, D), D ** -0.5, 0.1875, ((0, 8),)),
        "w_key": normal_values(splits[6], (D, D), D ** -0.5, 0.1875, ((0, 8),)),
        "w_value": normal_values(splits[7], (D, D), D ** -0.5, 0.1875, ((0, 8),)),
        "w_out": normal_values(splits[8], (D, D), (D // 32) ** -0.5, 1.0, ((0, 8),)),
        "norm2_gain": jnp.clip(1.0 + 0.1 * jax.random.normal(splits[9], (D,), jnp.float32), 0.5, 1.5),
        "norm2_shift": normal_values(splits[10], (D,), 0.2, 1.0, (), jnp.float32),
        "w_up": normal_values(splits[11], (D, FF), D ** -0.5, 0.1875, ((1, 8),)),
        "w_down": normal_values(splits[12], (FF, D), FF ** -0.5, 0.09375, ((0, 8),)),
        "rel_table": normal_values(splits[13], (BUCKETS, HEADS), 1.0, 5.0, ((1, 8),), jnp.float32),
        "out_grad": normal_values(splits[14], (TOKENS, D), 1.0, 6.0, ((0, 32),)),
    }


EPSILON = 1e-05
MASKED_SCORE = -1e+30

@jax.custom_vjp
def low(v):
    return lax.optimization_barrier(v.astype(jnp.bfloat16)).astype(jnp.float32)

@jax.custom_vjp
def low_back(v):
    return v

def low_keep(v):
    return (low(v), None)

def low_pass(kept, grad):
    return (grad,)

def back_keep(v):
    return (v, None)

def back_low(kept, grad):
    return (low(grad),)
low.defvjp(low_keep, low_pass)
low_back.defvjp(back_keep, back_low)

def matmul(left, right):
    return jnp.dot(left, right, precision=lax.Precision.HIGHEST, preferred_element_type=jnp.float32)

def normalize(values, gain, shift):
    mean = lax.optimization_barrier(jnp.mean(values, axis=1, keepdims=True))
    centred = values - mean
    spread = lax.optimization_barrier(jnp.mean(centred * centred, axis=1, keepdims=True))
    return centred * lax.rsqrt(spread + EPSILON) * gain + shift

def attention(queries, keys, values, segments, extended):
    columns = jnp.arange(LEN)

    def one_block(index):
        start = (index * BLOCK).astype(jnp.int32)
        chosen = lax.dynamic_slice_in_dim(queries, start, BLOCK, 2)
        scores = jnp.einsum('ghqe,ghke->ghqk', chosen, keys, precision=lax.Precision.HIGHEST)
        rows = start + jnp.arange(BLOCK)
        offsets = rows[:, None] - columns[None, :] + LEN - 1
        bias = extended[offsets]
        scores = low_back(scores + jnp.transpose(bias, (2, 0, 1))[None])
        own = lax.dynamic_slice_in_dim(segments, start, BLOCK, 1)
        allowed = (own[:, :, None] == segments[:, None, :]) & (columns[None, :] <= rows[:, None])[None]
        scores = jnp.where(allowed[:, None], scores, MASKED_SCORE)
        top = lax.optimization_barrier(jnp.max(scores, axis=3, keepdims=True))
        expo = jnp.exp(scores - top)
        probs = low(expo / lax.optimization_barrier(jnp.sum(expo, axis=3, keepdims=True)))
        return jnp.einsum('ghqk,ghke->ghqe', probs, values, precision=lax.Precision.HIGHEST)
    blocks = lax.map(jax.checkpoint(one_block), jnp.arange(LEN // BLOCK).astype(jnp.int32))
    return jnp.moveaxis(blocks, 0, 2).reshape(queries.shape)

def layer(values_in, params, segments, bucket_ids):
    gain1, shift1, w_query, w_key, w_value, w_out, gain2, shift2, w_up, w_down, table = params
    groups = segments.shape[0]
    scale = HD ** (-0.5)
    normed1 = low(normalize(values_in, gain1, shift1))

    def split_heads(matrix):
        return jnp.transpose(matrix.reshape(groups, LEN, HEADS, HD), (0, 2, 1, 3))
    queries = split_heads(low(low_back(matmul(normed1, w_query.T) * scale)))
    keys = split_heads(low(low_back(matmul(normed1, w_key.T))))
    values = split_heads(low(low_back(matmul(normed1, w_value.T))))
    extended = jnp.concatenate([jnp.zeros((LEN - 1, HEADS), jnp.float32), table[bucket_ids]], 0)
    mixed = attention(queries, keys, values, segments, extended)
    mixed = low(low_back(jnp.transpose(mixed, (0, 2, 1, 3)).reshape(groups * LEN, D)))
    hidden_state = values_in + low_back(matmul(mixed, w_out))
    normed2 = low(normalize(hidden_state, gain2, shift2))
    active = low(jax.nn.gelu(low_back(matmul(normed2, w_up))))
    return hidden_state + low_back(matmul(active, w_down))

def reference(inputs, seg_ids, buckets, norm1_gain, norm1_shift, w_query, w_key, w_value, w_out, norm2_gain, norm2_shift, w_up, w_down, rel_table, out_grad):
    params = (norm1_gain, norm1_shift, w_query.astype(jnp.float32), w_key.astype(jnp.float32), w_value.astype(jnp.float32), w_out.astype(jnp.float32), norm2_gain, norm2_shift, w_up.astype(jnp.float32), w_down.astype(jnp.float32), rel_table)
    groups = seg_ids.shape[0] // ROWS_DEV
    inputs_grouped = inputs.astype(jnp.float32).reshape(groups, ROWS_DEV * LEN, D)
    grads_grouped = out_grad.astype(jnp.float32).reshape(groups, ROWS_DEV * LEN, D)
    segs_grouped = seg_ids.reshape(groups, ROWS_DEV, LEN)

    def one_group(totals, piece):
        group_in, group_grad, group_segs = piece

        def apply(values_in, weights):
            return layer(values_in, weights, group_segs, buckets)
        result, pullback = jax.vjp(apply, group_in, params)
        value_grad, weight_grad = pullback(group_grad)
        totals = jax.tree.map(jnp.add, totals, weight_grad)
        return (totals, (result.astype(jnp.bfloat16), value_grad))
    zeros = jax.tree.map(jnp.zeros_like, params)
    totals, (outputs, value_grads) = lax.scan(one_group, zeros, (inputs_grouped, grads_grouped, segs_grouped))
    return (outputs.reshape(TOKENS, D), value_grads.reshape(TOKENS, D), totals[0], totals[1], totals[2], totals[3], totals[4], totals[5], totals[6], totals[7], totals[8], totals[9], totals[10])
```

```python
import functools

import jax
import jax.numpy as jnp
from jax import lax
from jax.experimental import pallas as pl
from jax.experimental.pallas import tpu as pltpu
from jax.sharding import PartitionSpec as P

HD = 64
PAIR = 128
REACH = 1024
EPSILON = 1e-05
MASKED_SCORE = -1e30
NT = (((1,), (1,)), ((), ()))
TN = (((0,), (0,)), ((), ()))


def row_norm(values):
    mean = jnp.mean(values, axis=1, keepdims=True)
    centred = values - mean
    spread = jnp.mean(centred * centred, axis=1, keepdims=True)
    inverse = lax.rsqrt(spread + EPSILON)
    return (centred * inverse, inverse)


def norm_backward(upstream, normed, inverse, gain):
    scaled = upstream * gain
    mean_plain = jnp.mean(scaled, axis=1, keepdims=True)
    mean_cross = jnp.mean(scaled * normed, axis=1, keepdims=True)
    result = inverse * (scaled - mean_plain - normed * mean_cross)
    return (result, jnp.sum(upstream * normed, axis=0), jnp.sum(upstream, axis=0))


def dot_nt(left, right):
    return lax.dot_general(left, right, NT, preferred_element_type=jnp.float32)


def dot_nn(left, right):
    return jnp.dot(left, right, preferred_element_type=jnp.float32)


def dot_tn(left, right):
    return lax.dot_general(left, right, TN, preferred_element_type=jnp.float32)


def make_bias_tiles(line_ref, tiles_ref, block, reach_blocks):
    for h in range(2):
        for b in range(reach_blocks):
            line = line_ref[0, h : h + 1, b * block : (b + 2) * block]
            spread = jnp.broadcast_to(line, (block, 2 * block))
            rolled = pltpu.roll(spread, 0, 1, stride=1, stride_axis=0)
            tiles_ref[h, b] = rolled[:, block:]


def diagonal_line(tile, block):
    wide = jnp.concatenate([jnp.zeros((block, block), jnp.float32), tile], axis=1)
    rows = block
    while rows > 1:
        rows //= 2
        wide = wide[:rows] + pltpu.roll(wide[rows : 2 * rows], 2 * block - rows, 1)
    return wide


def place_of(index, me, per_slot):
    return ((index // per_slot) ^ me) * per_slot + index % per_slot


def head_lanes(block, h):
    lanes = lax.broadcasted_iota(jnp.int32, block.shape, 1)
    return jnp.where((lanes // HD) == h, block, jnp.zeros_like(block))


def attend_kernel(
    scalars, q_ref, k_ref, v_ref, first_ref, line_ref, out_ref, lse_ref, tiles, v_t, *, block, per_slot
):
    i = pl.program_id(1)
    me = scalars[0]
    low = scalars[1 + i]
    reach_blocks = tiles.shape[1]

    @pl.when(i == 0)
    def _():
        make_bias_tiles(line_ref, tiles, block, reach_blocks)
        v_t[...] = v_ref[...].T

    queries = q_ref[...]
    own = [head_lanes(queries, h) for h in range(2)]
    first = first_ref[...]
    key_index = lax.broadcasted_iota(jnp.int32, (block, block), 0)

    def step(t, carry):
        j = i - t
        start = pl.multiple_of(place_of(j, me, per_slot) * block, block)
        keys = k_ref[pl.ds(start, block), :]
        allowed = key_index >= (first - j * block)
        result = []
        for h in range(2):
            top, total, acc = carry[h]
            scores = dot_nt(keys, own[h]) + tiles[h, t]
            scores = jnp.where(allowed, scores, MASKED_SCORE)
            new_top = jnp.maximum(top, jnp.max(scores, axis=0, keepdims=True))
            shrink = jnp.exp(top - new_top)
            expo = jnp.exp(scores - new_top)
            total = total * shrink + jnp.sum(expo, axis=0, keepdims=True)
            values = v_t[h * HD : (h + 1) * HD, pl.ds(start, block)]
            acc = acc * shrink + dot_nn(values, expo.astype(jnp.bfloat16))
            result.append((new_top, total, acc))
        return tuple(result)

    zero = (
        jnp.full((1, block), MASKED_SCORE, jnp.float32),
        jnp.zeros((1, block), jnp.float32),
        jnp.zeros((HD, block), jnp.float32),
    )
    done = lax.fori_loop(0, i - low + 1, step, (zero, zero))
    both = jnp.concatenate([acc / total for _, total, acc in done], axis=0)
    out_ref[...] = both.T.astype(jnp.bfloat16)
    lse_ref[0] = jnp.concatenate([top + jnp.log(total) for top, total, _ in done], axis=0)


def attend_back_kernel(
    scalars,
    q_ref,
    k_ref,
    v_ref,
    up_ref,
    first_ref,
    line_ref,
    lse_ref,
    delta_ref,
    grad_ref,
    sums_ref,
    tiles,
    tile_sums,
    k_t,
    dk,
    dv,
    *,
    block,
    per_slot,
):
    i = pl.program_id(1)
    me = scalars[0]
    low = scalars[1 + i]
    reach_blocks = tiles.shape[1]

    @pl.when(i == 0)
    def _():
        make_bias_tiles(line_ref, tiles, block, reach_blocks)
        k_t[...] = k_ref[...].T
        dk[...] = jnp.zeros_like(dk)
        dv[...] = jnp.zeros_like(dv)
        tile_sums[...] = jnp.zeros_like(tile_sums)

    queries = q_ref[...]
    upstream = up_ref[...]
    own_q = [head_lanes(queries, h) for h in range(2)]
    own_up = [head_lanes(upstream, h) for h in range(2)]
    first = first_ref[...]
    key_index = lax.broadcasted_iota(jnp.int32, (block, block), 0)

    def step(t, carry):
        j = i - t
        start = pl.multiple_of(place_of(j, me, per_slot) * block, block)
        rows = pl.ds(start, block)
        keys = k_ref[rows, :]
        values = v_ref[rows, :]
        allowed = key_index >= (first - j * block)
        dq = []
        dk_new = dk[rows, :]
        dv_new = dv[rows, :]
        for h in range(2):
            scores = dot_nt(keys, own_q[h]) + tiles[h, t]
            scores = jnp.where(allowed, scores, MASKED_SCORE)
            probs = jnp.exp(scores - lse_ref[0, h : h + 1, :])
            prob_grad = dot_nt(values, own_up[h])
            score_grad = probs * (prob_grad - delta_ref[0, h : h + 1, :])
            tile_sums[h, t] += score_grad
            low_grad = score_grad.astype(jnp.bfloat16)
            dv_new = dv_new + dot_nn(probs.astype(jnp.bfloat16), own_up[h])
            dk_new = dk_new + dot_nn(low_grad, own_q[h])
            dq.append(carry[h] + dot_nn(k_t[h * HD : (h + 1) * HD, rows], low_grad))
        dk[rows, :] = dk_new
        dv[rows, :] = dv_new
        return tuple(dq)

    zero = jnp.zeros((HD, block), jnp.float32)
    dq = lax.fori_loop(0, i - low + 1, step, (zero, zero))
    here = pl.multiple_of(place_of(i, me, per_slot) * block, block)
    grad_ref[pl.ds(here, block), 0:PAIR] = jnp.concatenate(dq, axis=0).T.astype(jnp.bfloat16)

    @pl.when(i == pl.num_programs(1) - 1)
    def _():
        grad_ref[:, PAIR : 2 * PAIR] = dk[...].astype(jnp.bfloat16)
        grad_ref[:, 2 * PAIR :] = dv[...].astype(jnp.bfloat16)
        for h in range(2):
            for b in range(reach_blocks):
                sums_ref[0, h * reach_blocks + b : h * reach_blocks + b + 1, :] = diagonal_line(
                    tile_sums[h, b], block
                )


def attend(joined, first, lines, scalars, block, per_slot):
    length = joined.shape[0]
    pairs = joined.shape[1] // (3 * PAIR)
    blocks = length // block
    reach_blocks = lines.shape[2] // block - 1

    def spot(p, i, s):
        return (place_of(i, s[0], per_slot), 3 * p)

    grid_spec = pltpu.PrefetchScalarGridSpec(
        num_scalar_prefetch=1,
        grid=(pairs, blocks),
        in_specs=[
            pl.BlockSpec((block, PAIR), spot),
            pl.BlockSpec((length, PAIR), lambda p, i, s: (0, 3 * p + 1)),
            pl.BlockSpec((length, PAIR), lambda p, i, s: (0, 3 * p + 2)),
            pl.BlockSpec((1, block), lambda p, i, s: (0, i)),
            pl.BlockSpec((1, 2, lines.shape[2]), lambda p, i, s: (p, 0, 0)),
        ],
        out_specs=[
            pl.BlockSpec((block, PAIR), lambda p, i, s: (place_of(i, s[0], per_slot), p)),
            pl.BlockSpec((1, 2, block), lambda p, i, s: (p, 0, place_of(i, s[0], per_slot))),
        ],
        scratch_shapes=[
            pltpu.VMEM((2, reach_blocks, block, block), jnp.float32),
            pltpu.VMEM((PAIR, length), jnp.bfloat16),
        ],
    )
    tiles = pairs * 2 * blocks * 3
    return pl.pallas_call(
        functools.partial(attend_kernel, block=block, per_slot=per_slot),
        grid_spec=grid_spec,
        out_shape=[
            jax.ShapeDtypeStruct((length, pairs * PAIR), jnp.bfloat16),
            jax.ShapeDtypeStruct((pairs, 2, length), jnp.float32),
        ],
        compiler_params=pltpu.CompilerParams(vmem_limit_bytes=32 * 1024 * 1024),
        cost_estimate=pl.CostEstimate(
            flops=tiles * 4 * block**3, bytes_accessed=8 * length * PAIR * pairs, transcendentals=tiles * block**2
        ),
    )(scalars, joined, joined, joined, first, lines)


def attend_back(joined, upstream, first, lines, lse, delta, scalars, block, per_slot):
    length = joined.shape[0]
    pairs = joined.shape[1] // (3 * PAIR)
    blocks = length // block
    reach_blocks = lines.shape[2] // block - 1

    def row_spot(p, i, s):
        return (p, 0, place_of(i, s[0], per_slot))

    grid_spec = pltpu.PrefetchScalarGridSpec(
        num_scalar_prefetch=1,
        grid=(pairs, blocks),
        in_specs=[
            pl.BlockSpec((block, PAIR), lambda p, i, s: (place_of(i, s[0], per_slot), 3 * p)),
            pl.BlockSpec((length, PAIR), lambda p, i, s: (0, 3 * p + 1)),
            pl.BlockSpec((length, PAIR), lambda p, i, s: (0, 3 * p + 2)),
            pl.BlockSpec((block, PAIR), lambda p, i, s: (place_of(i, s[0], per_slot), p)),
            pl.BlockSpec((1, block), lambda p, i, s: (0, i)),
            pl.BlockSpec((1, 2, lines.shape[2]), lambda p, i, s: (p, 0, 0)),
            pl.BlockSpec((1, 2, block), row_spot),
            pl.BlockSpec((1, 2, block), row_spot),
        ],
        out_specs=[
            pl.BlockSpec((length, 3 * PAIR), lambda p, i, s: (0, p)),
            pl.BlockSpec((1, 2 * reach_blocks, 2 * block), lambda p, i, s: (p, 0, 0)),
        ],
        scratch_shapes=[
            pltpu.VMEM((2, reach_blocks, block, block), jnp.float32),
            pltpu.VMEM((2, reach_blocks, block, block), jnp.float32),
            pltpu.VMEM((PAIR, length), jnp.bfloat16),
            pltpu.VMEM((length, PAIR), jnp.float32),
            pltpu.VMEM((length, PAIR), jnp.float32),
        ],
    )
    tiles = pairs * 2 * blocks * 3
    return pl.pallas_call(
        functools.partial(attend_back_kernel, block=block, per_slot=per_slot),
        grid_spec=grid_spec,
        out_shape=[
            jax.ShapeDtypeStruct((length, pairs * 3 * PAIR), jnp.bfloat16),
            jax.ShapeDtypeStruct((pairs, 2 * reach_blocks, 2 * block), jnp.float32),
        ],
        compiler_params=pltpu.CompilerParams(vmem_limit_bytes=32 * 1024 * 1024),
        cost_estimate=pl.CostEstimate(
            flops=tiles * 10 * block**3, bytes_accessed=20 * length * PAIR * pairs, transcendentals=tiles * block**2
        ),
    )(scalars, joined, joined, joined, upstream, first, lines, lse, delta)


class Net:
    def __init__(self, wide, narrow, group):
        self.wide, self.narrow, self.group = wide, narrow, group
        self.ring = narrow // group
        self.bits = wide.bit_length() - 1

    def from_group(self, value, s):
        g = self.group
        return lax.ppermute(value, "narrow", [(i, (i // g) * g + ((i % g) ^ s)) for i in range(self.narrow)])

    def from_ring(self, value, r):
        if r == 0:
            return value
        g, z = self.group, self.ring
        return lax.ppermute(
            value, "narrow", [(i, ((i // g - r) % z) * g + i % g) for i in range(self.narrow)]
        )

    def to_ring(self, value, r):
        return self.from_ring(value, (self.ring - r) % self.ring)

    def from_wide(self, value, s):
        if s == 0:
            return value
        return lax.ppermute(value, "wide", [(i, i ^ s) for i in range(self.wide)])

    def bit_order(self, half):
        return [(b + half) % self.bits for b in range(self.bits)]

    def slot_order(self, half):
        order = [0]
        for b in self.bit_order(half):
            order = order + [s ^ (1 << b) for s in order]
        return order

    def spread(self, unit, half):
        pieces = [unit]
        for b in self.bit_order(half):
            pieces = pieces + [self.from_wide(piece, 1 << b) for piece in pieces]
        return pieces

    def halves(self):
        z = self.ring
        cut = max(z // 2, 1)
        return [list(range(cut)), list(range(cut, z))] if z > 1 else [[0]]

    def gather(self, quarter):
        slots = [self.from_ring(quarter, r) for r in range(self.ring)]
        result = []
        for half, places in enumerate(self.halves()):
            unit = jnp.stack([slots[r] for r in places], axis=0)
            result.append(self.spread(unit, half))
        return result

    def reduce(self, halves):
        total = None
        for half, places in enumerate(self.halves()):
            value = halves[half]
            for b in reversed(self.bit_order(half)):
                keep = value.shape[0] // 2
                arrived = self.from_wide(value[keep:], 1 << b)
                value = (value[:keep].astype(jnp.float32) + arrived.astype(jnp.float32)).astype(jnp.bfloat16)
            for at, r in enumerate(places):
                part = self.to_ring(value[0, at], r).astype(jnp.float32)
                total = part if total is None else total + part
        return total

    def share(self, own):
        me = lax.axis_index("wide")
        pieces = jnp.stack([self.from_wide(own, s) for s in range(self.wide)], axis=0)
        order = jnp.arange(self.wide) ^ me
        return jnp.take(pieces, order, axis=0)

    def total(self, value):
        for s in range(1, self.group):
            pass
        value = value + sum(self.from_group(value, s) for s in range(1, self.group))
        value = value + sum(self.from_ring(value, r) for r in range(1, self.ring))
        return value + sum(self.from_wide(value, s) for s in range(1, self.wide))


def on_device(
    inputs,
    seg_ids,
    buckets,
    norm1_gain,
    norm1_shift,
    w_query,
    w_key,
    w_value,
    w_out,
    norm2_gain,
    norm2_shift,
    w_up,
    w_down,
    rel_table,
    out_grad,
    *,
    wide,
    narrow,
):
    bf16, f32 = jnp.bfloat16, jnp.float32
    tokens, width = inputs.shape
    seqs, length = seg_ids.shape
    group = length // tokens
    net = Net(wide, narrow, group)
    ring = net.ring
    head_rows = w_query.shape[0]
    heads_here = rel_table.shape[1]
    piece_rows = head_rows // wide
    scale = HD ** (-0.5)
    block = min(256, tokens)
    per_slot = tokens // block
    blocks = length // block
    reach_blocks = min(blocks, -(-REACH // block) + 1)
    me_wide = lax.axis_index("wide")
    me_narrow = lax.axis_index("narrow")
    me_group = me_narrow % group
    me_ring = me_narrow // group
    halves = net.halves()

    def my_part(shard, axis=0):
        size = shard.shape[axis] // wide
        return lax.dynamic_slice_in_dim(shard, me_wide * size, size, axis)

    def all_group(own):
        return jnp.concatenate([own] + [net.from_group(own, s) for s in range(1, group)], axis=0)

    def group_sum(parts_of):
        away = [net.from_group(parts_of(s).astype(bf16), s) for s in range(1, group)]
        result = parts_of(0)
        for part in away:
            result = result + part.astype(f32)
        return result

    qkv_quarter = my_part(jnp.stack([w_query, w_key, w_value], axis=0), 1)
    qkv_halves = net.gather(qkv_quarter)
    table_slots = [net.from_ring(rel_table, r) for r in range(ring)]
    out_slots = [net.from_ring(w_out, r) for r in range(ring)]
    up_halves = net.gather(my_part(w_up, 1).T)
    down_halves = net.gather(my_part(w_down))

    values_in = inputs.astype(f32)
    normed1, inverse1 = row_norm(values_in)
    a1 = all_group((normed1 * norm1_gain + norm1_shift).astype(bf16))
    dy = all_group(out_grad)

    per_pair = PAIR // head_rows
    pairs = ring // per_pair

    def qkv_piece(r, t, s):
        for half, places in enumerate(halves):
            if r in places:
                at = net.slot_order(half).index(s)
                return qkv_halves[half][at][places.index(r), t]

    order = [
        (p * per_pair + r, t, s)
        for p in range(pairs)
        for t in range(3)
        for r in range(per_pair)
        for s in range(wide)
    ]
    w_joined = jnp.concatenate([qkv_piece(*spot) for spot in order], axis=0)
    column_kind = (jnp.arange(w_joined.shape[0]) // PAIR) % 3
    column_scale = jnp.where(column_kind == 0, jnp.asarray(scale, f32), jnp.asarray(1.0, f32))
    joined = (dot_nt(a1, w_joined) * column_scale).astype(bf16)

    reach = reach_blocks * block
    one_hot = (buckets[:reach, None] == jnp.arange(rel_table.shape[0])[None, :]).astype(f32)

    def head_of(r, h):
        return ((me_wide ^ (h * (HD // piece_rows))) * piece_rows) // HD

    table_here = jnp.concatenate(
        [
            lax.dynamic_slice_in_dim(table_slots[r], head_of(r, h), 1, 1)
            for r in range(ring)
            for h in range(heads_here)
        ],
        axis=1,
    )
    line = jnp.dot(one_hot, table_here, precision=lax.Precision.HIGHEST, preferred_element_type=f32).T
    lines = jnp.concatenate([jnp.full((line.shape[0], block), MASKED_SCORE, f32), line], axis=1)
    lines = lines.reshape(pairs, 2, block + reach)

    segments = lax.dynamic_slice_in_dim(seg_ids, me_ring, 1, 0)[0]
    first = jnp.sum((segments[None, :] < segments[:, None]).astype(jnp.int32), axis=1)
    scalars = jnp.concatenate([me_group[None], first[::block] // block]).astype(jnp.int32)
    first = first[None, :]

    mixed, lse = attend(joined, first, lines, scalars, block, per_slot)

    w_out_full = jnp.concatenate(
        [net_piece for r in range(ring) for net_piece in _xor_rows(out_slots[r], me_wide, wide)], axis=0
    )
    attended = group_sum(lambda s: dot_nn(mixed[s * tokens : (s + 1) * tokens], w_out_full))
    hidden_state = values_in + attended
    normed2, inverse2 = row_norm(hidden_state)
    a2 = all_group((normed2 * norm2_gain + norm2_shift).astype(bf16))

    w_up_t = jnp.concatenate([piece.reshape(-1, width) for part in up_halves for piece in part], axis=0)
    w_down_full = jnp.concatenate([piece.reshape(-1, width) for part in down_halves for piece in part], axis=0)
    up = dot_nt(a2, w_up_t)
    gelu_value, gelu_pull = jax.vjp(jax.nn.gelu, up)
    active = gelu_value.astype(bf16)
    up_grad = gelu_pull(dot_nt(dy, w_down_full))[0].astype(bf16)
    normed2_grad = group_sum(lambda s: dot_nn(up_grad[s * tokens : (s + 1) * tokens], w_up_t))
    grad_down = dot_tn(active, dy).astype(bf16)
    grad_up = dot_tn(up_grad, a2).astype(bf16)

    def in_halves(grad):
        result, at = [], 0
        for places in halves:
            size = grad.shape[0] * len(places) // ring
            result.append(grad[at : at + size].reshape(wide, len(places), -1, width))
            at += size
        return result

    down_part = net.reduce(in_halves(grad_down))
    up_part = net.reduce(in_halves(grad_up))

    feed = group_sum(lambda s: dot_nn(active[s * tokens : (s + 1) * tokens], w_down_full))
    out = (hidden_state + feed).astype(bf16)

    back2, grad_gain2, grad_shift2 = norm_backward(normed2_grad, normed2, inverse2, norm2_gain)
    state_grad = out_grad.astype(f32) + back2
    state_whole = all_group(state_grad.astype(bf16))
    mixed_grad = dot_nt(state_whole, w_out_full).astype(bf16)
    grad_out = dot_tn(mixed, state_whole).astype(bf16)
    heads = mixed.shape[1] // HD
    delta = jnp.sum((mixed.astype(f32) * mixed_grad.astype(f32)).reshape(length, heads, HD), axis=2)
    delta = delta.T.reshape(pairs, 2, length)
    joined_grad, tile_lines = attend_back(
        joined, mixed_grad, first, lines, lse, delta, scalars, block, per_slot
    )
    joined_grad = (joined_grad.astype(f32) * column_scale).astype(bf16)
    grad_joined = dot_tn(joined_grad, a1).astype(bf16)
    normed1_grad = group_sum(lambda s: dot_nn(joined_grad[s * tokens : (s + 1) * tokens], w_joined))

    def piece_of(r, t, s):
        at = order.index((r, t, s)) * piece_rows
        return grad_joined[at : at + piece_rows]

    def out_piece(r, s):
        at = r * head_rows + s * piece_rows
        return grad_out[at : at + piece_rows]

    attention_halves = [
        jnp.concatenate(
            [
                piece
                for s in net.slot_order(half)
                for r in places
                for piece in [piece_of(r, t, s) for t in range(3)] + [out_piece(r, s)]
            ],
            axis=0,
        ).reshape(wide, len(places), 4, piece_rows, width)
        for half, places in enumerate(halves)
    ]
    attention_part = net.reduce(attention_halves)

    back1, grad_gain1, grad_shift1 = norm_backward(normed1_grad, normed1, inverse1, norm1_gain)
    input_grad = state_grad + back1

    tile_lines = tile_lines.reshape(pairs * 2, reach_blocks, 2 * block)
    line_grad = tile_lines[:, :, block:].reshape(pairs * 2, reach)
    line_grad = line_grad.at[:, : reach - block].add(tile_lines[:, 1:, :block].reshape(pairs * 2, -1))
    table_grad = jnp.dot(line_grad, one_hot, precision=lax.Precision.HIGHEST, preferred_element_type=f32)
    all_heads = heads_here * narrow
    head_ids = jnp.stack(
        [
            ((me_ring + r) % ring * group + me_group) * heads_here + head_of(r, h)
            for r in range(ring)
            for h in range(heads_here)
        ]
    )
    placed = (jnp.arange(all_heads)[:, None] == head_ids[None, :]).astype(f32)
    table_all = jnp.dot(placed, table_grad, precision=lax.Precision.HIGHEST, preferred_element_type=f32)

    small = jnp.concatenate([grad_gain1, grad_shift1, grad_gain2, grad_shift2, table_all.reshape(-1)])
    pad = -small.shape[0] % 1024
    small = net.total(jnp.pad(small, (0, pad)).reshape(-1, 128)).reshape(-1)
    gain1, shift1, gain2, shift2 = (small[k * width : (k + 1) * width] for k in range(4))
    table_sum = small[4 * width : 4 * width + table_all.size].reshape(table_all.shape)
    table_out = lax.dynamic_slice_in_dim(table_sum, me_narrow * heads_here, heads_here, 0).T

    attention_all = net.share(attention_part.astype(bf16)).astype(f32)
    attention_all = jnp.moveaxis(attention_all, 1, 0).reshape(4, head_rows, width)
    down_all = net.share(down_part.astype(bf16)).astype(f32).reshape(-1, width)
    up_all = net.share(up_part.astype(bf16)).astype(f32).reshape(-1, width).T
    return (
        out,
        input_grad,
        gain1,
        shift1,
        attention_all[0],
        attention_all[1],
        attention_all[2],
        attention_all[3],
        gain2,
        shift2,
        up_all,
        down_all,
        table_out,
    )


def _xor_rows(matrix, me, count):
    rows = matrix.shape[0] // count
    return [lax.dynamic_slice_in_dim(matrix, (me ^ s) * rows, rows, 0) for s in range(count)]


def solution(mesh):
    placed = (
        P(("wide", "narrow"), None),
        P("wide", None),
        P(),
        P(),
        P(),
        P("narrow", None),
        P("narrow", None),
        P("narrow", None),
        P("narrow", None),
        P(),
        P(),
        P(None, "narrow"),
        P("narrow", None),
        P(None, "narrow"),
        P(("wide", "narrow"), None),
    )
    return jax.shard_map(
        functools.partial(on_device, wide=mesh.shape["wide"], narrow=mesh.shape["narrow"]),
        mesh=mesh,
        in_specs=placed,
        out_specs=(
            P(("wide", "narrow"), None),
            P(("wide", "narrow"), None),
            P(),
            P(),
            P("narrow", None),
            P("narrow", None),
            P("narrow", None),
            P("narrow", None),
            P(),
            P(),
            P(None, "narrow"),
            P("narrow", None),
            P(None, "narrow"),
        ),
        check_vma=False,
    )
```

```python
import functools

import jax
import jax.numpy as jnp
from jax import lax
from jax.experimental import pallas as pl
from jax.experimental.pallas import tpu as pltpu
from jax.sharding import PartitionSpec as P

HD = 64
PAIR = 128
REACH = 1024
EPSILON = 1e-05
MASKED_SCORE = -1e30
FORWARD_VMEM = 44 * 1024 * 1024
BACKWARD_VMEM = 52 * 1024 * 1024
FORWARD_FLOPS = 20_000_000_000
BACKWARD_FLOPS = 40_000_000_000
NT = (((1,), (1,)), ((), ()))
TN = (((0,), (0,)), ((), ()))


def row_norm(values):
    mean = jnp.mean(values, axis=1, keepdims=True)
    centred = values - mean
    spread = jnp.mean(centred * centred, axis=1, keepdims=True)
    inverse = lax.rsqrt(spread + EPSILON)
    return (centred * inverse, inverse)


def norm_backward(upstream, normed, inverse, gain):
    scaled = upstream * gain
    mean_plain = jnp.mean(scaled, axis=1, keepdims=True)
    mean_cross = jnp.mean(scaled * normed, axis=1, keepdims=True)
    result = inverse * (scaled - mean_plain - normed * mean_cross)
    return (result, jnp.sum(upstream * normed, axis=0), jnp.sum(upstream, axis=0))


def dot_nt(left, right):
    return lax.dot_general(left, right, NT, preferred_element_type=jnp.float32)


def dot_nn(left, right):
    return jnp.dot(left, right, preferred_element_type=jnp.float32)


def dot_tn(left, right):
    return lax.dot_general(left, right, TN, preferred_element_type=jnp.float32)


def make_strip(line_ref, strips, begin=0):
    for h in range(strips.shape[0]):
        spread = jnp.broadcast_to(line_ref[begin + h : begin + h + 1, :], strips.shape[1:])
        strips[h] = pltpu.roll(spread, 0, 1, stride=1, stride_axis=0)


def strip_line(strip):
    rows, span = strip.shape
    while rows > 1:
        rows //= 2
        strip = strip[:rows] + pltpu.roll(strip[rows : 2 * rows], span - rows, 1)
    return strip


def strip_at(t, u, rows, block):
    return pl.ds(pl.multiple_of(t * block + (block - u * rows), rows), block)


def strip_tile(strips, h, t, block):
    rows = strips.shape[1]
    parts = [strips[h, :, strip_at(t, u, rows, block)] for u in range(block // rows)]
    return jnp.concatenate(parts, axis=0)


def add_to_strip(strips, h, t, tile):
    rows, block = strips.shape[1], tile.shape[0]
    for u in range(block // rows):
        strips[h, :, strip_at(t, u, rows, block)] += tile[u * rows : (u + 1) * rows]


def place_of(index, me, per_slot):
    return ((index // per_slot) ^ me) * per_slot + index % per_slot


def head_lanes(block, h):
    lanes = lax.broadcasted_iota(jnp.int32, block.shape, 1)
    return jnp.where((lanes // HD) == h, block, jnp.zeros_like(block))


def columns_of(p, kind):
    return slice((3 * p + kind) * PAIR, (3 * p + kind + 1) * PAIR)


def attend_kernel(scalars, x_ref, first_ref, line_ref, out_ref, lse_ref, strips, v_t, kept, *, block, per_slot):
    i = pl.program_id(0)
    me = scalars[0]
    low = scalars[1 + i]
    heads = strips.shape[0]
    pairs = heads // 2

    @pl.when(i == 0)
    def _():
        make_strip(line_ref, strips)
        for p in range(pairs):
            v_t[p * PAIR : (p + 1) * PAIR] = x_ref[:, columns_of(p, 2)].T

    rows = pl.ds(pl.multiple_of(place_of(i, me, per_slot) * block, block), block)
    own = [head_lanes(x_ref[rows, columns_of(h // 2, 0)], h % 2) for h in range(heads)]
    first = first_ref[pl.ds(i, 1), :]
    key_index = lax.broadcasted_iota(jnp.int32, (block, block), 0)

    def rows_of(t):
        return pl.ds(pl.multiple_of(place_of(i - t, me, per_slot) * block, block), block)

    def fold(value):
        return value.reshape(block // 8, 8, block)

    def score_step(t, tops):
        here = rows_of(t)
        allowed = key_index >= (first - (i - t) * block)
        result = []
        for h in range(heads):
            scores = dot_nt(x_ref[here, columns_of(h // 2, 1)], own[h]) + strip_tile(strips, h, t, block)
            scores = jnp.where(allowed, scores, MASKED_SCORE)
            kept[h, t] = scores
            result.append(jnp.maximum(tops[h], jnp.max(fold(scores), axis=0)))
        return tuple(result)

    def value_step(t, carry):
        here = rows_of(t)
        result = []
        for h in range(heads):
            total, acc = carry[h]
            expo = jnp.exp(kept[h, t] - tops[h])
            total = total + jnp.sum(fold(expo), axis=0)
            acc = acc + dot_nn(v_t[h * HD : (h + 1) * HD, here], expo.astype(jnp.bfloat16))
            result.append((total, acc))
        return tuple(result)

    tops = lax.fori_loop(
        0, i - low + 1, score_step, (jnp.full((8, block), MASKED_SCORE, jnp.float32),) * heads
    )
    tops = [jnp.max(top, axis=0, keepdims=True) for top in tops]
    zero = (jnp.zeros((8, block), jnp.float32), jnp.zeros((HD, block), jnp.float32))
    done = lax.fori_loop(0, i - low + 1, value_step, (zero,) * heads)
    totals = [jnp.sum(total, axis=0, keepdims=True) for total, _ in done]
    for p in range(pairs):
        both = jnp.concatenate([done[h][1] / totals[h] for h in (2 * p, 2 * p + 1)], axis=0)
        out_ref[rows, p * PAIR : (p + 1) * PAIR] = both.T.astype(jnp.bfloat16)
    lse_ref[pl.ds(i, 1)] = jnp.concatenate([tops[h] + jnp.log(totals[h]) for h in range(heads)], axis=0)[None]


def attend_back_kernel(
    scalars,
    x_ref,
    mixed_ref,
    up_ref,
    first_ref,
    line_ref,
    lse_ref,
    grad_ref,
    sums_ref,
    strips,
    sums,
    k_t,
    dk,
    dv,
    *,
    block,
    per_slot,
    begin,
):
    i = pl.program_id(0)
    me = scalars[0]
    low = scalars[1 + i]
    heads = strips.shape[0]
    pairs = heads // 2

    def columns(p, kind):
        return slice((3 * (p + begin) + kind) * PAIR, (3 * (p + begin) + kind + 1) * PAIR)

    def wide_columns(p):
        return slice((p + begin) * PAIR, (p + begin + 1) * PAIR)

    @pl.when(i == 0)
    def _():
        make_strip(line_ref, strips, 2 * begin)
        for p in range(pairs):
            k_t[p * PAIR : (p + 1) * PAIR] = x_ref[:, columns(p, 1)].T
        dk[...] = jnp.zeros_like(dk)
        dv[...] = jnp.zeros_like(dv)
        sums[...] = jnp.zeros_like(sums)

    rows = pl.ds(pl.multiple_of(place_of(i, me, per_slot) * block, block), block)
    own_q = [head_lanes(x_ref[rows, columns(h // 2, 0)], h % 2) for h in range(heads)]
    own_up = [head_lanes(up_ref[rows, wide_columns(h // 2)], h % 2) for h in range(heads)]
    picks = lax.broadcasted_iota(jnp.int32, (8, PAIR), 1) // HD == lax.broadcasted_iota(jnp.int32, (8, PAIR), 0)
    picks = picks.astype(jnp.bfloat16)
    deltas = []
    for p in range(pairs):
        span = wide_columns(p)
        product = up_ref[rows, span].astype(jnp.float32) * mixed_ref[rows, span].astype(jnp.float32)
        high = product.astype(jnp.bfloat16)
        rest = (product - high.astype(jnp.float32)).astype(jnp.bfloat16)
        both = dot_nt(picks, high) + dot_nt(picks, rest)
        deltas += [both[0:1], both[1:2]]
    first = first_ref[pl.ds(i, 1), :]
    key_index = lax.broadcasted_iota(jnp.int32, (block, block), 0)

    def step(t, carry):
        here = pl.ds(pl.multiple_of(place_of(i - t, me, per_slot) * block, block), block)
        allowed = key_index >= (first - (i - t) * block)
        dq = []
        for p in range(pairs):
            span = slice(p * PAIR, (p + 1) * PAIR)
            keys = x_ref[here, columns(p, 1)]
            values = x_ref[here, columns(p, 2)]
            dk_new = dk[here, span]
            dv_new = dv[here, span]
            for h in (2 * p, 2 * p + 1):
                scores = dot_nt(keys, own_q[h]) + strip_tile(strips, h, t, block)
                scores = jnp.where(allowed, scores, MASKED_SCORE)
                probs = jnp.exp(scores - lse_ref[i, 2 * begin + h : 2 * begin + h + 1, :])
                score_grad = probs * (dot_nt(values, own_up[h]) - deltas[h])
                add_to_strip(sums, h, t, score_grad)
                low_grad = score_grad.astype(jnp.bfloat16)
                dv_new = dv_new + dot_nn(probs.astype(jnp.bfloat16), own_up[h])
                dk_new = dk_new + dot_nn(low_grad, own_q[h])
                dq.append(carry[h] + dot_nn(k_t[h * HD : (h + 1) * HD, here], low_grad))
            dk[here, span] = dk_new
            dv[here, span] = dv_new
        return tuple(dq)

    dq = lax.fori_loop(0, i - low + 1, step, (jnp.zeros((HD, block), jnp.float32),) * heads)
    for p in range(pairs):
        both = jnp.concatenate(dq[2 * p : 2 * p + 2], axis=0).T * (HD ** (-0.5))
        grad_ref[rows, columns_of(p, 0)] = both.astype(jnp.bfloat16)

    @pl.when(i == pl.num_programs(0) - 1)
    def _():
        for p in range(pairs):
            span = slice(p * PAIR, (p + 1) * PAIR)
            grad_ref[:, columns_of(p, 1)] = dk[:, span].astype(jnp.bfloat16)
            grad_ref[:, columns_of(p, 2)] = dv[:, span].astype(jnp.bfloat16)
        for h in range(heads):
            sums_ref[h : h + 1, :] = strip_line(sums[h])


WHOLE = pl.BlockSpec(memory_space=pltpu.VMEM)


def ignoring(kernel, first, count):
    def body(*refs):
        kernel(*refs[:first], *refs[first + count :])

    return body


def attend(joined, first, lines, scalars, block, per_slot, waits):
    length = joined.shape[0]
    heads, span = lines.shape
    blocks = length // block
    strip = pltpu.VMEM((heads, min(128, block), span), jnp.float32)
    grid_spec = pltpu.PrefetchScalarGridSpec(
        num_scalar_prefetch=1,
        grid=(blocks,),
        in_specs=[WHOLE] * 3 + [ANYWHERE] * len(waits),
        out_specs=[WHOLE] * 2,
        scratch_shapes=[
            strip,
            pltpu.VMEM((heads * HD, length), jnp.bfloat16),
            pltpu.VMEM((heads, span // block - 1, block, block), jnp.float32),
        ],
    )
    return pl.pallas_call(
        ignoring(functools.partial(attend_kernel, block=block, per_slot=per_slot), 4, len(waits)),
        grid_spec=grid_spec,
        out_shape=[
            jax.ShapeDtypeStruct((length, heads * HD), jnp.bfloat16),
            jax.ShapeDtypeStruct((blocks, heads, block), jnp.float32),
        ],
        compiler_params=pltpu.CompilerParams(vmem_limit_bytes=FORWARD_VMEM),
        cost_estimate=pl.CostEstimate(flops=FORWARD_FLOPS, bytes_accessed=8 * length * heads * HD, transcendentals=0),
    )(scalars, joined, first, lines, *waits)


def attend_back(joined, mixed, upstream, first, lines, lse, scalars, block, per_slot, begin, end, waits):
    length = joined.shape[0]
    span = lines.shape[1]
    heads = 2 * (end - begin)
    blocks = length // block
    strip = pltpu.VMEM((heads, min(128, block), span), jnp.float32)
    grid_spec = pltpu.PrefetchScalarGridSpec(
        num_scalar_prefetch=1,
        grid=(blocks,),
        in_specs=[WHOLE] * 6 + [ANYWHERE] * len(waits),
        out_specs=[WHOLE] * 2,
        scratch_shapes=[
            strip,
            strip,
            pltpu.VMEM((heads * HD, length), jnp.bfloat16),
            pltpu.VMEM((length, heads * HD), jnp.float32),
            pltpu.VMEM((length, heads * HD), jnp.float32),
        ],
    )
    return pl.pallas_call(
        ignoring(
            functools.partial(attend_back_kernel, block=block, per_slot=per_slot, begin=begin), 7, len(waits)
        ),
        grid_spec=grid_spec,
        out_shape=[
            jax.ShapeDtypeStruct((length, 3 * heads * HD), jnp.bfloat16),
            jax.ShapeDtypeStruct((heads, span), jnp.float32),
        ],
        compiler_params=pltpu.CompilerParams(vmem_limit_bytes=BACKWARD_VMEM),
        cost_estimate=pl.CostEstimate(
            flops=BACKWARD_FLOPS // 8 * heads, bytes_accessed=20 * length * heads * HD, transcendentals=0
        ),
    )(scalars, joined, mixed, upstream, first, lines, lse, *waits)


class Net:
    def __init__(self, wide, narrow, group):
        self.wide, self.narrow, self.group = wide, narrow, group
        self.ring = narrow // group
        self.bits = wide.bit_length() - 1

    def from_group(self, value, s):
        if s == 0:
            return value
        return lax.ppermute(value, "narrow", [(i, i ^ s) for i in range(self.narrow)])

    def from_ring(self, value, r):
        return self.from_group(value, r * self.group)

    def from_wide(self, value, s):
        if s == 0:
            return value
        return lax.ppermute(value, "wide", [(i, i ^ s) for i in range(self.wide)])

    def bit_order(self, turn):
        return [(b + turn) % self.bits for b in range(self.bits)]

    def halves(self):
        cut = max(self.ring // 2, 1)
        return [list(range(cut)), list(range(cut, self.ring))]

    def ring_slots(self, quarter):
        return [self.from_ring(quarter, r) for r in range(self.ring)]

    def ring_doubling(self, own):
        slots = [own]
        r = 1
        while r < self.ring:
            away = self.from_ring(jnp.stack(slots, axis=0), r)
            slots = slots + [away[k] for k in range(r)]
            r *= 2
        return slots

    def spread(self, unit, turn):
        pieces, steps = {0: unit}, []
        for b in self.bit_order(turn):
            steps.append({s ^ (1 << b): self.from_wide(piece, 1 << b) for s, piece in pieces.items()})
            pieces.update(steps[-1])
        return [pieces[s] for s in range(self.wide)]

    def spread_doubling(self, unit, turn):
        order, pieces = [0], [unit]
        for b in self.bit_order(turn):
            away = self.from_wide(jnp.stack(pieces, axis=0), 1 << b)
            order = order + [s ^ (1 << b) for s in order]
            pieces = pieces + [away[k] for k in range(len(pieces))]
        return [pieces[order.index(s)] for s in range(self.wide)]

    def share(self, own):
        me = lax.axis_index("wide")
        pieces = [self.from_wide(own, s) for s in range(self.wide)]
        for b in range(self.bits):
            swap = (me >> b) & 1 == 1
            pieces = [jnp.where(swap, pieces[s ^ (1 << b)], piece) for s, piece in enumerate(pieces)]
        return pieces

    def total(self, value):
        value = value + sum(self.from_group(value, s) for s in range(1, self.group))
        value = value + sum(self.from_ring(value, r) for r in range(1, self.ring))
        return value + sum(self.from_wide(value, s) for s in range(1, self.wide))


ANYWHERE = pl.BlockSpec(memory_space=pl.ANY)


def hold_kernel(*refs):
    pass


def after(value, *others):
    values, tree = jax.tree.flatten(value)
    waits = jax.tree.leaves(others)
    if len(values) + len(waits) < 2 or not values:
        return value
    held = pl.pallas_call(
        hold_kernel,
        in_specs=[ANYWHERE] * (len(values) + len(waits)),
        out_specs=[ANYWHERE] * len(values),
        out_shape=[jax.ShapeDtypeStruct(one.shape, one.dtype) for one in values],
        input_output_aliases={k: k for k in range(len(values))},
    )(*values, *waits)
    return jax.tree.unflatten(tree, held)


def add_low(kept, arrived):
    return (kept.astype(jnp.float32) + arrived.astype(jnp.float32)).astype(jnp.bfloat16)


class WideSum:
    def __init__(self, net, value, turn):
        self.net = net
        self.bits = list(reversed(net.bit_order(turn)))
        self.value = value.reshape((2,) * net.bits + value.shape[1:])
        self.left = list(range(net.bits - 1, -1, -1))
        self.sent = False

    def send(self):
        self.sent = True
        bit = self.bits.pop(0)
        axis = self.left.index(bit)
        self.left.pop(axis)
        self.kept = lax.index_in_dim(self.value, 0, axis, keepdims=False)
        self.arrived = self.net.from_wide(lax.index_in_dim(self.value, 1, axis, keepdims=False), 1 << bit)
        return self

    def add(self, *others):
        self.value = add_low(self.kept, after(self.arrived, *others))
        self.sent = False
        return self

    def finish(self):
        if self.sent:
            self.add()
        while self.bits:
            self.send().add()
        return self.value


class RingSum:
    def __init__(self, net, values):
        self.net, self.values = net, list(values)
        self.sent = False

    def send(self):
        self.sent = True
        keep = len(self.values) // 2
        self.arrived = self.net.from_ring(jnp.stack(self.values[keep:], axis=0), keep)
        return self

    def add(self, *others):
        arrived = after(self.arrived, *others)
        self.sent = False
        keep = len(self.values) // 2
        self.values = [add_low(value, arrived[k]) for k, value in enumerate(self.values[:keep])]
        return self

    def finish(self):
        if self.sent:
            self.add()
        while len(self.values) > 1:
            self.send().add()
        return self.values[0]


def assemble_kernel(*refs, plan):
    out_ref = refs[-1]
    for ref, source, rows, begin in plan:
        out_ref[begin : begin + rows, :] = refs[ref][source]


def assemble(arrays, plan, rows, waits=()):
    return pl.pallas_call(
        ignoring(functools.partial(assemble_kernel, plan=plan), len(arrays), len(waits)),
        in_specs=[WHOLE] * len(arrays) + [ANYWHERE] * len(waits),
        out_specs=WHOLE,
        out_shape=jax.ShapeDtypeStruct((rows, arrays[0].shape[-1]), arrays[0].dtype),
        compiler_params=pltpu.CompilerParams(vmem_limit_bytes=24 * 1024 * 1024),
    )(*arrays, *waits)


def on_device(
    inputs,
    seg_ids,
    buckets,
    norm1_gain,
    norm1_shift,
    w_query,
    w_key,
    w_value,
    w_out,
    norm2_gain,
    norm2_shift,
    w_up,
    w_down,
    rel_table,
    out_grad,
    *,
    wide,
    narrow,
):
    bf16, f32 = jnp.bfloat16, jnp.float32
    tokens, width = inputs.shape
    length = seg_ids.shape[1]
    group = length // tokens
    net = Net(wide, narrow, group)
    ring = net.ring
    head_rows = w_query.shape[0]
    heads_here = rel_table.shape[1]
    piece_rows = head_rows // wide
    scale = HD ** (-0.5)
    block = min(256, tokens)
    per_slot = tokens // block
    blocks = length // block
    reach_blocks = min(blocks, -(-REACH // block) + 1)
    me_wide = lax.axis_index("wide")
    me_narrow = lax.axis_index("narrow")
    me_group = me_narrow % group
    me_ring = me_narrow // group
    halves = net.halves()

    def my_part(shard, axis=0):
        size = shard.shape[axis] // wide
        return lax.dynamic_slice_in_dim(shard, me_wide * size, size, axis)

    def all_group(own):
        return jnp.concatenate([own] + [net.from_group(own, s) for s in range(1, group)], axis=0)

    def away_parts(parts_of):
        return [net.from_group(parts_of(s).astype(bf16), s) for s in range(1, group)]

    def slot(value, s):
        return value[s * tokens : (s + 1) * tokens]

    def add_parts(own, away):
        for part in away:
            own = own + part.astype(f32)
        return own

    table_low = []
    left = rel_table
    for _ in range(3):
        table_low.append(lax.reduce_precision(left, 8, 7))
        left = left - table_low[-1]
    table_flat = jnp.stack(table_low, axis=0).astype(bf16).reshape(-1)
    table_row = jnp.pad(table_flat, (0, 16 * width - table_flat.size)).reshape(16, width)
    attention_quarter = my_part(jnp.stack([w_query, w_key, w_value, w_out], axis=0), 1).reshape(-1, width)
    first_slots = net.ring_slots(jnp.concatenate([attention_quarter, table_row], axis=0))
    attention_rows = attention_quarter.shape[0]
    table_slots = [
        rows[attention_rows][: table_flat.size].reshape((3,) + rel_table.shape).astype(f32).sum(0)
        for rows in first_slots
    ]
    attention_units = [
        jnp.stack([first_slots[r][:attention_rows].reshape(4, piece_rows, width) for r in places], axis=0)
        for places in halves
    ]
    attention_pieces = [net.spread_doubling(unit, turn) for turn, unit in enumerate(attention_units)]

    ffn_own = jnp.concatenate([my_part(w_up, 1).T, my_part(w_down)], axis=0)
    unit = ffn_own.shape[0] // 2
    own_out = {1 << b: net.from_wide(ffn_own, 1 << b) for b in range(net.bits)}

    values_in = inputs.astype(f32)
    normed1, inverse1 = row_norm(values_in)
    a1_own = (normed1 * norm1_gain + norm1_shift).astype(bf16)
    a1_away = [net.from_group(a1_own, s) for s in range(1, group)]
    a1 = jnp.concatenate([a1_own] + a1_away, axis=0)
    ffn_slots = net.ring_slots(after(ffn_own, first_slots[1:], a1_away, list(own_out.values())))

    per_pair = PAIR // head_rows
    pairs = ring // per_pair
    order = [
        (p * per_pair + r, t, s)
        for p in range(pairs)
        for t in range(3)
        for r in range(per_pair)
        for s in range(wide)
    ] + [(r, 3, s) for r in range(ring) for s in range(wide)]
    place_in_half = {r: (half, at) for half, places in enumerate(halves) for at, r in enumerate(places)}
    plan = []
    for at, (r, t, s) in enumerate(order):
        half, place = place_in_half[r]
        plan.append((half * wide + s, (place, t), piece_rows, at * piece_rows))
    w_attention = assemble(attention_pieces[0] + attention_pieces[1], plan, len(order) * piece_rows)
    w_joined = w_attention[: 3 * ring * head_rows]
    w_out_full = w_attention[3 * ring * head_rows :]
    column_kind = (jnp.arange(w_joined.shape[0]) // PAIR) % 3
    column_scale = jnp.where(column_kind == 0, jnp.asarray(scale, f32), jnp.asarray(1.0, f32))
    joined = (dot_nt(a1, w_joined) * column_scale).astype(bf16)
    dy = all_group(out_grad)

    reach = reach_blocks * block
    one_hot = (buckets[:reach, None] == jnp.arange(rel_table.shape[0])[None, :]).astype(f32)

    def head_of(r, h):
        return ((me_wide ^ (h * (HD // piece_rows))) * piece_rows) // HD

    table_here = jnp.concatenate(
        [
            lax.dynamic_slice_in_dim(table_slots[r], head_of(r, h), 1, 1)
            for r in range(ring)
            for h in range(heads_here)
        ],
        axis=1,
    )
    line = jnp.dot(one_hot, table_here, precision=lax.Precision.HIGHEST, preferred_element_type=f32).T
    lines = jnp.concatenate([jnp.full((line.shape[0], block), MASKED_SCORE, f32), line], axis=1)

    segments = lax.dynamic_slice_in_dim(seg_ids, me_ring, 1, 0)[0]
    first = jnp.sum((segments[None, :] < segments[:, None]).astype(jnp.int32), axis=1)
    scalars = jnp.concatenate([me_group[None], first[::block] // block]).astype(jnp.int32)
    first = first.reshape(blocks, block)

    mixed, lse = attend(joined, first, lines, scalars, block, per_slot, ffn_slots[1:])

    ffn_pieces, first_hops, second_hops = [], [], []
    for k in range(2):
        own = [rows[k * unit : (k + 1) * unit] for rows in ffn_slots]
        bits = net.bit_order(k)
        pieces = {0: jnp.stack(own, axis=0)}
        for at, b in enumerate(bits):
            away = {}
            for s, piece in pieces.items():
                if s == 0:
                    rest = net.from_wide(jnp.stack(own[1:], axis=0), 1 << b)
                    (first_hops if at == 0 else second_hops).append(rest)
                    away[1 << b] = jnp.concatenate([own_out[1 << b][None, k * unit : (k + 1) * unit], rest], axis=0)
                else:
                    away[s ^ (1 << b)] = net.from_wide(piece, 1 << b)
            pieces.update(away)
        ffn_pieces.append([pieces[s] for s in range(wide)])
    mixed = after(mixed, first_hops)

    attended_away = away_parts(lambda s: dot_nn(slot(mixed, s), w_out_full))
    attended = add_parts(dot_nn(slot(mixed, 0), w_out_full), attended_away)
    hidden_state = values_in + attended
    normed2, inverse2 = row_norm(hidden_state)
    a2_own = (normed2 * norm2_gain + norm2_shift).astype(bf16)
    a2_own = after(a2_own, second_hops)
    a2 = all_group(a2_own)

    w_up_t, w_down_full = (jnp.concatenate(pieces, axis=0).reshape(-1, width) for pieces in ffn_pieces)
    up = dot_nt(a2, w_up_t)
    gelu_value, gelu_pull = jax.vjp(jax.nn.gelu, up)
    active = gelu_value.astype(bf16)
    up_grad = gelu_pull(dot_nt(dy, w_down_full))[0].astype(bf16)
    normed2_part = [dot_nn(slot(up_grad, s), w_up_t).astype(bf16) for s in range(1, group)]
    normed2_away = [net.from_group(part, s + 1) for s, part in enumerate(normed2_part)]
    grad_down = dot_tn(active, dy).astype(bf16)
    up_grad = after(up_grad, grad_down, normed2_part)
    normed2_own = dot_nn(slot(up_grad, 0), w_up_t)

    def wide_sums(grad):
        value = grad.reshape(wide, ring, -1, width)
        return [
            WideSum(net, value[:, places[0] : places[-1] + 1], turn).send() for turn, places in enumerate(halves)
        ]

    def step(many, *others):
        for one in many:
            one.add(*others)
        for one in many:
            if one.bits:
                one.send()

    def arrive(value, *many):
        many = [one for one in many if one.sent]
        held = after([value] + [one.arrived for one in many])
        for one, arrived in zip(many, held[1:]):
            one.arrived = arrived
        return held[0]

    def ring_sum(many):
        return RingSum(net, [value[at] for value in (one.finish() for one in many) for at in range(value.shape[0])])

    down_sums = wide_sums(grad_down)

    normed2_grad = add_parts(normed2_own, after(normed2_away, grad_down))
    back2, grad_gain2, grad_shift2 = norm_backward(normed2_grad, normed2, inverse2, norm2_gain)
    state_grad = out_grad.astype(f32) + back2
    state_low = state_grad.astype(bf16)
    state_away = [net.from_group(state_low, s) for s in range(1, group)]
    grad_up = dot_tn(arrive(after(up_grad, state_low), *down_sums), a2).astype(bf16)
    state_away = after(state_away, grad_up)
    up_sums = wide_sums(grad_up)
    step(down_sums)
    state_whole = jnp.concatenate([state_low] + state_away, axis=0)
    mixed_grad = dot_nt(state_whole, w_out_full).astype(bf16)
    grad_out = dot_tn(mixed, state_whole).astype(bf16)

    def grads_of(begin, end, waits):
        return attend_back(
            joined, mixed, mixed_grad, first, lines, lse, scalars, block, per_slot, begin, end, waits
        )

    def attention_sums(grads, begin, end):
        grad_part = dot_tn(grads, a1).astype(bf16)
        grad_part = grad_part.reshape(end - begin, 3, per_pair, wide, piece_rows, width)
        result = []
        for r in range(begin * per_pair, end * per_pair):
            grad_qkv = grad_part[r // per_pair - begin, :, r % per_pair]
            grad_o = grad_out[r * head_rows : (r + 1) * head_rows].reshape(1, wide, piece_rows, width)
            value = jnp.moveaxis(jnp.concatenate([grad_qkv, grad_o], axis=0), 1, 0)
            result.append(WideSum(net, value, r % 2).send())
        return grad_part, result

    cut = pairs // 2
    grads, line_sums = grads_of(cut, pairs, [one.kept for one in down_sums])
    grads = arrive(grads, *down_sums, *up_sums)
    all_grads, all_lines = [grads], [line_sums]
    step(down_sums)
    step(up_sums)
    down_ring = ring_sum(down_sums).send()
    part, far_sums = attention_sums(grads, cut, pairs)
    near_sums, up_ring, far_ring = [], None, None
    for p in reversed(range(cut)):
        flying = up_sums + far_sums + near_sums + [down_ring]
        grads, line_sums = grads_of(p, p + 1, [part])
        grads = arrive(grads, *(flying + [ring for ring in (up_ring, far_ring) if ring is not None]))
        all_grads, all_lines = [grads] + all_grads, [line_sums] + all_lines
        if up_ring is None:
            step(up_sums)
            up_ring = ring_sum(up_sums).send()
            step(far_sums)
        elif far_ring is None:
            far_ring = RingSum(net, [None] * cut * per_pair + [one.finish() for one in far_sums]).send()
        if down_ring.sent:
            down_ring.add()
        if len(down_ring.values) > 1:
            down_ring.send()
        step(near_sums)
        part, sums = attention_sums(grads, p, p + 1)
        near_sums = sums + near_sums
    if far_ring is None:
        far_ring = RingSum(net, [None] * cut * per_pair + [one.finish() for one in far_sums]).send()
    w_late, active_late = after((w_joined, active), part)

    def normed1_part(s):
        total, at = None, 0
        for grads in all_grads:
            part = dot_nn(slot(grads, s), w_late[at : at + grads.shape[1]])
            total = part if total is None else total + part
            at += grads.shape[1]
        return total

    normed1_away = away_parts(normed1_part)
    normed1_own = normed1_part(0)

    normed1_grad = add_parts(normed1_own, normed1_away)
    back1, grad_gain1, grad_shift1 = norm_backward(normed1_grad, normed1, inverse1, norm1_gain)
    input_grad = state_grad + back1

    line_grad = jnp.concatenate(all_lines, axis=0)[:, block:]
    table_grad = jnp.dot(line_grad, one_hot, precision=lax.Precision.HIGHEST, preferred_element_type=f32)
    all_heads = heads_here * narrow
    head_ids = jnp.stack(
        [
            ((me_ring ^ r) * group + me_group) * heads_here + head_of(r, h)
            for r in range(ring)
            for h in range(heads_here)
        ]
    )
    placed = (jnp.arange(all_heads)[:, None] == head_ids[None, :]).astype(f32)
    table_all = jnp.dot(placed, table_grad, precision=lax.Precision.HIGHEST, preferred_element_type=f32)

    small = jnp.concatenate([grad_gain1, grad_shift1, grad_gain2, grad_shift2, table_all.reshape(-1)])
    pad = -small.shape[0] % 1024
    small = net.total(jnp.pad(small, (0, pad)).reshape(-1, 128)).reshape(-1)
    gain1, shift1, gain2, shift2 = (small[k * width : (k + 1) * width] for k in range(4))
    table_sum = small[4 * width : 4 * width + table_all.size].reshape(table_all.shape)
    table_out = lax.dynamic_slice_in_dim(table_sum, me_narrow * heads_here, heads_here, 0).T

    feed_away = away_parts(lambda s: dot_nn(slot(active_late, s), w_down_full))
    feed = add_parts(dot_nn(slot(active_late, 0), w_down_full), feed_away)
    out = (hidden_state + feed).astype(bf16)

    far_ring.values[: len(near_sums)] = [one.finish() for one in near_sums]
    ffn_part = jnp.concatenate([down_ring.finish(), up_ring.finish()], axis=0)
    ffn_all = net.share(ffn_part)
    down_all = jnp.concatenate([part[:unit] for part in ffn_all], axis=0).astype(f32)
    up_all = jnp.concatenate([part[unit:] for part in ffn_all], axis=0).T.astype(f32)
    attention_all = net.share(far_ring.finish())
    attention_all = jnp.concatenate(attention_all, axis=1).astype(f32)
    return (
        out,
        input_grad,
        gain1,
        shift1,
        attention_all[0],
        attention_all[1],
        attention_all[2],
        attention_all[3],
        gain2,
        shift2,
        up_all,
        down_all,
        table_out,
    )


def _xor_rows(matrix, me, count):
    rows = matrix.shape[0] // count
    return [lax.dynamic_slice_in_dim(matrix, (me ^ s) * rows, rows, 0) for s in range(count)]


def solution(mesh):
    placed = (
        P(("wide", "narrow"), None),
        P("wide", None),
        P(),
        P(),
        P(),
        P("narrow", None),
        P("narrow", None),
        P("narrow", None),
        P("narrow", None),
        P(),
        P(),
        P(None, "narrow"),
        P("narrow", None),
        P(None, "narrow"),
        P(("wide", "narrow"), None),
    )
    return jax.shard_map(
        functools.partial(on_device, wide=mesh.shape["wide"], narrow=mesh.shape["narrow"]),
        mesh=mesh,
        in_specs=placed,
        out_specs=(
            P(("wide", "narrow"), None),
            P(("wide", "narrow"), None),
            P(),
            P(),
            P("narrow", None),
            P("narrow", None),
            P("narrow", None),
            P("narrow", None),
            P(),
            P(),
            P(None, "narrow"),
            P("narrow", None),
            P(None, "narrow"),
        ),
        check_vma=False,
    )
```

```python
import functools

import jax
import jax.numpy as jnp
from jax import lax
from jax.experimental import pallas as pl
from jax.experimental.pallas import tpu as pltpu
from jax.sharding import PartitionSpec as P

HD = 64
PAIR = 128
REACH = 1024
EPSILON = 1e-05
MASKED_SCORE = -1e30
ROOT = (2.0 / 3.141592653589793) ** 0.5
VMEM = 60 * 1024 * 1024
LIGHT = pl.CostEstimate(flops=1, bytes_accessed=1, transcendentals=0)
NT = (((1,), (1,)), ((), ()))
TN = (((0,), (0,)), ((), ()))


def row_norm(values):
    mean = jnp.mean(values, axis=1, keepdims=True)
    centred = values - mean
    spread = jnp.mean(centred * centred, axis=1, keepdims=True)
    inverse = lax.rsqrt(spread + EPSILON)
    return (centred * inverse, inverse)


def norm_backward(upstream, normed, inverse, gain):
    scaled = upstream * gain
    mean_plain = jnp.mean(scaled, axis=1, keepdims=True)
    mean_cross = jnp.mean(scaled * normed, axis=1, keepdims=True)
    result = inverse * (scaled - mean_plain - normed * mean_cross)
    return (result, jnp.sum(upstream * normed, axis=0), jnp.sum(upstream, axis=0))


def dot_nt(left, right):
    return lax.dot_general(left, right, NT, preferred_element_type=jnp.float32)


def dot_nn(left, right):
    return jnp.dot(left, right, preferred_element_type=jnp.float32)


def dot_tn(left, right):
    return lax.dot_general(left, right, TN, preferred_element_type=jnp.float32)


def make_strip(line_ref, strips, begin=0):
    for h in range(strips.shape[0]):
        spread = jnp.broadcast_to(line_ref[begin + h : begin + h + 1, :], strips.shape[1:])
        strips[h] = pltpu.roll(spread, 0, 1, stride=1, stride_axis=0)


def strip_line(strip):
    rows, span = strip.shape
    while rows > 1:
        rows //= 2
        strip = strip[:rows] + pltpu.roll(strip[rows : 2 * rows], span - rows, 1)
    return strip


def strip_at(t, u, rows, block):
    return pl.ds(pl.multiple_of(t * block + (block - u * rows), rows), block)


def strip_tile(strips, h, t, block):
    rows = strips.shape[1]
    parts = [strips[h, :, strip_at(t, u, rows, block)] for u in range(block // rows)]
    return jnp.concatenate(parts, axis=0)


def add_to_strip(strips, h, t, tile):
    rows, block = strips.shape[1], tile.shape[0]
    for u in range(block // rows):
        strips[h, :, strip_at(t, u, rows, block)] += tile[u * rows : (u + 1) * rows]


def place_of(index, me, per_slot):
    return ((index // per_slot) ^ me) * per_slot + index % per_slot


def head_lanes(block, h):
    lanes = lax.broadcasted_iota(jnp.int32, block.shape, 1)
    return jnp.where((lanes // HD) == h, block, jnp.zeros_like(block))


def columns_of(p, kind):
    return slice((3 * p + kind) * PAIR, (3 * p + kind + 1) * PAIR)


def attend_kernel(scalars, x_ref, first_ref, line_ref, out_ref, lse_ref, strips, v_t, kept, *, block, per_slot):
    i = pl.program_id(0)
    me = scalars[0]
    low = scalars[1 + i]
    heads = strips.shape[0]
    pairs = heads // 2

    @pl.when(i == 0)
    def _():
        make_strip(line_ref, strips)
        for p in range(pairs):
            v_t[p * PAIR : (p + 1) * PAIR] = x_ref[:, columns_of(p, 2)].T

    rows = pl.ds(pl.multiple_of(place_of(i, me, per_slot) * block, block), block)
    own = [head_lanes(x_ref[rows, columns_of(h // 2, 0)], h % 2) for h in range(heads)]
    first = first_ref[pl.ds(i, 1), :]
    key_index = lax.broadcasted_iota(jnp.int32, (block, block), 0)

    def rows_of(t):
        return pl.ds(pl.multiple_of(place_of(i - t, me, per_slot) * block, block), block)

    def fold(value):
        return value.reshape(block // 8, 8, block)

    def score_step(t, tops):
        here = rows_of(t)
        allowed = key_index >= (first - (i - t) * block)
        result = []
        for h in range(heads):
            scores = dot_nt(x_ref[here, columns_of(h // 2, 1)], own[h]) + strip_tile(strips, h, t, block)
            scores = jnp.where(allowed, scores, MASKED_SCORE)
            kept[h, t] = scores
            result.append(jnp.maximum(tops[h], jnp.max(fold(scores), axis=0)))
        return tuple(result)

    def value_step(t, carry):
        here = rows_of(t)
        result = []
        for h in range(heads):
            total, acc = carry[h]
            expo = jnp.exp(kept[h, t] - tops[h])
            total = total + jnp.sum(fold(expo), axis=0)
            acc = acc + dot_nn(v_t[h * HD : (h + 1) * HD, here], expo.astype(jnp.bfloat16))
            result.append((total, acc))
        return tuple(result)

    tops = lax.fori_loop(
        0, i - low + 1, score_step, (jnp.full((8, block), MASKED_SCORE, jnp.float32),) * heads
    )
    tops = [jnp.max(top, axis=0, keepdims=True) for top in tops]
    zero = (jnp.zeros((8, block), jnp.float32), jnp.zeros((HD, block), jnp.float32))
    done = lax.fori_loop(0, i - low + 1, value_step, (zero,) * heads)
    totals = [jnp.sum(total, axis=0, keepdims=True) for total, _ in done]
    for p in range(pairs):
        both = jnp.concatenate([done[h][1] / totals[h] for h in (2 * p, 2 * p + 1)], axis=0)
        out_ref[rows, p * PAIR : (p + 1) * PAIR] = both.T.astype(jnp.bfloat16)
    lse_ref[pl.ds(i, 1)] = jnp.concatenate([tops[h] + jnp.log(totals[h]) for h in range(heads)], axis=0)[None]


def attend_back_kernel(
    scalars,
    x_ref,
    mixed_ref,
    up_ref,
    first_ref,
    line_ref,
    lse_ref,
    grad_ref,
    sums_ref,
    strips,
    sums,
    k_t,
    dk,
    dv,
    *,
    block,
    per_slot,
    begin,
):
    i = pl.program_id(0)
    me = scalars[0]
    low = scalars[1 + i]
    heads = strips.shape[0]
    pairs = heads // 2

    def columns(p, kind):
        return slice((3 * (p + begin) + kind) * PAIR, (3 * (p + begin) + kind + 1) * PAIR)

    def wide_columns(p):
        return slice((p + begin) * PAIR, (p + begin + 1) * PAIR)

    @pl.when(i == 0)
    def _():
        make_strip(line_ref, strips, 2 * begin)
        for p in range(pairs):
            k_t[p * PAIR : (p + 1) * PAIR] = x_ref[:, columns(p, 1)].T
        dk[...] = jnp.zeros_like(dk)
        dv[...] = jnp.zeros_like(dv)
        sums[...] = jnp.zeros_like(sums)

    rows = pl.ds(pl.multiple_of(place_of(i, me, per_slot) * block, block), block)
    own_q = [head_lanes(x_ref[rows, columns(h // 2, 0)], h % 2) for h in range(heads)]
    own_up = [head_lanes(up_ref[rows, wide_columns(h // 2)], h % 2) for h in range(heads)]
    picks = lax.broadcasted_iota(jnp.int32, (8, PAIR), 1) // HD == lax.broadcasted_iota(jnp.int32, (8, PAIR), 0)
    picks = picks.astype(jnp.bfloat16)
    deltas = []
    for p in range(pairs):
        span = wide_columns(p)
        product = up_ref[rows, span].astype(jnp.float32) * mixed_ref[rows, span].astype(jnp.float32)
        high = product.astype(jnp.bfloat16)
        rest = (product - high.astype(jnp.float32)).astype(jnp.bfloat16)
        both = dot_nt(picks, high) + dot_nt(picks, rest)
        deltas += [both[0:1], both[1:2]]
    first = first_ref[pl.ds(i, 1), :]
    key_index = lax.broadcasted_iota(jnp.int32, (block, block), 0)

    def step(t, carry):
        here = pl.ds(pl.multiple_of(place_of(i - t, me, per_slot) * block, block), block)
        allowed = key_index >= (first - (i - t) * block)
        dq = []
        for p in range(pairs):
            span = slice(p * PAIR, (p + 1) * PAIR)
            keys = x_ref[here, columns(p, 1)]
            values = x_ref[here, columns(p, 2)]
            dk_new = dk[here, span]
            dv_new = dv[here, span]
            for h in (2 * p, 2 * p + 1):
                scores = dot_nt(keys, own_q[h]) + strip_tile(strips, h, t, block)
                scores = jnp.where(allowed, scores, MASKED_SCORE)
                probs = jnp.exp(scores - lse_ref[i, 2 * begin + h : 2 * begin + h + 1, :])
                score_grad = probs * (dot_nt(values, own_up[h]) - deltas[h])
                add_to_strip(sums, h, t, score_grad)
                low_grad = score_grad.astype(jnp.bfloat16)
                dv_new = dv_new + dot_nn(probs.astype(jnp.bfloat16), own_up[h])
                dk_new = dk_new + dot_nn(low_grad, own_q[h])
                dq.append(carry[h] + dot_nn(k_t[h * HD : (h + 1) * HD, here], low_grad))
            dk[here, span] = dk_new
            dv[here, span] = dv_new
        return tuple(dq)

    dq = lax.fori_loop(0, i - low + 1, step, (jnp.zeros((HD, block), jnp.float32),) * heads)
    for p in range(pairs):
        both = jnp.concatenate(dq[2 * p : 2 * p + 2], axis=0).T * (HD ** (-0.5))
        grad_ref[rows, columns_of(p, 0)] = both.astype(jnp.bfloat16)

    @pl.when(i == pl.num_programs(0) - 1)
    def _():
        for p in range(pairs):
            span = slice(p * PAIR, (p + 1) * PAIR)
            grad_ref[:, columns_of(p, 1)] = dk[:, span].astype(jnp.bfloat16)
            grad_ref[:, columns_of(p, 2)] = dv[:, span].astype(jnp.bfloat16)
        for h in range(heads):
            sums_ref[h : h + 1, :] = strip_line(sums[h])


WHOLE = pl.BlockSpec(memory_space=pltpu.VMEM)
ANYWHERE = pl.BlockSpec(memory_space=pl.ANY)


def ignoring(kernel, first, count):
    def body(*refs):
        kernel(*refs[:first], *refs[first + count :])

    return body


def attend(joined, first, lines, scalars, block, per_slot, waits):
    length = joined.shape[0]
    heads, span = lines.shape
    blocks = length // block
    strip = pltpu.VMEM((heads, min(128, block), span), jnp.float32)
    grid_spec = pltpu.PrefetchScalarGridSpec(
        num_scalar_prefetch=1,
        grid=(blocks,),
        in_specs=[WHOLE] * 3 + [ANYWHERE] * len(waits),
        out_specs=[WHOLE] * 2,
        scratch_shapes=[
            strip,
            pltpu.VMEM((heads * HD, length), jnp.bfloat16),
            pltpu.VMEM((heads, span // block - 1, block, block), jnp.float32),
        ],
    )
    return pl.pallas_call(
        ignoring(functools.partial(attend_kernel, block=block, per_slot=per_slot), 4, len(waits)),
        grid_spec=grid_spec,
        out_shape=[
            jax.ShapeDtypeStruct((length, heads * HD), jnp.bfloat16),
            jax.ShapeDtypeStruct((blocks, heads, block), jnp.float32),
        ],
        compiler_params=pltpu.CompilerParams(vmem_limit_bytes=VMEM),
        cost_estimate=LIGHT,
    )(scalars, joined, first, lines, *waits)


def attend_back(joined, mixed, upstream, first, lines, lse, scalars, block, per_slot, begin, end, waits):
    length = joined.shape[0]
    span = lines.shape[1]
    heads = 2 * (end - begin)
    blocks = length // block
    strip = pltpu.VMEM((heads, min(128, block), span), jnp.float32)
    grid_spec = pltpu.PrefetchScalarGridSpec(
        num_scalar_prefetch=1,
        grid=(blocks,),
        in_specs=[WHOLE] * 6 + [ANYWHERE] * len(waits),
        out_specs=[WHOLE] * 2,
        scratch_shapes=[
            strip,
            strip,
            pltpu.VMEM((heads * HD, length), jnp.bfloat16),
            pltpu.VMEM((length, heads * HD), jnp.float32),
            pltpu.VMEM((length, heads * HD), jnp.float32),
        ],
    )
    return pl.pallas_call(
        ignoring(
            functools.partial(attend_back_kernel, block=block, per_slot=per_slot, begin=begin), 7, len(waits)
        ),
        grid_spec=grid_spec,
        out_shape=[
            jax.ShapeDtypeStruct((length, 3 * heads * HD), jnp.bfloat16),
            jax.ShapeDtypeStruct((heads, span), jnp.float32),
        ],
        compiler_params=pltpu.CompilerParams(vmem_limit_bytes=VMEM),
        cost_estimate=LIGHT,
    )(scalars, joined, mixed, upstream, first, lines, lse, *waits)


def hidden_kernel(*refs, slots, blocks, chunk):
    a2_refs, dy_refs = refs[:slots], refs[slots : 2 * slots]
    up_ref, down_ref, act_ref, up_grad_ref = refs[2 * slots : 2 * slots + 4]
    back_refs = refs[2 * slots + 4 :]
    for s in range(slots):

        @pl.when(pl.program_id(0) // blocks == s)
        def _(s=s):
            tokens = a2_refs[s][...]
            grads = dy_refs[s][...]
            total = jnp.zeros(tokens.shape, jnp.float32)
            for begin in range(0, up_ref.shape[0], chunk):
                rows = slice(begin, begin + chunk)
                x = dot_nt(tokens, up_ref[rows, :])
                square = x * x
                bend = jnp.tanh(x * (ROOT + ROOT * 0.044715 * square))
                half = 0.5 + 0.5 * bend
                act_ref[:, rows] = (x * half).astype(jnp.bfloat16)
                slope = half + 0.5 * x * (1.0 - bend * bend) * (ROOT + 3.0 * ROOT * 0.044715 * square)
                up_grad = (dot_nt(grads, down_ref[rows, :]) * slope).astype(jnp.bfloat16)
                up_grad_ref[:, rows] = up_grad
                total = total + dot_nn(up_grad, up_ref[rows, :])
            back_refs[s][...] = total.astype(jnp.bfloat16)


def hidden_units(a2, dy, w_up_t, w_down):
    tokens, width = a2[0].shape
    slots = len(a2)
    units = w_up_t.shape[0]
    block = min(256, tokens)
    blocks = tokens // block
    unit_block = pl.BlockSpec((block, units), lambda i: (i, 0))
    by_slot = [
        pl.BlockSpec((block, width), functools.partial(lambda i, s: (spot_in(i, s, blocks), 0), s=s))
        for s in range(slots)
    ]
    return pl.pallas_call(
        functools.partial(hidden_kernel, slots=slots, blocks=blocks, chunk=min(512, units)),
        grid=(slots * blocks,),
        in_specs=by_slot + by_slot + [WHOLE, WHOLE],
        out_specs=[unit_block, unit_block] + by_slot,
        out_shape=[jax.ShapeDtypeStruct((slots * tokens, units), jnp.bfloat16)] * 2
        + [jax.ShapeDtypeStruct((tokens, width), jnp.bfloat16)] * slots,
        compiler_params=pltpu.CompilerParams(vmem_limit_bytes=VMEM),
        cost_estimate=LIGHT,
    )(*a2, *dy, w_up_t, w_down)


def norm_back_kernel(*refs, parts):
    values_ref, add_ref, gain_ref = refs[:3]
    part_refs = refs[3 : 3 + parts]
    out_ref, low_ref, sums_ref = refs[3 + parts :]
    values = values_ref[...].astype(jnp.float32)
    normed, inverse = row_norm(values)
    upstream = part_refs[0][...].astype(jnp.float32)
    for ref in part_refs[1:]:
        upstream = upstream + ref[...].astype(jnp.float32)
    result, gain_grad, shift_grad = norm_backward(upstream, normed, inverse, gain_ref[...])
    result = result + add_ref[...].astype(jnp.float32)
    out_ref[...] = result
    low_ref[...] = result.astype(jnp.bfloat16)

    @pl.when(pl.program_id(0) == 0)
    def _():
        sums_ref[...] = jnp.zeros_like(sums_ref)

    sums_ref[0:1, :] += gain_grad[None]
    sums_ref[1:2, :] += shift_grad[None]


def norm_back(values, add, gain, parts, waits=()):
    tokens, width = values.shape
    block = min(256, tokens)
    rows = pl.BlockSpec((block, width), lambda i: (i, 0))
    result, low, sums = pl.pallas_call(
        ignoring(functools.partial(norm_back_kernel, parts=len(parts)), 3 + len(parts), len(waits)),
        grid=(tokens // block,),
        in_specs=[rows, rows, pl.BlockSpec((1, width), lambda i: (0, 0))]
        + [rows] * len(parts)
        + [ANYWHERE] * len(waits),
        out_specs=[rows, rows, pl.BlockSpec((8, width), lambda i: (0, 0))],
        out_shape=[
            jax.ShapeDtypeStruct((tokens, width), jnp.float32),
            jax.ShapeDtypeStruct((tokens, width), jnp.bfloat16),
            jax.ShapeDtypeStruct((8, width), jnp.float32),
        ],
        compiler_params=pltpu.CompilerParams(vmem_limit_bytes=VMEM),
        cost_estimate=LIGHT,
    )(values, add, gain[None], *parts, *waits)
    return result, low, sums[0], sums[1]


def spot_in(i, slot, blocks):
    return jnp.clip(i - slot * blocks, 0, blocks - 1)


def project_kernel(*refs, blocks):
    weight_ref, scale_ref, out_ref = refs[-3:]
    for s, ref in enumerate(refs[:-3]):

        @pl.when(pl.program_id(0) // blocks == s)
        def _(ref=ref):
            out_ref[...] = (dot_nt(ref[...], weight_ref[...]) * scale_ref[...]).astype(jnp.bfloat16)


def project(slots, weight, scale):
    tokens, width = slots[0].shape
    rows = min(256, tokens)
    blocks = tokens // rows
    units = weight.shape[0]
    return pl.pallas_call(
        functools.partial(project_kernel, blocks=blocks),
        grid=(len(slots) * blocks,),
        in_specs=[
            pl.BlockSpec((rows, width), functools.partial(lambda i, s: (spot_in(i, s, blocks), 0), s=s))
            for s in range(len(slots))
        ]
        + [WHOLE, WHOLE],
        out_specs=pl.BlockSpec((rows, units), lambda i: (i, 0)),
        out_shape=jax.ShapeDtypeStruct((len(slots) * tokens, units), jnp.bfloat16),
        compiler_params=pltpu.CompilerParams(vmem_limit_bytes=VMEM),
        cost_estimate=LIGHT,
    )(*slots, weight, scale)


def product_kernel(*refs, parts, added):
    weight_ref, out_ref = refs[parts], refs[-1]
    total = None
    at = 0
    for ref in refs[:parts]:
        depth = ref.shape[1]
        part = dot_nn(ref[...], weight_ref[at : at + depth, :])
        total = part if total is None else total + part
        at += depth
    for ref in refs[parts + 1 : parts + 1 + added]:
        total = total + ref[...].astype(jnp.float32)
    out_ref[...] = total.astype(out_ref.dtype)


def product(parts, slot, tokens, weight, addends, dtype, waits=()):
    rows = min(256, tokens)
    blocks = tokens // rows
    width = weight.shape[1]
    own = pl.BlockSpec((rows, width), lambda i: (i, 0))
    return pl.pallas_call(
        ignoring(
            functools.partial(product_kernel, parts=len(parts), added=len(addends)),
            len(parts) + 1 + len(addends),
            len(waits),
        ),
        grid=(blocks,),
        in_specs=[pl.BlockSpec((rows, part.shape[1]), lambda i: (slot * blocks + i, 0)) for part in parts]
        + [WHOLE]
        + [own] * len(addends)
        + [ANYWHERE] * len(waits),
        out_specs=own,
        out_shape=jax.ShapeDtypeStruct((tokens, width), dtype),
        compiler_params=pltpu.CompilerParams(vmem_limit_bytes=VMEM),
        cost_estimate=LIGHT,
    )(*parts, weight, *addends, *waits)


def unit_grads_kernel(me_ref, x_ref, *refs, slots, runs):
    outs = refs[slots:]
    tokens = refs[0].shape[0]
    total = None
    for k, ref in enumerate(refs[:slots]):
        part = dot_tn(x_ref[k * tokens : (k + 1) * tokens, :], ref[...])
        total = part if total is None else total + part
    low = total.astype(jnp.bfloat16)
    if len(outs) == 1:
        outs[0][...] = low
        return
    for s, ref in enumerate(outs):

        @pl.when(pl.program_id(0) // runs == s)
        def _(ref=ref):
            ref[...] = low


def unit_grads(x, slots, me, wide, split, waits=()):
    tokens, units = x.shape
    width = slots[0].shape[1]
    each = units // wide
    rows = min(256, each)
    runs = each // rows
    if split:
        out_specs = [
            pl.BlockSpec((rows, width), functools.partial(lambda i, m, s: (spot_in(i, s, runs), 0), s=s))
            for s in range(wide)
        ]
        out_shape = [jax.ShapeDtypeStruct((each, width), jnp.bfloat16)] * wide
    else:
        out_specs = pl.BlockSpec((rows, width), lambda i, m: (i, 0))
        out_shape = jax.ShapeDtypeStruct((units, width), jnp.bfloat16)
    grid_spec = pltpu.PrefetchScalarGridSpec(
        num_scalar_prefetch=1,
        grid=(units // rows,),
        in_specs=[pl.BlockSpec((tokens, rows), lambda i, m: (0, ((i // runs) ^ m[0]) * runs + i % runs))]
        + [WHOLE] * len(slots)
        + [ANYWHERE] * len(waits),
        out_specs=out_specs,
    )
    return pl.pallas_call(
        ignoring(
            functools.partial(unit_grads_kernel, slots=len(slots), runs=runs), 2 + len(slots), len(waits)
        ),
        grid_spec=grid_spec,
        out_shape=out_shape,
        compiler_params=pltpu.CompilerParams(vmem_limit_bytes=VMEM),
        cost_estimate=LIGHT,
    )(me, x, *slots, *waits)


def head_grads_kernel(me_ref, grads_ref, mixed_ref, *refs, group, wide):
    outs, low = refs[2 * group : 2 * group + wide], refs[-1]

    def give(left_ref, slots):
        tokens = slots[0].shape[0]
        total = None
        for k, ref in enumerate(slots):
            part = dot_tn(left_ref[k * tokens : (k + 1) * tokens, :], ref[...])
            total = part if total is None else total + part
        return total.astype(jnp.bfloat16)

    low[: 3 * PAIR] = give(grads_ref, refs[:group])
    low[3 * PAIR :] = give(mixed_ref, refs[group : 2 * group])
    rows = PAIR // wide
    for t in range(4):
        for s, ref in enumerate(outs):
            begin = pl.multiple_of(t * PAIR + (me_ref[0] ^ s) * rows, rows)
            ref[0, t] = low[pl.ds(begin, rows), :]


def head_grads(grads, mixed, a1, states, me, begin, wide):
    length = grads.shape[0]
    width = a1[0].shape[1]
    pairs = grads.shape[1] // (3 * PAIR)
    rows = PAIR // wide
    grid_spec = pltpu.PrefetchScalarGridSpec(
        num_scalar_prefetch=1,
        grid=(pairs,),
        in_specs=[
            pl.BlockSpec((length, 3 * PAIR), lambda p, m: (0, p)),
            pl.BlockSpec((length, PAIR), lambda p, m: (0, begin + p)),
        ]
        + [WHOLE] * (2 * len(states)),
        out_specs=[pl.BlockSpec((1, 4, rows, width), lambda p, m: (p, 0, 0, 0))] * wide,
        scratch_shapes=[pltpu.VMEM((4 * PAIR, width), jnp.bfloat16)],
    )
    return pl.pallas_call(
        functools.partial(head_grads_kernel, group=len(states), wide=wide),
        grid_spec=grid_spec,
        out_shape=[jax.ShapeDtypeStruct((pairs, 4, rows, width), jnp.bfloat16)] * wide,
        compiler_params=pltpu.CompilerParams(vmem_limit_bytes=VMEM),
        cost_estimate=LIGHT,
    )(me, grads, mixed, *a1, *states)


class Net:
    def __init__(self, wide, narrow, group):
        self.wide, self.narrow, self.group = wide, narrow, group
        self.ring = narrow // group

    def from_group(self, value, s):
        return lax.ppermute(value, "narrow", [(i, i ^ s) for i in range(self.narrow)])

    def from_ring(self, value, r):
        return self.from_group(value, r * self.group)

    def from_wide(self, value, s):
        return lax.ppermute(value, "wide", [(i, i ^ s) for i in range(self.wide)])

    def bit_order(self, turn):
        bits = self.wide.bit_length() - 1
        return [1 << ((b + turn) % bits) for b in range(bits)]

    def hops(self, unit, turn):
        return {bit: self.from_wide(unit, bit) for bit in self.bit_order(turn)}

    def spread(self, unit, turn, hops):
        pieces = {0: unit}
        for bit in self.bit_order(turn):
            more = {s ^ bit: self.from_wide(piece, bit) for s, piece in pieces.items() if s}
            pieces.update(more)
            pieces[bit] = hops[bit]
        return [pieces[s] for s in range(self.wide)]

    def scatter_wide(self, parts):
        return [parts[0]] + [self.from_wide(parts[s], s) for s in range(1, self.wide)]

    def spread_doubling(self, unit, turn):
        order, pieces = [0], [unit]
        for bit in self.bit_order(turn):
            away = self.from_wide(jnp.stack(pieces, axis=0), bit)
            order = order + [s ^ bit for s in order]
            pieces = pieces + [away[k] for k in range(len(pieces))]
        return [pieces[order.index(s)] for s in range(self.wide)]

    def swap_wide(self, parts):
        return lax.all_to_all(parts, "wide", 0, 0, tiled=True)

    def gather_wide(self, own):
        return self.swap_wide(jnp.broadcast_to(own[None], (self.wide,) + own.shape))

    def ring_slots(self, own):
        return [own] + [self.from_ring(own, r) for r in range(1, self.ring)]

    def total(self, value):
        value = value + sum(self.from_group(value, s) for s in range(1, self.group))
        value = value + sum(self.from_ring(value, r) for r in range(1, self.ring))
        return value + sum(self.from_wide(value, s) for s in range(1, self.wide))


def by_xor(parts, me):
    bit = 1
    while bit < len(parts):
        swap = me & bit != 0
        parts = [jnp.where(swap, parts[k ^ bit], part) for k, part in enumerate(parts)]
        bit *= 2
    return parts


def hold_kernel(*refs):
    pass


def after(value, *others):
    values, tree = jax.tree.flatten(value)
    waits = jax.tree.leaves(others)
    if len(values) + len(waits) < 2 or not values:
        return value
    held = pl.pallas_call(
        hold_kernel,
        in_specs=[ANYWHERE] * (len(values) + len(waits)),
        out_specs=[ANYWHERE] * len(values),
        out_shape=[jax.ShapeDtypeStruct(one.shape, one.dtype) for one in values],
        input_output_aliases={k: k for k in range(len(values))},
        cost_estimate=LIGHT,
    )(*values, *waits)
    return jax.tree.unflatten(tree, held)


def sum_low(parts):
    return jnp.sum(parts.astype(jnp.float32), axis=0).astype(jnp.bfloat16)


class RingSum:
    def __init__(self, net, parts):
        self.net, self.parts = net, list(parts)

    def send(self):
        keep = len(self.parts) // 2
        self.gone = jnp.stack(self.parts[keep:], axis=0)
        self.arrived = self.net.from_ring(self.gone, keep)
        return self

    def add(self):
        keep = len(self.parts) // 2
        self.parts = [sum_low(jnp.stack([part, self.arrived[k]])) for k, part in enumerate(self.parts[:keep])]
        return self


def place_rows_kernel(me_ref, *refs, order, rows, wide):
    sources, out_ref = refs[:-1], refs[-1]
    places = {}
    for at, (r, t, w) in enumerate(order):
        places[r, t, w] = at
    half = sources[0].shape[0]
    for r, t, w in order:
        ref = sources[(r // half) * wide + w]
        at = jnp.int32(0)
        true_r, true_w = me_ref[0] ^ r, me_ref[1] ^ w
        first_r = {k: places[k, t, 0] for k in {key[0] for key in places}}
        for k, begin in first_r.items():
            at = jnp.where(true_r == k, begin, at)
        begin = pl.multiple_of((at + true_w) * rows, rows)
        out_ref[pl.ds(begin, rows), :] = ref[r % half, t * rows : (t + 1) * rows]


def place_rows(me, sources, order, rows, wide, waits=()):
    return pl.pallas_call(
        ignoring(
            functools.partial(place_rows_kernel, order=order, rows=rows, wide=wide), 1 + len(sources), len(waits)
        ),
        in_specs=[pl.BlockSpec(memory_space=pltpu.SMEM)] + [WHOLE] * len(sources) + [ANYWHERE] * len(waits),
        out_specs=WHOLE,
        out_shape=jax.ShapeDtypeStruct((len(order) * rows, sources[0].shape[-1]), sources[0].dtype),
        compiler_params=pltpu.CompilerParams(vmem_limit_bytes=VMEM),
        cost_estimate=LIGHT,
    )(me, *sources, *waits)


def place_units_kernel(me_ref, *refs, ring, wide):
    sources, out_ref = refs[:wide], refs[wide]
    unit = out_ref.shape[0] // (ring * wide)
    for s, ref in enumerate(sources):
        for r in range(ring):
            begin = pl.multiple_of(((me_ref[1] ^ s) * ring + (me_ref[0] ^ r)) * unit, unit)
            out_ref[pl.ds(begin, unit), :] = ref[r]


def place_units(me, pieces, ring):
    wide = len(pieces)
    unit, width = pieces[0].shape[1:]
    return pl.pallas_call(
        functools.partial(place_units_kernel, ring=ring, wide=wide),
        in_specs=[pl.BlockSpec(memory_space=pltpu.SMEM)] + [WHOLE] * wide,
        out_specs=WHOLE,
        out_shape=jax.ShapeDtypeStruct((wide * ring * unit, width), pieces[0].dtype),
        compiler_params=pltpu.CompilerParams(vmem_limit_bytes=VMEM),
        cost_estimate=LIGHT,
    )(me, *pieces)


def on_device(
    inputs,
    seg_ids,
    buckets,
    norm1_gain,
    norm1_shift,
    w_query,
    w_key,
    w_value,
    w_out,
    norm2_gain,
    norm2_shift,
    w_up,
    w_down,
    rel_table,
    out_grad,
    *,
    wide,
    narrow,
):
    bf16, f32 = jnp.bfloat16, jnp.float32
    tokens, width = inputs.shape
    length = seg_ids.shape[1]
    group = length // tokens
    net = Net(wide, narrow, group)
    ring = net.ring
    head_rows = w_query.shape[0]
    heads_here = rel_table.shape[1]
    piece_rows = head_rows // wide
    scale = HD ** (-0.5)
    block = min(256, tokens)
    per_slot = tokens // block
    blocks = length // block
    reach_blocks = min(blocks, -(-REACH // block) + 1)
    me_wide = lax.axis_index("wide")
    me_narrow = lax.axis_index("narrow")
    me_group = me_narrow % group
    me_ring = me_narrow // group

    def my_part(shard, axis=0):
        size = shard.shape[axis] // wide
        return lax.dynamic_slice_in_dim(shard, me_wide * size, size, axis)

    def slot(value, s):
        return value[s * tokens : (s + 1) * tokens]

    table_low = []
    left = rel_table
    for _ in range(3):
        table_low.append(lax.reduce_precision(left, 8, 7))
        left = left - table_low[-1]
    table_flat = jnp.stack(table_low, axis=0).astype(bf16).reshape(-1)
    table_row = jnp.pad(table_flat, (0, 16 * width - table_flat.size)).reshape(16, width)
    attention_quarter = my_part(jnp.stack([w_query, w_key, w_value, w_out], axis=0), 1).reshape(-1, width)
    attention_rows = attention_quarter.shape[0]
    first_parts = net.ring_slots(jnp.concatenate([attention_quarter, table_row], axis=0))
    tables = [
        jnp.sum(part[attention_rows, : table_flat.size].reshape((3,) + rel_table.shape).astype(f32), axis=0)
        for part in first_parts
    ]
    tables = by_xor(tables, me_ring)
    cut_ring = ring // 2
    attention_pieces = [
        net.spread_doubling(jnp.stack([part[:attention_rows] for part in half], axis=0), turn)
        for turn, half in enumerate([first_parts[:cut_ring], first_parts[cut_ring:]])
    ]
    ffn_own = jnp.concatenate([my_part(w_up, 1).T, my_part(w_down)], axis=0)
    unit = ffn_own.shape[0] // 2

    values_in = inputs.astype(f32)
    normed1, inverse1 = row_norm(values_in)
    a1_own = (normed1 * norm1_gain + norm1_shift).astype(bf16)
    a1_away = [net.from_group(a1_own, s) for s in range(1, group)]
    a1 = [a1_own] + a1_away
    dy_away = [net.from_group(out_grad, s) for s in range(1, group)]
    dy = [out_grad] + dy_away
    ffn_slots = net.ring_slots(after(ffn_own, first_parts[1:]))
    ffn_units = [jnp.stack([rows[k * unit : (k + 1) * unit] for rows in ffn_slots], axis=0) for k in range(2)]
    ffn_hops = [net.hops(units, k) for k, units in enumerate(ffn_units)]

    per_pair = PAIR // head_rows
    pairs = ring // per_pair
    order = [
        (p * per_pair + r, t, w)
        for p in range(pairs)
        for t in range(3)
        for r in range(per_pair)
        for w in range(wide)
    ] + [(r, 3, w) for r in range(ring) for w in range(wide)]
    cut_at = 3 * ring * wide

    me = jnp.stack([me_ring, me_wide]).astype(jnp.int32)
    sources = attention_pieces[0] + attention_pieces[1]
    w_joined = place_rows(me, sources, order[:cut_at], piece_rows, wide, dy_away + ffn_units)
    w_out_full = place_rows(me, sources, order[cut_at:], piece_rows, wide)
    column_kind = (jnp.arange(w_joined.shape[0]) // PAIR) % 3
    column_scale = jnp.where(column_kind == 0, jnp.asarray(scale, f32), jnp.asarray(1.0, f32))
    joined = project(a1, w_joined, column_scale[None])

    reach = reach_blocks * block
    one_hot = (buckets[:reach, None] == jnp.arange(rel_table.shape[0])[None, :]).astype(f32)

    table_here = jnp.concatenate([tables[r] for r in range(ring)], axis=1)
    line = jnp.dot(one_hot, table_here, precision=lax.Precision.HIGHEST, preferred_element_type=f32).T
    lines = jnp.concatenate([jnp.full((line.shape[0], block), MASKED_SCORE, f32), line], axis=1)

    segments = lax.dynamic_slice_in_dim(seg_ids, me_ring, 1, 0)[0]
    first = jnp.sum((segments[None, :] < segments[:, None]).astype(jnp.int32), axis=1)
    scalars = jnp.concatenate([me_group[None], first[::block] // block]).astype(jnp.int32)
    first = first.reshape(blocks, block)

    mixed, lse = attend(joined, first, lines, scalars, block, per_slot, ffn_units)
    mixed, ffn_hops = after((mixed, ffn_hops))
    ffn_pieces = [net.spread(units, k, ffn_hops[k]) for k, units in enumerate(ffn_units)]

    attended_part = [product([mixed], s, tokens, w_out_full, [], bf16) for s in range(1, group)]
    attended_away = [net.from_group(part, s + 1) for s, part in enumerate(attended_part)]
    hidden_state = product([mixed], 0, tokens, w_out_full, [inputs] + attended_away, f32)
    normed2, inverse2 = row_norm(hidden_state)
    a2_own = (normed2 * norm2_gain + norm2_shift).astype(bf16)
    a2_own, ffn_pieces = after((a2_own, ffn_pieces))
    a2 = [a2_own] + [net.from_group(a2_own, s) for s in range(1, group)]

    w_up_t, w_down_full = (place_units(me, pieces, ring) for pieces in ffn_pieces)
    active, up_grad, *normed2_part = hidden_units(a2, dy, w_up_t, w_down_full)
    normed2_away = [net.from_group(normed2_part[s], s) for s in range(1, group)]
    here = jnp.zeros((1,), jnp.int32)
    down_grads = unit_grads(active, dy, here, wide, False).reshape(wide, -1, width)
    down_parts = net.swap_wide(down_grads)
    state_grad, state_low, grad_gain2, grad_shift2 = norm_back(
        hidden_state, out_grad, norm2_gain, [normed2_part[0]] + normed2_away, [down_grads]
    )
    state_away = [net.from_group(state_low, s) for s in range(1, group)]
    up_grads = unit_grads(up_grad, a2, me[1:], wide, True, [state_low])
    states = [state_low] + after(state_away, up_grads)
    mixed_grad = project(states, w_out_full, jnp.ones((1, w_out_full.shape[0]), f32))
    feed_part = [product([active], s, tokens, w_down_full, [], bf16, [mixed_grad]) for s in range(1, group)]
    feed_away = [net.from_group(rows, s + 1) for s, rows in enumerate(feed_part)]

    def grads_of(begin, end, waits):
        return attend_back(
            joined, mixed, mixed_grad, first, lines, lse, scalars, block, per_slot, begin, end, waits
        )

    def attention_grads(grads, begin, end, place):
        if per_pair == 1 and piece_rows % 16 == 0:
            return head_grads(grads, mixed, a1, states, place, begin, wide)
        grad_part = sum(dot_tn(slot(grads, s), rows) for s, rows in enumerate(a1)).astype(bf16).reshape(end - begin, 3, per_pair, wide, piece_rows, width)
        grad_part = jnp.transpose(grad_part, (3, 0, 2, 1, 4, 5)).reshape(wide, -1, 3, piece_rows, width)
        columns = slice(begin * PAIR, end * PAIR)
        grad_out = sum(dot_tn(slot(mixed, s)[:, columns], state) for s, state in enumerate(states)).astype(bf16)
        grad_out = jnp.moveaxis(grad_out.reshape(-1, wide, 1, piece_rows, width), 1, 0)
        whole = jnp.concatenate([grad_part, grad_out], axis=2)
        return by_xor([whole[w] for w in range(wide)], place[0])

    cut = pairs // 2
    up_parts = net.scatter_wide(up_grads)
    grads_a, lines_a = grads_of(0, cut, list(up_grads) + feed_part)
    grads_a, down_parts = after((grads_a, down_parts))
    head_a = attention_grads(grads_a, 0, cut, me[1:])
    head_a, up_parts = after((head_a, up_parts))
    parts_a = net.scatter_wide(head_a)
    down_low = sum_low(down_parts).reshape(ring, -1, width)
    up_low = sum_low(jnp.stack(up_parts)).reshape(ring, -1, width)
    ffn_low = jnp.concatenate([down_low, up_low], axis=1)
    ffn_ring = RingSum(net, by_xor([ffn_low[z] for z in range(ring)], me_ring)).send()
    grads_b, lines_b = grads_of(cut, pairs, list(head_a) + [ffn_ring.gone])
    grads_b, ffn_ring.arrived, parts_a = after((grads_b, ffn_ring.arrived, parts_a))
    ffn_ring.add().send()
    head_b = attention_grads(grads_b, cut, pairs, me[1:])
    parts_b = net.scatter_wide(head_b)
    all_grads, all_lines = [grads_a, grads_b], [lines_a, lines_b]

    w_late = after(w_joined, head_b, ffn_ring.gone)

    normed1_part = [product(all_grads, s, tokens, w_late, [], bf16) for s in range(1, group)]
    normed1_away = [net.from_group(part, s + 1) for s, part in enumerate(normed1_part)]
    w_late, ffn_ring.arrived = after((w_late, ffn_ring.arrived), normed1_part)
    normed1_own = product(all_grads, 0, tokens, w_late, [], f32)
    parts_b = after(parts_b, normed1_own)
    head_low = jnp.concatenate([sum_low(jnp.stack(parts_a)), sum_low(jnp.stack(parts_b))], axis=0)
    head_ring = RingSum(net, by_xor([head_low[z] for z in range(ring)], me_ring)).send()
    ffn_part = after(ffn_ring.add().parts[0], head_ring.gone)
    ffn_pieces = [net.from_wide(ffn_part, s) for s in range(1, wide)]
    out = product(
        [active], 0, tokens, w_down_full, [hidden_state] + feed_away, bf16, [head_ring.gone, ffn_part]
    )
    input_grad, _, grad_gain1, grad_shift1 = norm_back(
        inputs, state_grad, norm1_gain, [normed1_own] + normed1_away, [out] + ffn_pieces
    )

    line_grad = jnp.concatenate(all_lines, axis=0)[:, block:]
    table_grad = jnp.dot(line_grad, one_hot, precision=lax.Precision.HIGHEST, preferred_element_type=f32)
    all_heads = heads_here * narrow
    head_ids = jnp.stack([(r * group + me_group) * heads_here + h for r in range(ring) for h in range(heads_here)])
    placed = (jnp.arange(all_heads)[:, None] == head_ids[None, :]).astype(f32)
    table_all = jnp.dot(placed, table_grad, precision=lax.Precision.HIGHEST, preferred_element_type=f32)

    small = jnp.concatenate([grad_gain1, grad_shift1, grad_gain2, grad_shift2, table_all.reshape(-1)])
    pad = -small.shape[0] % 1024
    small_own = small
    small = jnp.pad(small, (0, pad)).reshape(-1, 128)
    small = small + sum(net.from_group(small, s) for s in range(1, group))
    small = small + sum(net.from_wide(small, s) for s in range(1, wide))
    head_ring.arrived = after(head_ring.arrived, small_own)
    head_ring.add().send()
    small, head_gone = after((small, head_ring.gone))
    small = small + sum(net.from_ring(small, r) for r in range(1, ring))
    small = small.reshape(-1)
    gain1, shift1, gain2, shift2 = (small[k * width : (k + 1) * width] for k in range(4))
    table_sum = small[4 * width : 4 * width + table_all.size].reshape(table_all.shape)
    table_out = lax.dynamic_slice_in_dim(table_sum, me_narrow * heads_here, heads_here, 0).T

    attention_part = head_ring.add().parts[0]
    attention_part = jnp.broadcast_to(after(attention_part, small_own)[None], (wide,) + attention_part.shape)
    ffn_pieces = after(ffn_pieces, attention_part)
    ffn_all = jnp.stack(by_xor([ffn_part] + ffn_pieces, me_wide), axis=0)
    down_all = ffn_all[:, :unit].reshape(-1, width).astype(f32)
    up_all = ffn_all[:, unit:].reshape(-1, width).T.astype(f32)
    attention_all = net.swap_wide(attention_part)
    attention_all = jnp.moveaxis(attention_all, 1, 0).reshape(4, head_rows, width).astype(f32)
    return (
        out,
        input_grad,
        gain1,
        shift1,
        attention_all[0],
        attention_all[1],
        attention_all[2],
        attention_all[3],
        gain2,
        shift2,
        up_all,
        down_all,
        table_out,
    )


def solution(mesh):
    placed = (
        P(("wide", "narrow"), None),
        P("wide", None),
        P(),
        P(),
        P(),
        P("narrow", None),
        P("narrow", None),
        P("narrow", None),
        P("narrow", None),
        P(),
        P(),
        P(None, "narrow"),
        P("narrow", None),
        P(None, "narrow"),
        P(("wide", "narrow"), None),
    )
    return jax.shard_map(
        functools.partial(on_device, wide=mesh.shape["wide"], narrow=mesh.shape["narrow"]),
        mesh=mesh,
        in_specs=placed,
        out_specs=(
            P(("wide", "narrow"), None),
            P(("wide", "narrow"), None),
            P(),
            P(),
            P("narrow", None),
            P("narrow", None),
            P("narrow", None),
            P("narrow", None),
            P(),
            P(),
            P(None, "narrow"),
            P("narrow", None),
            P(None, "narrow"),
        ),
        check_vma=False,
    )
```

```python
import functools
import math

import jax
import jax.numpy as jnp
from jax import lax
from jax.experimental import pallas as pl
from jax.experimental.pallas import tpu as pltpu
from jax.sharding import PartitionSpec as P

HD = 64
PAIR = 128
REACH = 1024
EPSILON = 1e-05
MASKED_SCORE = -1e30
ROOT = (2.0 / 3.141592653589793) ** 0.5
VMEM = 60 * 1024 * 1024
LIGHT = pl.CostEstimate(flops=1, bytes_accessed=1, transcendentals=0)
NT = (((1,), (1,)), ((), ()))
TN = (((0,), (0,)), ((), ()))


def row_norm(values):
    mean = jnp.mean(values, axis=1, keepdims=True)
    centred = values - mean
    spread = jnp.mean(centred * centred, axis=1, keepdims=True)
    inverse = lax.rsqrt(spread + EPSILON)
    return (centred * inverse, inverse)


def norm_backward(upstream, normed, inverse, gain):
    scaled = upstream * gain
    mean_plain = jnp.mean(scaled, axis=1, keepdims=True)
    mean_cross = jnp.mean(scaled * normed, axis=1, keepdims=True)
    result = inverse * (scaled - mean_plain - normed * mean_cross)
    return (result, jnp.sum(upstream * normed, axis=0), jnp.sum(upstream, axis=0))


def dot_nt(left, right):
    return lax.dot_general(left, right, NT, preferred_element_type=jnp.float32)


def dot_nn(left, right):
    return jnp.dot(left, right, preferred_element_type=jnp.float32)


def dot_tn(left, right):
    return lax.dot_general(left, right, TN, preferred_element_type=jnp.float32)


def make_strip(line_ref, strips, begin=0):
    for h in range(strips.shape[0]):
        spread = jnp.broadcast_to(line_ref[begin + h : begin + h + 1, :], strips.shape[1:])
        strips[h] = pltpu.roll(spread, 0, 1, stride=1, stride_axis=0)


def strip_line(strip):
    rows, span = strip.shape
    while rows > 1:
        rows //= 2
        strip = strip[:rows] + pltpu.roll(strip[rows : 2 * rows], span - rows, 1)
    return strip


def strip_at(t, u, rows, block):
    return pl.ds(pl.multiple_of(t * block + (block - u * rows), rows), block)


def strip_tile(strips, h, t, block):
    rows = strips.shape[1]
    parts = [strips[h, :, strip_at(t, u, rows, block)] for u in range(block // rows)]
    return jnp.concatenate(parts, axis=0)


def add_to_strip(strips, h, t, tile):
    rows, block = strips.shape[1], tile.shape[0]
    for u in range(block // rows):
        strips[h, :, strip_at(t, u, rows, block)] += tile[u * rows : (u + 1) * rows]


def place_of(index, me, per_slot):
    return ((index // per_slot) ^ me) * per_slot + index % per_slot


def head_lanes(block, h):
    lanes = lax.broadcasted_iota(jnp.int32, block.shape, 1)
    return jnp.where((lanes // HD) == h, block, jnp.zeros_like(block))


def columns_of(p, kind):
    return slice((3 * p + kind) * PAIR, (3 * p + kind + 1) * PAIR)


def attend_kernel(scalars, x_ref, first_ref, line_ref, out_ref, lse_ref, strips, v_t, kept, *, block, per_slot):
    i = pl.program_id(0)
    me = scalars[0]
    low = scalars[1 + i]
    heads = strips.shape[0]
    pairs = heads // 2

    @pl.when(i == 0)
    def _():
        make_strip(line_ref, strips)
        for p in range(pairs):
            v_t[p * PAIR : (p + 1) * PAIR] = x_ref[:, columns_of(p, 2)].T

    rows = pl.ds(pl.multiple_of(place_of(i, me, per_slot) * block, block), block)
    own = [head_lanes(x_ref[rows, columns_of(h // 2, 0)], h % 2) for h in range(heads)]
    first = first_ref[pl.ds(i, 1), :]
    key_index = lax.broadcasted_iota(jnp.int32, (block, block), 0)

    def rows_of(t):
        return pl.ds(pl.multiple_of(place_of(i - t, me, per_slot) * block, block), block)

    def fold(value):
        return value.reshape(block // 8, 8, block)

    def score_step(t, tops):
        here = rows_of(t)
        allowed = key_index >= (first - (i - t) * block)
        result = []
        for h in range(heads):
            scores = dot_nt(x_ref[here, columns_of(h // 2, 1)], own[h]) + strip_tile(strips, h, t, block)
            scores = jnp.where(allowed, scores, MASKED_SCORE)
            kept[h, t] = scores
            result.append(jnp.maximum(tops[h], jnp.max(fold(scores), axis=0)))
        return tuple(result)

    def value_step(t, carry):
        here = rows_of(t)
        result = []
        for h in range(heads):
            total, acc = carry[h]
            expo = jnp.exp(kept[h, t] - tops[h])
            total = total + jnp.sum(fold(expo), axis=0)
            acc = acc + dot_nn(v_t[h * HD : (h + 1) * HD, here], expo.astype(jnp.bfloat16))
            result.append((total, acc))
        return tuple(result)

    tops = lax.fori_loop(
        0, i - low + 1, score_step, (jnp.full((8, block), MASKED_SCORE, jnp.float32),) * heads
    )
    tops = [jnp.max(top, axis=0, keepdims=True) for top in tops]
    zero = (jnp.zeros((8, block), jnp.float32), jnp.zeros((HD, block), jnp.float32))
    done = lax.fori_loop(0, i - low + 1, value_step, (zero,) * heads)
    totals = [jnp.sum(total, axis=0, keepdims=True) for total, _ in done]
    for p in range(pairs):
        both = jnp.concatenate([done[h][1] / totals[h] for h in (2 * p, 2 * p + 1)], axis=0)
        out_ref[rows, p * PAIR : (p + 1) * PAIR] = both.T.astype(jnp.bfloat16)
    lse_ref[pl.ds(i, 1)] = jnp.concatenate([tops[h] + jnp.log(totals[h]) for h in range(heads)], axis=0)[None]


def attend_back_kernel(
    scalars,
    x_ref,
    mixed_ref,
    up_ref,
    first_ref,
    line_ref,
    lse_ref,
    grad_ref,
    sums_ref,
    strips,
    sums,
    k_t,
    dk,
    dv,
    *,
    block,
    per_slot,
    begin,
):
    i = pl.program_id(0)
    me = scalars[0]
    low = scalars[1 + i]
    heads = strips.shape[0]
    pairs = heads // 2

    columns = columns_of

    def wide_columns(p):
        return slice(p * PAIR, (p + 1) * PAIR)

    @pl.when(i == 0)
    def _():
        make_strip(line_ref, strips, 2 * begin)
        for p in range(pairs):
            k_t[p * PAIR : (p + 1) * PAIR] = x_ref[:, columns(p, 1)].T
        dk[...] = jnp.zeros_like(dk)
        dv[...] = jnp.zeros_like(dv)
        sums[...] = jnp.zeros_like(sums)

    rows = pl.ds(pl.multiple_of(place_of(i, me, per_slot) * block, block), block)
    own_q = [head_lanes(x_ref[rows, columns(h // 2, 0)], h % 2) for h in range(heads)]
    own_up = [head_lanes(up_ref[rows, wide_columns(h // 2)], h % 2) for h in range(heads)]
    picks = lax.broadcasted_iota(jnp.int32, (8, PAIR), 1) // HD == lax.broadcasted_iota(jnp.int32, (8, PAIR), 0)
    picks = picks.astype(jnp.bfloat16)
    deltas = []
    for p in range(pairs):
        span = wide_columns(p)
        product = up_ref[rows, span].astype(jnp.float32) * mixed_ref[rows, span].astype(jnp.float32)
        high = product.astype(jnp.bfloat16)
        rest = (product - high.astype(jnp.float32)).astype(jnp.bfloat16)
        both = dot_nt(picks, high) + dot_nt(picks, rest)
        deltas += [both[0:1], both[1:2]]
    first = first_ref[pl.ds(i, 1), :]
    key_index = lax.broadcasted_iota(jnp.int32, (block, block), 0)

    def step(t, carry):
        here = pl.ds(pl.multiple_of(place_of(i - t, me, per_slot) * block, block), block)
        allowed = key_index >= (first - (i - t) * block)
        dq = []
        for p in range(pairs):
            span = slice(p * PAIR, (p + 1) * PAIR)
            keys = x_ref[here, columns(p, 1)]
            values = x_ref[here, columns(p, 2)]
            dk_new = dk[here, span]
            dv_new = dv[here, span]
            both_scores = dot_nt(keys, jnp.concatenate(own_q[2 * p : 2 * p + 2], axis=0))
            both_grads = dot_nt(values, jnp.concatenate(own_up[2 * p : 2 * p + 2], axis=0))
            for h in (2 * p, 2 * p + 1):
                half = slice((h - 2 * p) * block, (h - 2 * p + 1) * block)
                scores = both_scores[:, half] + strip_tile(strips, h, t, block)
                scores = jnp.where(allowed, scores, MASKED_SCORE)
                probs = jnp.exp(scores - lse_ref[i, 2 * begin + h : 2 * begin + h + 1, :])
                score_grad = probs * (both_grads[:, half] - deltas[h])
                add_to_strip(sums, h, t, score_grad)
                low_grad = score_grad.astype(jnp.bfloat16)
                dv_new = dv_new + dot_nn(probs.astype(jnp.bfloat16), own_up[h])
                dk_new = dk_new + dot_nn(low_grad, own_q[h])
                dq.append(carry[h] + dot_nn(k_t[h * HD : (h + 1) * HD, here], low_grad))
            dk[here, span] = dk_new
            dv[here, span] = dv_new
        return tuple(dq)

    dq = lax.fori_loop(0, i - low + 1, step, (jnp.zeros((HD, block), jnp.float32),) * heads)
    for p in range(pairs):
        both = jnp.concatenate(dq[2 * p : 2 * p + 2], axis=0).T * (HD ** (-0.5))
        grad_ref[rows, columns_of(p, 0)] = both.astype(jnp.bfloat16)

    @pl.when(i == pl.num_programs(0) - 1)
    def _():
        for p in range(pairs):
            span = slice(p * PAIR, (p + 1) * PAIR)
            grad_ref[:, columns_of(p, 1)] = dk[:, span].astype(jnp.bfloat16)
            grad_ref[:, columns_of(p, 2)] = dv[:, span].astype(jnp.bfloat16)
        for h in range(heads):
            sums_ref[h : h + 1, :] = strip_line(sums[h])


WHOLE = pl.BlockSpec(memory_space=pltpu.VMEM)
ANYWHERE = pl.BlockSpec(memory_space=pl.ANY)


def ignoring(kernel, first, count):
    def body(*refs):
        kernel(*refs[:first], *refs[first + count :])

    return body


def attend(joined, first, lines, scalars, block, per_slot, waits):
    length = joined.shape[0]
    heads, span = lines.shape
    blocks = length // block
    strip = pltpu.VMEM((heads, min(128, block), span), jnp.float32)
    grid_spec = pltpu.PrefetchScalarGridSpec(
        num_scalar_prefetch=1,
        grid=(blocks,),
        in_specs=[WHOLE] * 3 + [ANYWHERE] * len(waits),
        out_specs=[WHOLE] * 2,
        scratch_shapes=[
            strip,
            pltpu.VMEM((heads * HD, length), jnp.bfloat16),
            pltpu.VMEM((heads, span // block - 1, block, block), jnp.float32),
        ],
    )
    return pl.pallas_call(
        ignoring(functools.partial(attend_kernel, block=block, per_slot=per_slot), 4, len(waits)),
        grid_spec=grid_spec,
        out_shape=[
            jax.ShapeDtypeStruct((length, heads * HD), jnp.bfloat16),
            jax.ShapeDtypeStruct((blocks, heads, block), jnp.float32),
        ],
        compiler_params=pltpu.CompilerParams(vmem_limit_bytes=VMEM),
        cost_estimate=LIGHT,
    )(scalars, joined, first, lines, *waits)


def attend_back(joined, mixed, upstream, first, lines, lse, scalars, block, per_slot, begin, end, waits):
    length = joined.shape[0]
    span = lines.shape[1]
    heads = 2 * (end - begin)
    part = begin // (end - begin)
    blocks = length // block
    strip = pltpu.VMEM((heads, min(128, block), span), jnp.float32)
    grid_spec = pltpu.PrefetchScalarGridSpec(
        num_scalar_prefetch=1,
        grid=(blocks,),
        in_specs=[
            pl.BlockSpec((length, 3 * heads * HD), lambda i, s: (0, part)),
            pl.BlockSpec((length, heads * HD), lambda i, s: (0, part)),
            pl.BlockSpec((length, heads * HD), lambda i, s: (0, part)),
        ]
        + [WHOLE] * 3
        + [ANYWHERE] * len(waits),
        out_specs=[WHOLE] * 2,
        scratch_shapes=[
            strip,
            strip,
            pltpu.VMEM((heads * HD, length), jnp.bfloat16),
            pltpu.VMEM((length, heads * HD), jnp.float32),
            pltpu.VMEM((length, heads * HD), jnp.float32),
        ],
    )
    return pl.pallas_call(
        ignoring(
            functools.partial(attend_back_kernel, block=block, per_slot=per_slot, begin=begin), 7, len(waits)
        ),
        grid_spec=grid_spec,
        out_shape=[
            jax.ShapeDtypeStruct((length, 3 * heads * HD), jnp.bfloat16),
            jax.ShapeDtypeStruct((heads, span), jnp.float32),
        ],
        compiler_params=pltpu.CompilerParams(vmem_limit_bytes=VMEM),
        cost_estimate=LIGHT,
    )(scalars, joined, mixed, upstream, first, lines, lse, *waits)


def hidden_kernel(*refs, slots, blocks, wide, chunk):
    a2_refs, dy_refs = refs[:slots], refs[slots : 2 * slots]
    at = 2 * slots
    up_parts, down_parts = refs[at : at + wide], refs[at + wide : at + 2 * wide]
    act_ref, up_grad_ref = refs[at + 2 * wide : at + 2 * wide + 2]
    back_refs = refs[at + 2 * wide + 2 : -2]
    up_ref, down_ref = refs[-2:]

    @pl.when(pl.program_id(0) == 0)
    def _():
        each = up_ref.shape[0] // wide
        for s in range(wide):
            up_ref[s * each : (s + 1) * each, :] = up_parts[s][...].reshape(each, up_ref.shape[1])
            down_ref[s * each : (s + 1) * each, :] = down_parts[s][...].reshape(each, up_ref.shape[1])

    for s in range(slots):

        @pl.when(pl.program_id(0) // blocks == s)
        def _(s=s):
            tokens = a2_refs[s][...]
            grads = dy_refs[s][...]
            total = jnp.zeros(tokens.shape, jnp.float32)
            for begin in range(0, up_ref.shape[0], chunk):
                rows = slice(begin, begin + chunk)
                x = dot_nt(tokens, up_ref[rows, :])
                square = x * x
                bend = jnp.tanh(x * (ROOT + ROOT * 0.044715 * square))
                half = 0.5 + 0.5 * bend
                act_ref[:, rows] = (x * half).astype(jnp.bfloat16)
                slope = half + 0.5 * x * (1.0 - bend * bend) * (ROOT + 3.0 * ROOT * 0.044715 * square)
                up_grad = (dot_nt(grads, down_ref[rows, :]) * slope).astype(jnp.bfloat16)
                up_grad_ref[:, rows] = up_grad
                total = total + dot_nn(up_grad, up_ref[rows, :])
            back_refs[s][...] = total.astype(jnp.bfloat16)


def hidden_units(a2, dy, up_parts, down_parts):
    tokens, width = a2[0].shape
    slots, wide = len(a2), len(up_parts)
    units = wide * up_parts[0].shape[0] * up_parts[0].shape[1]
    block = min(256, tokens)
    blocks = tokens // block
    unit_block = pl.BlockSpec((block, units), lambda i: (i, 0))
    by_slot = [
        pl.BlockSpec((block, width), functools.partial(lambda i, s: (spot_in(i, s, blocks), 0), s=s))
        for s in range(slots)
    ]
    return pl.pallas_call(
        functools.partial(hidden_kernel, slots=slots, blocks=blocks, wide=wide, chunk=min(1024, units)),
        grid=(slots * blocks,),
        in_specs=by_slot + by_slot + [WHOLE] * (2 * wide),
        out_specs=[unit_block, unit_block] + by_slot,
        out_shape=[jax.ShapeDtypeStruct((slots * tokens, units), jnp.bfloat16)] * 2
        + [jax.ShapeDtypeStruct((tokens, width), jnp.bfloat16)] * slots,
        scratch_shapes=[pltpu.VMEM((units, width), jnp.bfloat16)] * 2,
        compiler_params=pltpu.CompilerParams(vmem_limit_bytes=VMEM),
        cost_estimate=LIGHT,
    )(*a2, *dy, *up_parts, *down_parts)


def norm_back_kernel(*refs, parts):
    values_ref, add_ref, gain_ref = refs[:3]
    part_refs = refs[3 : 3 + parts]
    out_ref, low_ref, sums_ref = refs[3 + parts :]
    values = values_ref[...].astype(jnp.float32)
    normed, inverse = row_norm(values)
    upstream = part_refs[0][...].astype(jnp.float32)
    for ref in part_refs[1:]:
        upstream = upstream + ref[...].astype(jnp.float32)
    result, gain_grad, shift_grad = norm_backward(upstream, normed, inverse, gain_ref[...])
    result = result + add_ref[...].astype(jnp.float32)
    out_ref[...] = result
    low_ref[...] = result.astype(jnp.bfloat16)

    @pl.when(pl.program_id(0) == 0)
    def _():
        sums_ref[...] = jnp.zeros_like(sums_ref)

    sums_ref[0:1, :] += gain_grad[None]
    sums_ref[1:2, :] += shift_grad[None]


def norm_back(values, add, gain, parts, waits=()):
    tokens, width = values.shape
    block = min(512, tokens)
    rows = pl.BlockSpec((block, width), lambda i: (i, 0))
    result, low, sums = pl.pallas_call(
        ignoring(functools.partial(norm_back_kernel, parts=len(parts)), 3 + len(parts), len(waits)),
        grid=(tokens // block,),
        in_specs=[rows, rows, pl.BlockSpec((1, width), lambda i: (0, 0))]
        + [rows] * len(parts)
        + [ANYWHERE] * len(waits),
        out_specs=[rows, rows, pl.BlockSpec((8, width), lambda i: (0, 0))],
        out_shape=[
            jax.ShapeDtypeStruct((tokens, width), jnp.float32),
            jax.ShapeDtypeStruct((tokens, width), jnp.bfloat16),
            jax.ShapeDtypeStruct((8, width), jnp.float32),
        ],
        compiler_params=pltpu.CompilerParams(vmem_limit_bytes=VMEM),
        cost_estimate=LIGHT,
    )(values, add, gain[None], *parts, *waits)
    return result, low, sums[0], sums[1]


def spot_in(i, slot, blocks):
    return jnp.clip(i - slot * blocks, 0, blocks - 1)


def project_kernel(*refs, blocks):
    weight_ref, scale_ref, out_ref = refs[-3:]
    for s, ref in enumerate(refs[:-3]):

        @pl.when(pl.program_id(0) // blocks == s)
        def _(ref=ref):
            out_ref[...] = (dot_nt(ref[...], weight_ref[...]) * scale_ref[...]).astype(jnp.bfloat16)


def project(slots, weight, scale):
    tokens, width = slots[0].shape
    rows = min(512, tokens)
    blocks = tokens // rows
    units = weight.shape[0]
    return pl.pallas_call(
        functools.partial(project_kernel, blocks=blocks),
        grid=(len(slots) * blocks,),
        in_specs=[
            pl.BlockSpec((rows, width), functools.partial(lambda i, s: (spot_in(i, s, blocks), 0), s=s))
            for s in range(len(slots))
        ]
        + [WHOLE, WHOLE],
        out_specs=pl.BlockSpec((rows, units), lambda i: (i, 0)),
        out_shape=jax.ShapeDtypeStruct((len(slots) * tokens, units), jnp.bfloat16),
        compiler_params=pltpu.CompilerParams(vmem_limit_bytes=VMEM),
        cost_estimate=LIGHT,
    )(*slots, weight, scale)


def product_kernel(*refs, parts, weights, added):
    sides = refs[:parts]
    weight_refs = refs[parts : parts + weights]
    out_ref = refs[-1]
    depth = min([ref.shape[1] for ref in sides] + [math.prod(ref.shape[:-1]) for ref in weight_refs])
    total = None
    for at in range(0, sum(ref.shape[1] for ref in sides), depth):
        ref, here = sides[at // sides[0].shape[1]], at % sides[0].shape[1]
        rows = math.prod(weight_refs[0].shape[:-1])
        weight_ref, there = weight_refs[at // rows], at % rows
        if len(weight_ref.shape) == 2:
            weight = weight_ref[there : there + depth, :]
        else:
            weight = weight_ref[...].reshape(rows, weight_ref.shape[-1])
        part = dot_nn(ref[:, here : here + depth], weight)
        total = part if total is None else total + part
    for ref in refs[parts + weights : parts + weights + added]:
        total = total + ref[...].astype(jnp.float32)
    out_ref[...] = total.astype(out_ref.dtype)


def product(parts, slot, tokens, weights, addends, dtype, waits=()):
    rows = min(256, tokens)
    blocks = tokens // rows
    width = weights[0].shape[-1]
    own = pl.BlockSpec((rows, width), lambda i: (i, 0))
    return pl.pallas_call(
        ignoring(
            functools.partial(product_kernel, parts=len(parts), weights=len(weights), added=len(addends)),
            len(parts) + len(weights) + len(addends),
            len(waits),
        ),
        grid=(blocks,),
        in_specs=[pl.BlockSpec((rows, part.shape[1]), lambda i: (slot * blocks + i, 0)) for part in parts]
        + [WHOLE] * len(weights)
        + [own] * len(addends)
        + [ANYWHERE] * len(waits),
        out_specs=own,
        out_shape=jax.ShapeDtypeStruct((tokens, width), dtype),
        compiler_params=pltpu.CompilerParams(vmem_limit_bytes=VMEM),
        cost_estimate=LIGHT,
    )(*parts, *weights, *addends, *waits)


def unit_grads_kernel(me_ref, x_ref, *refs, slots, runs):
    outs = refs[slots:]
    tokens = refs[0].shape[0]
    total = None
    for k, ref in enumerate(refs[:slots]):
        part = dot_tn(x_ref[k * tokens : (k + 1) * tokens, :], ref[...])
        total = part if total is None else total + part
    low = total.astype(jnp.bfloat16)
    if len(outs) == 1:
        outs[0][...] = low
        return
    for s, ref in enumerate(outs):

        @pl.when(pl.program_id(0) // runs == s)
        def _(ref=ref):
            ref[...] = low


def unit_grads(x, slots, me, wide, split, waits=()):
    tokens, units = x.shape
    width = slots[0].shape[1]
    each = units // wide
    rows = min(512, each)
    runs = each // rows
    if split:
        out_specs = [
            pl.BlockSpec((rows, width), functools.partial(lambda i, m, s: (spot_in(i, s, runs), 0), s=s))
            for s in range(wide)
        ]
        out_shape = [jax.ShapeDtypeStruct((each, width), jnp.bfloat16)] * wide
    else:
        out_specs = pl.BlockSpec((rows, width), lambda i, m: (i, 0))
        out_shape = jax.ShapeDtypeStruct((units, width), jnp.bfloat16)
    grid_spec = pltpu.PrefetchScalarGridSpec(
        num_scalar_prefetch=1,
        grid=(units // rows,),
        in_specs=[pl.BlockSpec((tokens, rows), lambda i, m: (0, ((i // runs) ^ m[0]) * runs + i % runs))]
        + [WHOLE] * len(slots)
        + [ANYWHERE] * len(waits),
        out_specs=out_specs,
    )
    return pl.pallas_call(
        ignoring(
            functools.partial(unit_grads_kernel, slots=len(slots), runs=runs), 2 + len(slots), len(waits)
        ),
        grid_spec=grid_spec,
        out_shape=out_shape,
        compiler_params=pltpu.CompilerParams(vmem_limit_bytes=VMEM),
        cost_estimate=LIGHT,
    )(me, x, *slots, *waits)


def head_grads_kernel(me_ref, grads_ref, mixed_ref, *refs, group, wide):
    outs, low = refs[2 * group : 2 * group + wide], refs[-1]

    def give(left_ref, slots):
        tokens = slots[0].shape[0]
        total = None
        for k, ref in enumerate(slots):
            part = dot_tn(left_ref[k * tokens : (k + 1) * tokens, :], ref[...])
            total = part if total is None else total + part
        return total.astype(jnp.bfloat16)

    low[: 3 * PAIR] = give(grads_ref, refs[:group])
    low[3 * PAIR :] = give(mixed_ref, refs[group : 2 * group])
    rows = PAIR // wide
    for t in range(4):
        for s, ref in enumerate(outs):
            begin = pl.multiple_of(t * PAIR + (me_ref[0] ^ s) * rows, rows)
            ref[0, t] = low[pl.ds(begin, rows), :]


def head_grads(grads, mixed, a1, states, me, begin, wide):
    length = grads.shape[0]
    width = a1[0].shape[1]
    pairs = grads.shape[1] // (3 * PAIR)
    rows = PAIR // wide
    grid_spec = pltpu.PrefetchScalarGridSpec(
        num_scalar_prefetch=1,
        grid=(pairs,),
        in_specs=[
            pl.BlockSpec((length, 3 * PAIR), lambda p, m: (0, p)),
            pl.BlockSpec((length, PAIR), lambda p, m: (0, begin + p)),
        ]
        + [WHOLE] * (2 * len(states)),
        out_specs=[pl.BlockSpec((1, 4, rows, width), lambda p, m: (p, 0, 0, 0))] * wide,
        scratch_shapes=[pltpu.VMEM((4 * PAIR, width), jnp.bfloat16)],
    )
    return pl.pallas_call(
        functools.partial(head_grads_kernel, group=len(states), wide=wide),
        grid_spec=grid_spec,
        out_shape=[jax.ShapeDtypeStruct((pairs, 4, rows, width), jnp.bfloat16)] * wide,
        compiler_params=pltpu.CompilerParams(vmem_limit_bytes=VMEM),
        cost_estimate=LIGHT,
    )(me, grads, mixed, *a1, *states)


class Net:
    def __init__(self, wide, narrow, group):
        self.wide, self.narrow, self.group = wide, narrow, group
        self.ring = narrow // group

    def from_group(self, value, s):
        return lax.ppermute(value, "narrow", [(i, i ^ s) for i in range(self.narrow)])

    def from_ring(self, value, r):
        return self.from_group(value, r * self.group)

    def from_wide(self, value, s):
        return lax.ppermute(value, "wide", [(i, i ^ s) for i in range(self.wide)])

    def bit_order(self, turn):
        bits = self.wide.bit_length() - 1
        return [1 << ((b + turn) % bits) for b in range(bits)]

    def hops(self, unit, turn):
        return {bit: self.from_wide(unit, bit) for bit in self.bit_order(turn)}

    def spread(self, unit, turn, hops):
        pieces = {0: unit}
        for bit in self.bit_order(turn):
            more = {s ^ bit: self.from_wide(piece, bit) for s, piece in pieces.items() if s}
            pieces.update(more)
            pieces[bit] = hops[bit]
        return [pieces[s] for s in range(self.wide)]

    def scatter_wide(self, parts):
        return [parts[0]] + [self.from_wide(parts[s], s) for s in range(1, self.wide)]

    def spread_doubling(self, unit, turn):
        order, pieces = [0], [(unit[None], 0)]
        for bit in self.bit_order(turn):
            stacked = []
            for array, _ in pieces:
                if not any(array is other for other in stacked):
                    stacked.append(array)
            stacked = stacked[0] if len(stacked) == 1 else jnp.concatenate(stacked, axis=0)
            away = self.from_wide(stacked, bit)
            order = order + [s ^ bit for s in order]
            pieces = [(stacked, k) for k in range(len(pieces))] + [(away, k) for k in range(len(pieces))]
        return [pieces[order.index(s)] for s in range(self.wide)]

    def swap_wide(self, parts):
        return lax.all_to_all(parts, "wide", 0, 0, tiled=True)

    def gather_wide(self, own):
        return self.swap_wide(jnp.broadcast_to(own[None], (self.wide,) + own.shape))

    def ring_slots(self, own):
        return [own] + [self.from_ring(own, r) for r in range(1, self.ring)]

    def total(self, value):
        value = value + sum(self.from_group(value, s) for s in range(1, self.group))
        value = value + sum(self.from_ring(value, r) for r in range(1, self.ring))
        return value + sum(self.from_wide(value, s) for s in range(1, self.wide))


def by_xor(parts, me):
    bit = 1
    while bit < len(parts):
        swap = me & bit != 0
        parts = [jnp.where(swap, parts[k ^ bit], part) for k, part in enumerate(parts)]
        bit *= 2
    return parts


def hold_kernel(*refs):
    pass


def after(value, *others):
    values, tree = jax.tree.flatten(value)
    waits = jax.tree.leaves(others)
    if len(values) + len(waits) < 2 or not values:
        return value
    held = pl.pallas_call(
        hold_kernel,
        in_specs=[ANYWHERE] * (len(values) + len(waits)),
        out_specs=[ANYWHERE] * len(values),
        out_shape=[jax.ShapeDtypeStruct(one.shape, one.dtype) for one in values],
        input_output_aliases={k: k for k in range(len(values))},
        cost_estimate=LIGHT,
    )(*values, *waits)
    return jax.tree.unflatten(tree, held)


def sum_low(parts):
    return jnp.sum(parts.astype(jnp.float32), axis=0).astype(jnp.bfloat16)


class RingSum:
    def __init__(self, net, parts):
        self.net, self.parts = net, list(parts)

    def send(self):
        keep = len(self.parts) // 2
        self.gone = jnp.stack(self.parts[keep:], axis=0)
        self.arrived = self.net.from_ring(self.gone, keep)
        return self

    def add(self):
        keep = len(self.parts) // 2
        self.parts = [sum_low(jnp.stack([part, self.arrived[k]])) for k, part in enumerate(self.parts[:keep])]
        return self


def place_rows_kernel(me_ref, *refs, order, rows, wide, spots):
    out_ref = refs[-1]
    sources = [refs[k].at[at] for k, at in spots]
    places = {}
    for at, (r, t, w) in enumerate(order):
        places[r, t, w] = at
    half = sources[0].shape[0]
    for r, t, w in order:
        ref = sources[(r // half) * wide + w]
        at = jnp.int32(0)
        true_r, true_w = me_ref[0] ^ r, me_ref[1] ^ w
        first_r = {k: places[k, t, 0] for k in {key[0] for key in places}}
        for k, begin in first_r.items():
            at = jnp.where(true_r == k, begin, at)
        begin = pl.multiple_of((at + true_w) * rows, rows)
        out_ref[pl.ds(begin, rows), :] = ref[r % half, t * rows : (t + 1) * rows]


def place_rows(me, sources, order, rows, wide, waits=()):
    arrays, spots = [], []
    for array, at in sources:
        known = [k for k, other in enumerate(arrays) if other is array]
        if not known:
            arrays.append(array)
        spots.append((known[0] if known else len(arrays) - 1, at))
    return pl.pallas_call(
        ignoring(
            functools.partial(place_rows_kernel, order=order, rows=rows, wide=wide, spots=spots),
            1 + len(arrays),
            len(waits),
        ),
        in_specs=[pl.BlockSpec(memory_space=pltpu.SMEM)] + [WHOLE] * len(arrays) + [ANYWHERE] * len(waits),
        out_specs=WHOLE,
        out_shape=jax.ShapeDtypeStruct((len(order) * rows, arrays[0].shape[-1]), arrays[0].dtype),
        compiler_params=pltpu.CompilerParams(vmem_limit_bytes=VMEM),
        cost_estimate=LIGHT,
    )(me, *arrays, *waits)


def on_device(
    inputs,
    seg_ids,
    buckets,
    norm1_gain,
    norm1_shift,
    w_query,
    w_key,
    w_value,
    w_out,
    norm2_gain,
    norm2_shift,
    w_up,
    w_down,
    rel_table,
    out_grad,
    *,
    wide,
    narrow,
):
    bf16, f32 = jnp.bfloat16, jnp.float32
    tokens, width = inputs.shape
    length = seg_ids.shape[1]
    group = length // tokens
    net = Net(wide, narrow, group)
    ring = net.ring
    head_rows = w_query.shape[0]
    heads_here = rel_table.shape[1]
    piece_rows = head_rows // wide
    scale = HD ** (-0.5)
    block = min(256, tokens)
    per_slot = tokens // block
    blocks = length // block
    reach_blocks = min(blocks, -(-REACH // block) + 1)
    me_wide = lax.axis_index("wide")
    me_narrow = lax.axis_index("narrow")
    me_group = me_narrow % group
    me_ring = me_narrow // group

    def my_part(shard, axis=0):
        size = shard.shape[axis] // wide
        return lax.dynamic_slice_in_dim(shard, me_wide * size, size, axis)

    def slot(value, s):
        return value[s * tokens : (s + 1) * tokens]

    table_low = []
    left = rel_table
    for _ in range(3):
        table_low.append(lax.reduce_precision(left, 8, 7))
        left = left - table_low[-1]
    table_flat = jnp.stack(table_low, axis=0).astype(bf16).reshape(-1)
    table_row = jnp.pad(table_flat, (0, 16 * width - table_flat.size)).reshape(16, width)
    attention_quarter = my_part(jnp.stack([w_query, w_key, w_value, w_out], axis=0), 1).reshape(-1, width)
    attention_rows = attention_quarter.shape[0]
    first_parts = net.ring_slots(jnp.concatenate([attention_quarter, table_row], axis=0))
    tables = [
        jnp.sum(part[attention_rows, : table_flat.size].reshape((3,) + rel_table.shape).astype(f32), axis=0)
        for part in first_parts
    ]
    tables = by_xor(tables, me_ring)
    cut_ring = ring // 2
    attention_pieces = [
        net.spread_doubling(jnp.stack([part[:attention_rows] for part in half], axis=0), turn)
        for turn, half in enumerate([first_parts[:cut_ring], first_parts[cut_ring:]])
    ]
    ffn_own = jnp.concatenate([my_part(w_up, 1).T, my_part(w_down)], axis=0)
    unit = ffn_own.shape[0] // 2

    values_in = inputs.astype(f32)
    normed1, inverse1 = row_norm(values_in)
    a1_own = (normed1 * norm1_gain + norm1_shift).astype(bf16)
    a1_away = [net.from_group(a1_own, s) for s in range(1, group)]
    a1 = [a1_own] + a1_away
    dy_away = [net.from_group(out_grad, s) for s in range(1, group)]
    dy = [out_grad] + dy_away
    ffn_slots = net.ring_slots(after(ffn_own, first_parts[1:]))
    ffn_units = [jnp.stack([rows[k * unit : (k + 1) * unit] for rows in ffn_slots], axis=0) for k in range(2)]
    ffn_hops = [net.hops(units, k) for k, units in enumerate(ffn_units)]

    per_pair = PAIR // head_rows
    pairs = ring // per_pair
    order = [
        (p * per_pair + r, t, w)
        for p in range(pairs)
        for t in range(3)
        for r in range(per_pair)
        for w in range(wide)
    ] + [(r, 3, w) for r in range(ring) for w in range(wide)]
    cut_at = 3 * ring * wide

    me = jnp.stack([me_ring, me_wide]).astype(jnp.int32)
    sources = attention_pieces[0] + attention_pieces[1]
    w_joined = place_rows(me, sources, order[:cut_at], piece_rows, wide, dy_away + ffn_units)
    w_out_full = place_rows(me, sources, order[cut_at:], piece_rows, wide)
    column_kind = (jnp.arange(w_joined.shape[0]) // PAIR) % 3
    column_scale = jnp.where(column_kind == 0, jnp.asarray(scale, f32), jnp.asarray(1.0, f32))
    joined = project(a1, w_joined, column_scale[None])

    reach = reach_blocks * block
    one_hot = (buckets[:reach, None] == jnp.arange(rel_table.shape[0])[None, :]).astype(f32)

    table_here = jnp.concatenate([tables[r] for r in range(ring)], axis=1)
    line = jnp.dot(one_hot, table_here, precision=lax.Precision.HIGHEST, preferred_element_type=f32).T
    lines = jnp.concatenate([jnp.full((line.shape[0], block), MASKED_SCORE, f32), line], axis=1)

    segments = lax.dynamic_slice_in_dim(seg_ids, me_ring, 1, 0)[0]
    first = jnp.sum((segments[None, :] < segments[:, None]).astype(jnp.int32), axis=1)
    scalars = jnp.concatenate([me_group[None], first[::block] // block]).astype(jnp.int32)
    first = first.reshape(blocks, block)

    mixed, lse = attend(joined, first, lines, scalars, block, per_slot, ffn_units)
    mixed, ffn_hops = after((mixed, ffn_hops))
    ffn_pieces = [net.spread(units, k, ffn_hops[k]) for k, units in enumerate(ffn_units)]

    attended_part = [product([mixed], s, tokens, [w_out_full], [], bf16) for s in range(1, group)]
    attended_away = [net.from_group(part, s + 1) for s, part in enumerate(attended_part)]
    hidden_state = product([mixed], 0, tokens, [w_out_full], [inputs] + attended_away, f32)
    normed2, inverse2 = row_norm(hidden_state)
    a2_own = (normed2 * norm2_gain + norm2_shift).astype(bf16)
    a2_own, ffn_pieces = after((a2_own, ffn_pieces))
    a2 = [a2_own] + [net.from_group(a2_own, s) for s in range(1, group)]

    w_down = ffn_pieces[1]
    active, up_grad, *normed2_part = hidden_units(a2, dy, ffn_pieces[0], ffn_pieces[1])
    normed2_away = [net.from_group(normed2_part[s], s) for s in range(1, group)]
    here = jnp.zeros((1,), jnp.int32)
    down_grads = unit_grads(active, dy, me[1:], wide, False).reshape(wide, -1, width)
    down_parts = net.swap_wide(down_grads)
    state_grad, state_low, grad_gain2, grad_shift2 = norm_back(
        hidden_state, out_grad, norm2_gain, [normed2_part[0]] + normed2_away, [down_grads]
    )
    state_away = [net.from_group(state_low, s) for s in range(1, group)]
    up_grads = unit_grads(up_grad, a2, here, wide, True, [state_low])
    states = [state_low] + after(state_away, up_grads)
    mixed_grad = project(states, w_out_full, jnp.ones((1, w_out_full.shape[0]), f32))
    feed_part = [product([active], s, tokens, w_down, [], bf16, [mixed_grad]) for s in range(1, group)]
    feed_away = [net.from_group(rows, s + 1) for s, rows in enumerate(feed_part)]

    def grads_of(begin, end, waits):
        return attend_back(
            joined, mixed, mixed_grad, first, lines, lse, scalars, block, per_slot, begin, end, waits
        )

    def attention_grads(grads, begin, end, place):
        if per_pair == 1 and piece_rows % 16 == 0:
            return head_grads(grads, mixed, a1, states, place, begin, wide)
        grad_part = sum(dot_tn(slot(grads, s), rows) for s, rows in enumerate(a1)).astype(bf16).reshape(end - begin, 3, per_pair, wide, piece_rows, width)
        grad_part = jnp.transpose(grad_part, (3, 0, 2, 1, 4, 5)).reshape(wide, -1, 3, piece_rows, width)
        columns = slice(begin * PAIR, end * PAIR)
        grad_out = sum(dot_tn(slot(mixed, s)[:, columns], state) for s, state in enumerate(states)).astype(bf16)
        grad_out = jnp.moveaxis(grad_out.reshape(-1, wide, 1, piece_rows, width), 1, 0)
        whole = jnp.concatenate([grad_part, grad_out], axis=2)
        return by_xor([whole[w] for w in range(wide)], place[0])

    cut = pairs // 2
    up_parts = net.scatter_wide(up_grads)
    grads_a, lines_a = grads_of(0, cut, list(up_grads) + feed_part)
    grads_a, down_parts = after((grads_a, down_parts))
    head_a = attention_grads(grads_a, 0, cut, me[1:])
    head_a, up_parts = after((head_a, up_parts))
    parts_a = net.scatter_wide(head_a)
    down_low = sum_low(down_parts).reshape(ring, -1, width)
    up_low = sum_low(jnp.stack(up_parts)).reshape(ring, -1, width)
    ffn_low = jnp.concatenate([down_low, up_low], axis=1)
    ffn_ring = RingSum(net, [ffn_low[r] for r in range(ring)]).send()
    grads_b, lines_b = grads_of(cut, pairs, list(head_a) + [ffn_ring.gone])
    grads_b, ffn_ring.arrived, parts_a = after((grads_b, ffn_ring.arrived, parts_a))
    ffn_ring.add().send()
    head_b = attention_grads(grads_b, cut, pairs, me[1:])
    parts_b = net.scatter_wide(head_b)
    all_grads, all_lines = [grads_a, grads_b], [lines_a, lines_b]

    w_late = after(w_joined, head_b, ffn_ring.gone)

    normed1_part = [product(all_grads, s, tokens, [w_late], [], bf16) for s in range(1, group)]
    normed1_away = [net.from_group(part, s + 1) for s, part in enumerate(normed1_part)]
    w_late, ffn_ring.arrived = after((w_late, ffn_ring.arrived), normed1_part)
    normed1_own = product(all_grads, 0, tokens, [w_late], [], f32)
    parts_b = after(parts_b, normed1_own)
    head_low = jnp.concatenate([sum_low(jnp.stack(parts_a)), sum_low(jnp.stack(parts_b))], axis=0)
    head_ring = RingSum(net, by_xor([head_low[z] for z in range(ring)], me_ring)).send()
    ffn_part = after(ffn_ring.add().parts[0], head_ring.gone)
    ffn_pieces = [net.from_wide(ffn_part, s) for s in range(1, wide)]
    out = product(
        [active], 0, tokens, w_down, [hidden_state] + feed_away, bf16, [head_ring.gone, ffn_part]
    )
    input_grad, _, grad_gain1, grad_shift1 = norm_back(
        inputs, state_grad, norm1_gain, [normed1_own] + normed1_away, [out] + ffn_pieces
    )

    line_grad = jnp.concatenate(all_lines, axis=0)[:, block:]
    table_grad = jnp.dot(line_grad, one_hot, precision=lax.Precision.HIGHEST, preferred_element_type=f32)
    all_heads = heads_here * narrow
    head_ids = jnp.stack([(r * group + me_group) * heads_here + h for r in range(ring) for h in range(heads_here)])
    placed = (jnp.arange(all_heads)[:, None] == head_ids[None, :]).astype(f32)
    table_all = jnp.dot(placed, table_grad, precision=lax.Precision.HIGHEST, preferred_element_type=f32)

    small = jnp.concatenate([grad_gain1, grad_shift1, grad_gain2, grad_shift2, table_all.reshape(-1)])
    pad = -small.shape[0] % 1024
    small_own = small
    small = jnp.pad(small, (0, pad)).reshape(-1, 128)
    small = small + sum(net.from_group(small, s) for s in range(1, group))
    small = small + sum(net.from_wide(small, s) for s in range(1, wide))
    head_ring.arrived = after(head_ring.arrived, small_own)
    head_ring.add().send()
    small, head_gone = after((small, head_ring.gone))
    small = small + sum(net.from_ring(small, r) for r in range(1, ring))
    small = small.reshape(-1)
    gain1, shift1, gain2, shift2 = (small[k * width : (k + 1) * width] for k in range(4))
    table_sum = small[4 * width : 4 * width + table_all.size].reshape(table_all.shape)
    table_out = lax.dynamic_slice_in_dim(table_sum, me_narrow * heads_here, heads_here, 0).T

    attention_part = head_ring.add().parts[0]
    attention_part = jnp.broadcast_to(after(attention_part, small_own)[None], (wide,) + attention_part.shape)
    ffn_pieces = after(ffn_pieces, attention_part)
    ffn_all = jnp.stack(by_xor([ffn_part] + ffn_pieces, me_wide), axis=0)
    down_all = ffn_all[:, :unit].reshape(-1, width).astype(f32)
    up_all = ffn_all[:, unit:].reshape(-1, width).T.astype(f32)
    attention_all = net.swap_wide(attention_part)
    attention_all = jnp.moveaxis(attention_all, 1, 0).reshape(4, head_rows, width).astype(f32)
    return (
        out,
        input_grad,
        gain1,
        shift1,
        attention_all[0],
        attention_all[1],
        attention_all[2],
        attention_all[3],
        gain2,
        shift2,
        up_all,
        down_all,
        table_out,
    )


def solution(mesh):
    placed = (
        P(("wide", "narrow"), None),
        P("wide", None),
        P(),
        P(),
        P(),
        P("narrow", None),
        P("narrow", None),
        P("narrow", None),
        P("narrow", None),
        P(),
        P(),
        P(None, "narrow"),
        P("narrow", None),
        P(None, "narrow"),
        P(("wide", "narrow"), None),
    )
    return jax.shard_map(
        functools.partial(on_device, wide=mesh.shape["wide"], narrow=mesh.shape["narrow"]),
        mesh=mesh,
        in_specs=placed,
        out_specs=(
            P(("wide", "narrow"), None),
            P(("wide", "narrow"), None),
            P(),
            P(),
            P("narrow", None),
            P("narrow", None),
            P("narrow", None),
            P("narrow", None),
            P(),
            P(),
            P(None, "narrow"),
            P("narrow", None),
            P(None, "narrow"),
        ),
        check_vma=False,
    )
```

```python
import functools
import math

import jax
import jax.numpy as jnp
from jax import lax
from jax.experimental import pallas as pl
from jax.experimental.pallas import tpu as pltpu
from jax.sharding import PartitionSpec as P

HD = 64
PAIR = 128
REACH = 1024
EPSILON = 1e-05
MASKED_SCORE = -1e30
ROOT = (2.0 / 3.141592653589793) ** 0.5
VMEM = 60 * 1024 * 1024
LIGHT = pl.CostEstimate(flops=1, bytes_accessed=1, transcendentals=0)
NT = (((1,), (1,)), ((), ()))
TN = (((0,), (0,)), ((), ()))


def row_norm(values):
    mean = jnp.mean(values, axis=1, keepdims=True)
    centred = values - mean
    spread = jnp.mean(centred * centred, axis=1, keepdims=True)
    inverse = lax.rsqrt(spread + EPSILON)
    return (centred * inverse, inverse)


def norm_backward(upstream, normed, inverse, gain):
    scaled = upstream * gain
    mean_plain = jnp.mean(scaled, axis=1, keepdims=True)
    mean_cross = jnp.mean(scaled * normed, axis=1, keepdims=True)
    result = inverse * (scaled - mean_plain - normed * mean_cross)
    return (result, jnp.sum(upstream * normed, axis=0), jnp.sum(upstream, axis=0))


def dot_nt(left, right):
    return lax.dot_general(left, right, NT, preferred_element_type=jnp.float32)


def dot_nn(left, right):
    return jnp.dot(left, right, preferred_element_type=jnp.float32)


def dot_tn(left, right):
    return lax.dot_general(left, right, TN, preferred_element_type=jnp.float32)


def make_strip(line_ref, strips, begin=0):
    for h in range(strips.shape[0]):
        spread = jnp.broadcast_to(line_ref[begin + h : begin + h + 1, :], strips.shape[1:])
        strips[h] = pltpu.roll(spread, 0, 1, stride=1, stride_axis=0)


def strip_line(strip):
    rows, span = strip.shape
    while rows > 1:
        rows //= 2
        strip = strip[:rows] + pltpu.roll(strip[rows : 2 * rows], span - rows, 1)
    return strip


def strip_at(t, u, rows, block):
    return pl.ds(pl.multiple_of(t * block + (block - u * rows), rows), block)


def strip_tile(strips, h, t, block):
    rows = strips.shape[1]
    parts = [strips[h, :, strip_at(t, u, rows, block)] for u in range(block // rows)]
    return jnp.concatenate(parts, axis=0)


def add_to_strip(strips, h, t, tile):
    rows, block = strips.shape[1], tile.shape[0]
    for u in range(block // rows):
        strips[h, :, strip_at(t, u, rows, block)] += tile[u * rows : (u + 1) * rows]


def place_of(index, me, per_slot):
    return ((index // per_slot) ^ me) * per_slot + index % per_slot


def head_lanes(block, h):
    lanes = lax.broadcasted_iota(jnp.int32, block.shape, 1)
    return jnp.where((lanes // HD) == h, block, jnp.zeros_like(block))


def columns_of(p, kind):
    return slice((3 * p + kind) * PAIR, (3 * p + kind + 1) * PAIR)


def attend_kernel(scalars, x_ref, first_ref, line_ref, out_ref, lse_ref, strips, v_t, kept, *, block, per_slot):
    i = pl.program_id(0)
    me = scalars[0]
    low = scalars[1 + i]
    heads = strips.shape[0]
    pairs = heads // 2

    @pl.when(i == 0)
    def _():
        make_strip(line_ref, strips)
        for p in range(pairs):
            v_t[p * PAIR : (p + 1) * PAIR] = x_ref[:, columns_of(p, 2)].T

    rows = pl.ds(pl.multiple_of(place_of(i, me, per_slot) * block, block), block)
    own = [head_lanes(x_ref[rows, columns_of(h // 2, 0)], h % 2) for h in range(heads)]
    first = first_ref[pl.ds(i, 1), :]
    key_index = lax.broadcasted_iota(jnp.int32, (block, block), 0)

    def rows_of(t):
        return pl.ds(pl.multiple_of(place_of(i - t, me, per_slot) * block, block), block)

    def fold(value):
        return value.reshape(block // 8, 8, block)

    def score_step(t, tops):
        here = rows_of(t)
        allowed = key_index >= (first - (i - t) * block)
        result = []
        for h in range(heads):
            scores = dot_nt(x_ref[here, columns_of(h // 2, 1)], own[h]) + strip_tile(strips, h, t, block)
            scores = jnp.where(allowed, scores, MASKED_SCORE)
            kept[h, t] = scores
            result.append(jnp.maximum(tops[h], jnp.max(fold(scores), axis=0)))
        return tuple(result)

    def value_step(t, carry):
        here = rows_of(t)
        result = []
        for h in range(heads):
            total, acc = carry[h]
            expo = jnp.exp(kept[h, t] - tops[h])
            total = total + jnp.sum(fold(expo), axis=0)
            acc = acc + dot_nn(v_t[h * HD : (h + 1) * HD, here], expo.astype(jnp.bfloat16))
            result.append((total, acc))
        return tuple(result)

    tops = lax.fori_loop(
        0, i - low + 1, score_step, (jnp.full((8, block), MASKED_SCORE, jnp.float32),) * heads
    )
    tops = [jnp.max(top, axis=0, keepdims=True) for top in tops]
    zero = (jnp.zeros((8, block), jnp.float32), jnp.zeros((HD, block), jnp.float32))
    done = lax.fori_loop(0, i - low + 1, value_step, (zero,) * heads)
    totals = [jnp.sum(total, axis=0, keepdims=True) for total, _ in done]
    for p in range(pairs):
        both = jnp.concatenate([done[h][1] / totals[h] for h in (2 * p, 2 * p + 1)], axis=0)
        out_ref[rows, p * PAIR : (p + 1) * PAIR] = both.T.astype(jnp.bfloat16)
    lse_ref[pl.ds(i, 1)] = jnp.concatenate([tops[h] + jnp.log(totals[h]) for h in range(heads)], axis=0)[None]


def attend_back_kernel(
    scalars,
    x_ref,
    mixed_ref,
    up_ref,
    first_ref,
    line_ref,
    lse_ref,
    grad_ref,
    sums_ref,
    strips,
    sums,
    k_t,
    dk,
    dv,
    *,
    block,
    per_slot,
    begin,
):
    i = pl.program_id(0)
    me = scalars[0]
    low = scalars[1 + i]
    heads = strips.shape[0]
    pairs = heads // 2

    columns = columns_of

    def wide_columns(p):
        return slice(p * PAIR, (p + 1) * PAIR)

    @pl.when(i == 0)
    def _():
        make_strip(line_ref, strips, 2 * begin)
        for p in range(pairs):
            k_t[p * PAIR : (p + 1) * PAIR] = x_ref[:, columns(p, 1)].T
        dk[...] = jnp.zeros_like(dk)
        dv[...] = jnp.zeros_like(dv)
        sums[...] = jnp.zeros_like(sums)

    rows = pl.ds(pl.multiple_of(place_of(i, me, per_slot) * block, block), block)
    own_q = [head_lanes(x_ref[rows, columns(h // 2, 0)], h % 2) for h in range(heads)]
    own_up = [head_lanes(up_ref[rows, wide_columns(h // 2)], h % 2) for h in range(heads)]
    picks = lax.broadcasted_iota(jnp.int32, (8, PAIR), 1) // HD == lax.broadcasted_iota(jnp.int32, (8, PAIR), 0)
    picks = picks.astype(jnp.bfloat16)
    deltas = []
    for p in range(pairs):
        span = wide_columns(p)
        product = up_ref[rows, span].astype(jnp.float32) * mixed_ref[rows, span].astype(jnp.float32)
        high = product.astype(jnp.bfloat16)
        rest = (product - high.astype(jnp.float32)).astype(jnp.bfloat16)
        both = dot_nt(picks, high) + dot_nt(picks, rest)
        deltas += [both[0:1], both[1:2]]
    first = first_ref[pl.ds(i, 1), :]
    key_index = lax.broadcasted_iota(jnp.int32, (block, block), 0)

    def step(t, carry):
        here = pl.ds(pl.multiple_of(place_of(i - t, me, per_slot) * block, block), block)
        allowed = key_index >= (first - (i - t) * block)
        dq = []
        for p in range(pairs):
            span = slice(p * PAIR, (p + 1) * PAIR)
            keys = x_ref[here, columns(p, 1)]
            values = x_ref[here, columns(p, 2)]
            dk_new = dk[here, span]
            dv_new = dv[here, span]
            both_scores = dot_nt(keys, jnp.concatenate(own_q[2 * p : 2 * p + 2], axis=0))
            both_grads = dot_nt(values, jnp.concatenate(own_up[2 * p : 2 * p + 2], axis=0))
            for h in (2 * p, 2 * p + 1):
                half = slice((h - 2 * p) * block, (h - 2 * p + 1) * block)
                scores = both_scores[:, half] + strip_tile(strips, h, t, block)
                scores = jnp.where(allowed, scores, MASKED_SCORE)
                probs = jnp.exp(scores - lse_ref[i, 2 * begin + h : 2 * begin + h + 1, :])
                score_grad = probs * (both_grads[:, half] - deltas[h])
                add_to_strip(sums, h, t, score_grad)
                low_grad = score_grad.astype(jnp.bfloat16)
                dv_new = dv_new + dot_nn(probs.astype(jnp.bfloat16), own_up[h])
                dk_new = dk_new + dot_nn(low_grad, own_q[h])
                dq.append(carry[h] + dot_nn(k_t[h * HD : (h + 1) * HD, here], low_grad))
            dk[here, span] = dk_new
            dv[here, span] = dv_new
        return tuple(dq)

    dq = lax.fori_loop(0, i - low + 1, step, (jnp.zeros((HD, block), jnp.float32),) * heads)
    for p in range(pairs):
        both = jnp.concatenate(dq[2 * p : 2 * p + 2], axis=0).T * (HD ** (-0.5))
        grad_ref[rows, columns_of(p, 0)] = both.astype(jnp.bfloat16)

    @pl.when(i == pl.num_programs(0) - 1)
    def _():
        for p in range(pairs):
            span = slice(p * PAIR, (p + 1) * PAIR)
            grad_ref[:, columns_of(p, 1)] = dk[:, span].astype(jnp.bfloat16)
            grad_ref[:, columns_of(p, 2)] = dv[:, span].astype(jnp.bfloat16)
        for h in range(heads):
            sums_ref[h : h + 1, :] = strip_line(sums[h])


WHOLE = pl.BlockSpec(memory_space=pltpu.VMEM)
ANYWHERE = pl.BlockSpec(memory_space=pl.ANY)


def ignoring(kernel, first, count):
    def body(*refs):
        kernel(*refs[:first], *refs[first + count :])

    return body


def attend(joined, first, lines, scalars, block, per_slot, waits):
    length = joined.shape[0]
    heads, span = lines.shape
    blocks = length // block
    strip = pltpu.VMEM((heads, min(128, block), span), jnp.float32)
    grid_spec = pltpu.PrefetchScalarGridSpec(
        num_scalar_prefetch=1,
        grid=(blocks,),
        in_specs=[WHOLE] * 3 + [ANYWHERE] * len(waits),
        out_specs=[WHOLE] * 2,
        scratch_shapes=[
            strip,
            pltpu.VMEM((heads * HD, length), jnp.bfloat16),
            pltpu.VMEM((heads, span // block - 1, block, block), jnp.float32),
        ],
    )
    return pl.pallas_call(
        ignoring(functools.partial(attend_kernel, block=block, per_slot=per_slot), 4, len(waits)),
        grid_spec=grid_spec,
        out_shape=[
            jax.ShapeDtypeStruct((length, heads * HD), jnp.bfloat16),
            jax.ShapeDtypeStruct((blocks, heads, block), jnp.float32),
        ],
        compiler_params=pltpu.CompilerParams(vmem_limit_bytes=VMEM),
        cost_estimate=LIGHT,
    )(scalars, joined, first, lines, *waits)


def attend_back(joined, mixed, upstream, first, lines, lse, scalars, block, per_slot, begin, end, waits):
    length = joined.shape[0]
    span = lines.shape[1]
    heads = 2 * (end - begin)
    part = begin // (end - begin)
    blocks = length // block
    strip = pltpu.VMEM((heads, min(128, block), span), jnp.float32)
    grid_spec = pltpu.PrefetchScalarGridSpec(
        num_scalar_prefetch=1,
        grid=(blocks,),
        in_specs=[
            pl.BlockSpec((length, 3 * heads * HD), lambda i, s: (0, part)),
            pl.BlockSpec((length, heads * HD), lambda i, s: (0, part)),
            pl.BlockSpec((length, heads * HD), lambda i, s: (0, part)),
        ]
        + [WHOLE] * 3
        + [ANYWHERE] * len(waits),
        out_specs=[WHOLE] * 2,
        scratch_shapes=[
            strip,
            strip,
            pltpu.VMEM((heads * HD, length), jnp.bfloat16),
            pltpu.VMEM((length, heads * HD), jnp.float32),
            pltpu.VMEM((length, heads * HD), jnp.float32),
        ],
    )
    return pl.pallas_call(
        ignoring(
            functools.partial(attend_back_kernel, block=block, per_slot=per_slot, begin=begin), 7, len(waits)
        ),
        grid_spec=grid_spec,
        out_shape=[
            jax.ShapeDtypeStruct((length, 3 * heads * HD), jnp.bfloat16),
            jax.ShapeDtypeStruct((heads, span), jnp.float32),
        ],
        compiler_params=pltpu.CompilerParams(vmem_limit_bytes=VMEM),
        cost_estimate=LIGHT,
    )(scalars, joined, mixed, upstream, first, lines, lse, *waits)


def hidden_kernel(*refs, slots, blocks, wide, chunk):
    a2_refs, dy_refs = refs[:slots], refs[slots : 2 * slots]
    at = 2 * slots
    up_parts, down_parts = refs[at : at + wide], refs[at + wide : at + 2 * wide]
    act_ref, up_grad_ref = refs[at + 2 * wide : at + 2 * wide + 2]
    back_refs = refs[at + 2 * wide + 2 : -2]
    up_ref, down_ref = refs[-2:]

    @pl.when(pl.program_id(0) == 0)
    def _():
        each = up_ref.shape[0] // wide
        for s in range(wide):
            up_ref[s * each : (s + 1) * each, :] = up_parts[s][...].reshape(each, up_ref.shape[1])
            down_ref[s * each : (s + 1) * each, :] = down_parts[s][...].reshape(each, up_ref.shape[1])

    for s in range(slots):

        @pl.when(pl.program_id(0) // blocks == s)
        def _(s=s):
            tokens = a2_refs[s][...]
            grads = dy_refs[s][...]
            total = jnp.zeros(tokens.shape, jnp.float32)
            for begin in range(0, up_ref.shape[0], chunk):
                rows = slice(begin, begin + chunk)
                x = dot_nt(tokens, up_ref[rows, :])
                square = x * x
                bend = jnp.tanh(x * (ROOT + ROOT * 0.044715 * square))
                half = 0.5 + 0.5 * bend
                act_ref[:, rows] = (x * half).astype(jnp.bfloat16)
                slope = half + 0.5 * x * (1.0 - bend * bend) * (ROOT + 3.0 * ROOT * 0.044715 * square)
                up_grad = (dot_nt(grads, down_ref[rows, :]) * slope).astype(jnp.bfloat16)
                up_grad_ref[:, rows] = up_grad
                total = total + dot_nn(up_grad, up_ref[rows, :])
            back_refs[s][...] = total.astype(jnp.bfloat16)


def hidden_units(a2, dy, up_parts, down_parts):
    tokens, width = a2[0].shape
    slots, wide = len(a2), len(up_parts)
    units = wide * up_parts[0].shape[0] * up_parts[0].shape[1]
    block = min(256, tokens)
    blocks = tokens // block
    unit_block = pl.BlockSpec((block, units), lambda i: (i, 0))
    by_slot = [
        pl.BlockSpec((block, width), functools.partial(lambda i, s: (spot_in(i, s, blocks), 0), s=s))
        for s in range(slots)
    ]
    return pl.pallas_call(
        functools.partial(hidden_kernel, slots=slots, blocks=blocks, wide=wide, chunk=min(1024, units)),
        grid=(slots * blocks,),
        in_specs=by_slot + by_slot + [WHOLE] * (2 * wide),
        out_specs=[unit_block, unit_block] + by_slot,
        out_shape=[jax.ShapeDtypeStruct((slots * tokens, units), jnp.bfloat16)] * 2
        + [jax.ShapeDtypeStruct((tokens, width), jnp.bfloat16)] * slots,
        scratch_shapes=[pltpu.VMEM((units, width), jnp.bfloat16)] * 2,
        compiler_params=pltpu.CompilerParams(vmem_limit_bytes=VMEM),
        cost_estimate=LIGHT,
    )(*a2, *dy, *up_parts, *down_parts)


def norm_back_kernel(*refs, parts):
    values_ref, add_ref, gain_ref = refs[:3]
    part_refs = refs[3 : 3 + parts]
    out_ref, low_ref, sums_ref = refs[3 + parts :]
    values = values_ref[...].astype(jnp.float32)
    normed, inverse = row_norm(values)
    upstream = part_refs[0][...].astype(jnp.float32)
    for ref in part_refs[1:]:
        upstream = upstream + ref[...].astype(jnp.float32)
    result, gain_grad, shift_grad = norm_backward(upstream, normed, inverse, gain_ref[...])
    result = result + add_ref[...].astype(jnp.float32)
    out_ref[...] = result
    low_ref[...] = result.astype(jnp.bfloat16)

    @pl.when(pl.program_id(0) == 0)
    def _():
        sums_ref[...] = jnp.zeros_like(sums_ref)

    sums_ref[0:1, :] += gain_grad[None]
    sums_ref[1:2, :] += shift_grad[None]


def norm_back(values, add, gain, parts, waits=()):
    tokens, width = values.shape
    block = min(512, tokens)
    rows = pl.BlockSpec((block, width), lambda i: (i, 0))
    result, low, sums = pl.pallas_call(
        ignoring(functools.partial(norm_back_kernel, parts=len(parts)), 3 + len(parts), len(waits)),
        grid=(tokens // block,),
        in_specs=[rows, rows, pl.BlockSpec((1, width), lambda i: (0, 0))]
        + [rows] * len(parts)
        + [ANYWHERE] * len(waits),
        out_specs=[rows, rows, pl.BlockSpec((8, width), lambda i: (0, 0))],
        out_shape=[
            jax.ShapeDtypeStruct((tokens, width), jnp.float32),
            jax.ShapeDtypeStruct((tokens, width), jnp.bfloat16),
            jax.ShapeDtypeStruct((8, width), jnp.float32),
        ],
        compiler_params=pltpu.CompilerParams(vmem_limit_bytes=VMEM),
        cost_estimate=LIGHT,
    )(values, add, gain[None], *parts, *waits)
    return result, low, sums[0], sums[1]


def spot_in(i, slot, blocks):
    return jnp.clip(i - slot * blocks, 0, blocks - 1)


def project_kernel(*refs, blocks):
    weight_ref, scale_ref, out_ref = refs[-3:]
    for s, ref in enumerate(refs[:-3]):

        @pl.when(pl.program_id(0) // blocks == s)
        def _(ref=ref):
            out_ref[...] = (dot_nt(ref[...], weight_ref[...]) * scale_ref[...]).astype(jnp.bfloat16)


def project(slots, weight, scale):
    tokens, width = slots[0].shape
    rows = min(512, tokens)
    blocks = tokens // rows
    units = weight.shape[0]
    return pl.pallas_call(
        functools.partial(project_kernel, blocks=blocks),
        grid=(len(slots) * blocks,),
        in_specs=[
            pl.BlockSpec((rows, width), functools.partial(lambda i, s: (spot_in(i, s, blocks), 0), s=s))
            for s in range(len(slots))
        ]
        + [WHOLE, WHOLE],
        out_specs=pl.BlockSpec((rows, units), lambda i: (i, 0)),
        out_shape=jax.ShapeDtypeStruct((len(slots) * tokens, units), jnp.bfloat16),
        compiler_params=pltpu.CompilerParams(vmem_limit_bytes=VMEM),
        cost_estimate=LIGHT,
    )(*slots, weight, scale)


def product_kernel(*refs, parts, weights, added):
    sides = refs[:parts]
    weight_refs = refs[parts : parts + weights]
    out_ref = refs[-1]
    depth = min([ref.shape[1] for ref in sides] + [math.prod(ref.shape[:-1]) for ref in weight_refs])
    total = None
    for at in range(0, sum(ref.shape[1] for ref in sides), depth):
        ref, here = sides[at // sides[0].shape[1]], at % sides[0].shape[1]
        rows = math.prod(weight_refs[0].shape[:-1])
        weight_ref, there = weight_refs[at // rows], at % rows
        if len(weight_ref.shape) == 2:
            weight = weight_ref[there : there + depth, :]
        else:
            weight = weight_ref[...].reshape(rows, weight_ref.shape[-1])
        part = dot_nn(ref[:, here : here + depth], weight)
        total = part if total is None else total + part
    for ref in refs[parts + weights : parts + weights + added]:
        total = total + ref[...].astype(jnp.float32)
    out_ref[...] = total.astype(out_ref.dtype)


def product(parts, slot, tokens, weights, addends, dtype, waits=()):
    rows = min(256, tokens)
    blocks = tokens // rows
    width = weights[0].shape[-1]
    own = pl.BlockSpec((rows, width), lambda i: (i, 0))
    return pl.pallas_call(
        ignoring(
            functools.partial(product_kernel, parts=len(parts), weights=len(weights), added=len(addends)),
            len(parts) + len(weights) + len(addends),
            len(waits),
        ),
        grid=(blocks,),
        in_specs=[pl.BlockSpec((rows, part.shape[1]), lambda i: (slot * blocks + i, 0)) for part in parts]
        + [WHOLE] * len(weights)
        + [own] * len(addends)
        + [ANYWHERE] * len(waits),
        out_specs=own,
        out_shape=jax.ShapeDtypeStruct((tokens, width), dtype),
        compiler_params=pltpu.CompilerParams(vmem_limit_bytes=VMEM),
        cost_estimate=LIGHT,
    )(*parts, *weights, *addends, *waits)


def unit_grads_kernel(me_ref, x_ref, *refs, slots, runs):
    outs = refs[slots:]
    tokens = refs[0].shape[0]
    total = None
    for k, ref in enumerate(refs[:slots]):
        part = dot_tn(x_ref[k * tokens : (k + 1) * tokens, :], ref[...])
        total = part if total is None else total + part
    low = total.astype(jnp.bfloat16)
    if len(outs) == 1:
        outs[0][...] = low
        return
    for s, ref in enumerate(outs):

        @pl.when(pl.program_id(0) // runs == s)
        def _(ref=ref):
            ref[...] = low


def unit_grads(x, slots, me, wide, split, waits=()):
    tokens, units = x.shape
    width = slots[0].shape[1]
    each = units // wide
    rows = min(512, each)
    runs = each // rows
    if split:
        out_specs = [
            pl.BlockSpec((rows, width), functools.partial(lambda i, m, s: (spot_in(i, s, runs), 0), s=s))
            for s in range(wide)
        ]
        out_shape = [jax.ShapeDtypeStruct((each, width), jnp.bfloat16)] * wide
    else:
        out_specs = pl.BlockSpec((rows, width), lambda i, m: (i, 0))
        out_shape = jax.ShapeDtypeStruct((units, width), jnp.bfloat16)
    grid_spec = pltpu.PrefetchScalarGridSpec(
        num_scalar_prefetch=1,
        grid=(units // rows,),
        in_specs=[pl.BlockSpec((tokens, rows), lambda i, m: (0, ((i // runs) ^ m[0]) * runs + i % runs))]
        + [WHOLE] * len(slots)
        + [ANYWHERE] * len(waits),
        out_specs=out_specs,
    )
    return pl.pallas_call(
        ignoring(
            functools.partial(unit_grads_kernel, slots=len(slots), runs=runs), 2 + len(slots), len(waits)
        ),
        grid_spec=grid_spec,
        out_shape=out_shape,
        compiler_params=pltpu.CompilerParams(vmem_limit_bytes=VMEM),
        cost_estimate=LIGHT,
    )(me, x, *slots, *waits)


def head_grads_kernel(me_ref, grads_ref, mixed_ref, *refs, group, wide):
    outs, low = refs[2 * group : 2 * group + wide], refs[-1]

    def give(left_ref, slots):
        tokens = slots[0].shape[0]
        total = None
        for k, ref in enumerate(slots):
            part = dot_tn(left_ref[k * tokens : (k + 1) * tokens, :], ref[...])
            total = part if total is None else total + part
        return total.astype(jnp.bfloat16)

    low[: 3 * PAIR] = give(grads_ref, refs[:group])
    low[3 * PAIR :] = give(mixed_ref, refs[group : 2 * group])
    rows = PAIR // wide
    for t in range(4):
        for s, ref in enumerate(outs):
            begin = pl.multiple_of(t * PAIR + (me_ref[0] ^ s) * rows, rows)
            ref[0, t] = low[pl.ds(begin, rows), :]


def head_grads(grads, mixed, a1, states, me, begin, wide):
    length = grads.shape[0]
    width = a1[0].shape[1]
    pairs = grads.shape[1] // (3 * PAIR)
    rows = PAIR // wide
    grid_spec = pltpu.PrefetchScalarGridSpec(
        num_scalar_prefetch=1,
        grid=(pairs,),
        in_specs=[
            pl.BlockSpec((length, 3 * PAIR), lambda p, m: (0, p)),
            pl.BlockSpec((length, PAIR), lambda p, m: (0, begin + p)),
        ]
        + [WHOLE] * (2 * len(states)),
        out_specs=[pl.BlockSpec((1, 4, rows, width), lambda p, m: (p, 0, 0, 0))] * wide,
        scratch_shapes=[pltpu.VMEM((4 * PAIR, width), jnp.bfloat16)],
    )
    return pl.pallas_call(
        functools.partial(head_grads_kernel, group=len(states), wide=wide),
        grid_spec=grid_spec,
        out_shape=[jax.ShapeDtypeStruct((pairs, 4, rows, width), jnp.bfloat16)] * wide,
        compiler_params=pltpu.CompilerParams(vmem_limit_bytes=VMEM),
        cost_estimate=LIGHT,
    )(me, grads, mixed, *a1, *states)


class Net:
    def __init__(self, wide, narrow, group):
        self.wide, self.narrow, self.group = wide, narrow, group
        self.ring = narrow // group

    def from_group(self, value, s):
        return lax.ppermute(value, "narrow", [(i, i ^ s) for i in range(self.narrow)])

    def from_ring(self, value, r):
        return self.from_group(value, r * self.group)

    def from_wide(self, value, s):
        return lax.ppermute(value, "wide", [(i, i ^ s) for i in range(self.wide)])

    def bit_order(self, turn):
        bits = self.wide.bit_length() - 1
        return [1 << ((b + turn) % bits) for b in range(bits)]

    def hops(self, unit, turn):
        return {bit: self.from_wide(unit, bit) for bit in self.bit_order(turn)}

    def spread(self, unit, turn, hops):
        pieces = {0: unit}
        for bit in self.bit_order(turn):
            more = {s ^ bit: self.from_wide(piece, bit) for s, piece in pieces.items() if s}
            pieces.update(more)
            pieces[bit] = hops[bit]
        return [pieces[s] for s in range(self.wide)]

    def scatter_wide(self, parts):
        return [parts[0]] + [self.from_wide(parts[s], s) for s in range(1, self.wide)]

    def spread_doubling(self, unit, turn):
        order, pieces = [0], [(unit[None], 0)]
        for bit in self.bit_order(turn):
            stacked = []
            for array, _ in pieces:
                if not any(array is other for other in stacked):
                    stacked.append(array)
            stacked = stacked[0] if len(stacked) == 1 else jnp.concatenate(stacked, axis=0)
            away = self.from_wide(stacked, bit)
            order = order + [s ^ bit for s in order]
            pieces = [(stacked, k) for k in range(len(pieces))] + [(away, k) for k in range(len(pieces))]
        return [pieces[order.index(s)] for s in range(self.wide)]

    def swap_wide(self, parts):
        return lax.all_to_all(parts, "wide", 0, 0, tiled=True)

    def gather_wide(self, own):
        return self.swap_wide(jnp.broadcast_to(own[None], (self.wide,) + own.shape))

    def ring_slots(self, own):
        return [own] + [self.from_ring(own, r) for r in range(1, self.ring)]

    def total(self, value):
        value = value + sum(self.from_group(value, s) for s in range(1, self.group))
        value = value + sum(self.from_ring(value, r) for r in range(1, self.ring))
        return value + sum(self.from_wide(value, s) for s in range(1, self.wide))


def by_xor(parts, me):
    bit = 1
    while bit < len(parts):
        swap = me & bit != 0
        parts = [jnp.where(swap, parts[k ^ bit], part) for k, part in enumerate(parts)]
        bit *= 2
    return parts


def hold_kernel(*refs):
    pass


def after(value, *others):
    values, tree = jax.tree.flatten(value)
    waits = jax.tree.leaves(others)
    if len(values) + len(waits) < 2 or not values:
        return value
    held = pl.pallas_call(
        hold_kernel,
        in_specs=[ANYWHERE] * (len(values) + len(waits)),
        out_specs=[ANYWHERE] * len(values),
        out_shape=[jax.ShapeDtypeStruct(one.shape, one.dtype) for one in values],
        input_output_aliases={k: k for k in range(len(values))},
        cost_estimate=LIGHT,
    )(*values, *waits)
    return jax.tree.unflatten(tree, held)


def sum_low(parts):
    return jnp.sum(parts.astype(jnp.float32), axis=0).astype(jnp.bfloat16)


class RingSum:
    def __init__(self, net, parts):
        self.net, self.parts = net, list(parts)

    def send(self):
        keep = len(self.parts) // 2
        self.gone = jnp.stack(self.parts[keep:], axis=0)
        self.arrived = self.net.from_ring(self.gone, keep)
        return self

    def add(self):
        keep = len(self.parts) // 2
        self.parts = [sum_low(jnp.stack([part, self.arrived[k]])) for k, part in enumerate(self.parts[:keep])]
        return self


def place_rows_kernel(me_ref, *refs, order, rows, wide, spots):
    out_ref = refs[-1]
    sources = [refs[k].at[at] for k, at in spots]
    places = {}
    for at, (r, t, w) in enumerate(order):
        places[r, t, w] = at
    half = sources[0].shape[0]
    for r, t, w in order:
        ref = sources[(r // half) * wide + w]
        at = jnp.int32(0)
        true_r, true_w = me_ref[0] ^ r, me_ref[1] ^ w
        first_r = {k: places[k, t, 0] for k in {key[0] for key in places}}
        for k, begin in first_r.items():
            at = jnp.where(true_r == k, begin, at)
        begin = pl.multiple_of((at + true_w) * rows, rows)
        out_ref[pl.ds(begin, rows), :] = ref[r % half, t * rows : (t + 1) * rows]


def place_rows(me, sources, order, rows, wide, waits=()):
    arrays, spots = [], []
    for array, at in sources:
        known = [k for k, other in enumerate(arrays) if other is array]
        if not known:
            arrays.append(array)
        spots.append((known[0] if known else len(arrays) - 1, at))
    return pl.pallas_call(
        ignoring(
            functools.partial(place_rows_kernel, order=order, rows=rows, wide=wide, spots=spots),
            1 + len(arrays),
            len(waits),
        ),
        in_specs=[pl.BlockSpec(memory_space=pltpu.SMEM)] + [WHOLE] * len(arrays) + [ANYWHERE] * len(waits),
        out_specs=WHOLE,
        out_shape=jax.ShapeDtypeStruct((len(order) * rows, arrays[0].shape[-1]), arrays[0].dtype),
        compiler_params=pltpu.CompilerParams(vmem_limit_bytes=VMEM),
        cost_estimate=LIGHT,
    )(me, *arrays, *waits)


def on_device(
    inputs,
    seg_ids,
    buckets,
    norm1_gain,
    norm1_shift,
    w_query,
    w_key,
    w_value,
    w_out,
    norm2_gain,
    norm2_shift,
    w_up,
    w_down,
    rel_table,
    out_grad,
    *,
    wide,
    narrow,
):
    bf16, f32 = jnp.bfloat16, jnp.float32
    tokens, width = inputs.shape
    length = seg_ids.shape[1]
    group = length // tokens
    net = Net(wide, narrow, group)
    ring = net.ring
    head_rows = w_query.shape[0]
    heads_here = rel_table.shape[1]
    piece_rows = head_rows // wide
    scale = HD ** (-0.5)
    block = min(256, tokens)
    per_slot = tokens // block
    blocks = length // block
    reach_blocks = min(blocks, -(-REACH // block) + 1)
    me_wide = lax.axis_index("wide")
    me_narrow = lax.axis_index("narrow")
    me_group = me_narrow % group
    me_ring = me_narrow // group

    def my_part(shard, axis=0):
        size = shard.shape[axis] // wide
        return lax.dynamic_slice_in_dim(shard, me_wide * size, size, axis)

    def slot(value, s):
        return value[s * tokens : (s + 1) * tokens]

    table_low = []
    left = rel_table
    for _ in range(3):
        table_low.append(lax.reduce_precision(left, 8, 7))
        left = left - table_low[-1]
    table_flat = jnp.stack(table_low, axis=0).astype(bf16).reshape(-1)
    table_row = jnp.pad(table_flat, (0, 16 * width - table_flat.size)).reshape(16, width)
    attention_quarter = my_part(jnp.stack([w_query, w_key, w_value, w_out], axis=0), 1).reshape(-1, width)
    attention_rows = attention_quarter.shape[0]
    first_parts = net.ring_slots(jnp.concatenate([attention_quarter, table_row], axis=0))
    tables = [
        jnp.sum(part[attention_rows, : table_flat.size].reshape((3,) + rel_table.shape).astype(f32), axis=0)
        for part in first_parts
    ]
    tables = by_xor(tables, me_ring)
    cut_ring = ring // 2
    attention_pieces = [
        net.spread_doubling(jnp.stack([part[:attention_rows] for part in half], axis=0), turn)
        for turn, half in enumerate([first_parts[:cut_ring], first_parts[cut_ring:]])
    ]
    ffn_own = jnp.concatenate([my_part(w_up, 1).T, my_part(w_down)], axis=0)
    unit = ffn_own.shape[0] // 2

    values_in = inputs.astype(f32)
    normed1, inverse1 = row_norm(values_in)
    a1_own = (normed1 * norm1_gain + norm1_shift).astype(bf16)
    a1_away = [net.from_group(a1_own, s) for s in range(1, group)]
    a1 = [a1_own] + a1_away
    dy_away = [net.from_group(out_grad, s) for s in range(1, group)]
    dy = [out_grad] + dy_away
    ffn_slots = net.ring_slots(after(ffn_own, first_parts[1:]))
    ffn_units = [jnp.stack([rows[k * unit : (k + 1) * unit] for rows in ffn_slots], axis=0) for k in range(2)]
    ffn_hops = [net.hops(units, k) for k, units in enumerate(ffn_units)]

    per_pair = PAIR // head_rows
    pairs = ring // per_pair
    order = [
        (p * per_pair + r, t, w)
        for p in range(pairs)
        for t in range(3)
        for r in range(per_pair)
        for w in range(wide)
    ] + [(r, 3, w) for r in range(ring) for w in range(wide)]
    cut_at = 3 * ring * wide

    me = jnp.stack([me_ring, me_wide]).astype(jnp.int32)
    sources = attention_pieces[0] + attention_pieces[1]
    w_joined = place_rows(me, sources, order[:cut_at], piece_rows, wide, dy_away + ffn_units)
    w_out_full = place_rows(me, sources, order[cut_at:], piece_rows, wide)
    column_kind = (jnp.arange(w_joined.shape[0]) // PAIR) % 3
    column_scale = jnp.where(column_kind == 0, jnp.asarray(scale, f32), jnp.asarray(1.0, f32))
    joined = project(a1, w_joined, column_scale[None])

    reach = reach_blocks * block
    one_hot = (buckets[:reach, None] == jnp.arange(rel_table.shape[0])[None, :]).astype(f32)

    table_here = jnp.concatenate([tables[r] for r in range(ring)], axis=1)
    line = jnp.dot(one_hot, table_here, precision=lax.Precision.HIGHEST, preferred_element_type=f32).T
    lines = jnp.concatenate([jnp.full((line.shape[0], block), MASKED_SCORE, f32), line], axis=1)

    segments = lax.dynamic_slice_in_dim(seg_ids, me_ring, 1, 0)[0]
    first = jnp.sum((segments[None, :] < segments[:, None]).astype(jnp.int32), axis=1)
    scalars = jnp.concatenate([me_group[None], first[::block] // block]).astype(jnp.int32)
    first = first.reshape(blocks, block)

    mixed, lse = attend(joined, first, lines, scalars, block, per_slot, ffn_units)
    mixed, ffn_hops = after((mixed, ffn_hops))
    ffn_pieces = [net.spread(units, k, ffn_hops[k]) for k, units in enumerate(ffn_units)]

    attended_part = [product([mixed], s, tokens, [w_out_full], [], bf16) for s in range(1, group)]
    attended_away = [net.from_group(part, s + 1) for s, part in enumerate(attended_part)]
    hidden_state = product([mixed], 0, tokens, [w_out_full], [inputs] + attended_away, f32)
    normed2, inverse2 = row_norm(hidden_state)
    a2_own = (normed2 * norm2_gain + norm2_shift).astype(bf16)
    a2_own, ffn_pieces = after((a2_own, ffn_pieces))
    a2 = [a2_own] + [net.from_group(a2_own, s) for s in range(1, group)]

    w_down = ffn_pieces[1]
    active, up_grad, *normed2_part = hidden_units(a2, dy, ffn_pieces[0], ffn_pieces[1])
    normed2_away = [net.from_group(normed2_part[s], s) for s in range(1, group)]
    here = jnp.zeros((1,), jnp.int32)
    down_grads = unit_grads(active, dy, me[1:], wide, False).reshape(wide, -1, width)
    down_parts = net.swap_wide(down_grads)
    state_grad, state_low, grad_gain2, grad_shift2 = norm_back(
        hidden_state, out_grad, norm2_gain, [normed2_part[0]] + normed2_away, [down_grads]
    )
    state_away = [net.from_group(state_low, s) for s in range(1, group)]
    up_grads = unit_grads(up_grad, a2, here, wide, True, [state_low])
    states = [state_low] + after(state_away, up_grads)
    mixed_grad = project(states, w_out_full, jnp.ones((1, w_out_full.shape[0]), f32))
    feed_part = [product([active], s, tokens, w_down, [], bf16, [mixed_grad]) for s in range(1, group)]
    feed_away = [net.from_group(rows, s + 1) for s, rows in enumerate(feed_part)]

    def grads_of(begin, end, waits):
        return attend_back(
            joined, mixed, mixed_grad, first, lines, lse, scalars, block, per_slot, begin, end, waits
        )

    def attention_grads(grads, begin, end, place):
        if per_pair == 1 and piece_rows % 16 == 0:
            return head_grads(grads, mixed, a1, states, place, begin, wide)
        grad_part = sum(dot_tn(slot(grads, s), rows) for s, rows in enumerate(a1)).astype(bf16).reshape(end - begin, 3, per_pair, wide, piece_rows, width)
        grad_part = jnp.transpose(grad_part, (3, 0, 2, 1, 4, 5)).reshape(wide, -1, 3, piece_rows, width)
        columns = slice(begin * PAIR, end * PAIR)
        grad_out = sum(dot_tn(slot(mixed, s)[:, columns], state) for s, state in enumerate(states)).astype(bf16)
        grad_out = jnp.moveaxis(grad_out.reshape(-1, wide, 1, piece_rows, width), 1, 0)
        whole = jnp.concatenate([grad_part, grad_out], axis=2)
        return by_xor([whole[w] for w in range(wide)], place[0])

    cut = pairs // 2
    up_parts = net.scatter_wide(up_grads)
    grads_a, lines_a = grads_of(0, cut, list(up_grads) + feed_part)
    grads_a, down_parts = after((grads_a, down_parts))
    head_a = attention_grads(grads_a, 0, cut, me[1:])
    head_a, up_parts = after((head_a, up_parts))
    parts_a = net.scatter_wide(head_a)
    down_low = sum_low(down_parts).reshape(ring, -1, width)
    up_low = sum_low(jnp.stack(up_parts)).reshape(ring, -1, width)
    ffn_low = jnp.concatenate([down_low, up_low], axis=1)
    ffn_ring = RingSum(net, [ffn_low[r] for r in range(ring)]).send()
    grads_b, lines_b = grads_of(cut, pairs, list(head_a) + [ffn_ring.gone])
    grads_b, ffn_ring.arrived, parts_a = after((grads_b, ffn_ring.arrived, parts_a))
    ffn_ring.add().send()
    head_b = attention_grads(grads_b, cut, pairs, me[1:])
    parts_b = net.scatter_wide(head_b)
    all_grads, all_lines = [grads_a, grads_b], [lines_a, lines_b]

    w_late = after(w_joined, head_b, ffn_ring.gone)

    normed1_part = [product(all_grads, s, tokens, [w_late], [], bf16) for s in range(1, group)]
    normed1_away = [net.from_group(part, s + 1) for s, part in enumerate(normed1_part)]
    w_late, ffn_ring.arrived = after((w_late, ffn_ring.arrived), normed1_part)
    normed1_own = product(all_grads, 0, tokens, [w_late], [], bf16)
    parts_b = after(parts_b, normed1_own)
    head_low = jnp.concatenate([sum_low(jnp.stack(parts_a)), sum_low(jnp.stack(parts_b))], axis=0)
    head_ring = RingSum(net, by_xor([head_low[z] for z in range(ring)], me_ring)).send()
    ffn_part = after(ffn_ring.add().parts[0], head_ring.gone)
    ffn_pieces = [net.from_wide(ffn_part, s) for s in range(1, wide)]
    out = product(
        [active], 0, tokens, w_down, [hidden_state] + feed_away, bf16, [head_ring.gone, ffn_part]
    )
    input_grad, _, grad_gain1, grad_shift1 = norm_back(
        inputs, state_grad, norm1_gain, [normed1_own] + normed1_away, [out] + ffn_pieces
    )

    line_grad = jnp.concatenate(all_lines, axis=0)[:, block:]
    table_grad = jnp.dot(line_grad, one_hot, precision=lax.Precision.HIGHEST, preferred_element_type=f32)
    all_heads = heads_here * narrow
    head_ids = jnp.stack([(r * group + me_group) * heads_here + h for r in range(ring) for h in range(heads_here)])
    placed = (jnp.arange(all_heads)[:, None] == head_ids[None, :]).astype(f32)
    table_all = jnp.dot(placed, table_grad, precision=lax.Precision.HIGHEST, preferred_element_type=f32)

    small = jnp.concatenate([grad_gain1, grad_shift1, grad_gain2, grad_shift2, table_all.reshape(-1)])
    pad = -small.shape[0] % 1024
    small_own = small
    small = jnp.pad(small, (0, pad)).reshape(-1, 128)
    small = small + sum(net.from_group(small, s) for s in range(1, group))
    small_away = [net.from_wide(small, s) for s in range(1, wide)]
    head_ring.arrived = after(head_ring.arrived, small_own)
    head_ring.add().send()
    attention_part = head_ring.add().parts[0]
    attention_part = jnp.broadcast_to(attention_part[None], (wide,) + attention_part.shape)
    small = small + sum(after(small_away, attention_part))
    small = small + sum(net.from_ring(small, r) for r in range(1, ring))
    small = small.reshape(-1)
    gain1, shift1, gain2, shift2 = (small[k * width : (k + 1) * width] for k in range(4))
    table_sum = small[4 * width : 4 * width + table_all.size].reshape(table_all.shape)
    table_out = lax.dynamic_slice_in_dim(table_sum, me_narrow * heads_here, heads_here, 0).T

    ffn_pieces = after(ffn_pieces, attention_part)
    ffn_all = jnp.stack(by_xor([ffn_part] + ffn_pieces, me_wide), axis=0)
    down_all = ffn_all[:, :unit].reshape(-1, width).astype(f32)
    up_all = ffn_all[:, unit:].reshape(-1, width).T.astype(f32)
    attention_all = net.swap_wide(attention_part)
    attention_all = jnp.moveaxis(attention_all, 1, 0).reshape(4, head_rows, width).astype(f32)
    return (
        out,
        input_grad,
        gain1,
        shift1,
        attention_all[0],
        attention_all[1],
        attention_all[2],
        attention_all[3],
        gain2,
        shift2,
        up_all,
        down_all,
        table_out,
    )


def solution(mesh):
    placed = (
        P(("wide", "narrow"), None),
        P("wide", None),
        P(),
        P(),
        P(),
        P("narrow", None),
        P("narrow", None),
        P("narrow", None),
        P("narrow", None),
        P(),
        P(),
        P(None, "narrow"),
        P("narrow", None),
        P(None, "narrow"),
        P(("wide", "narrow"), None),
    )
    return jax.shard_map(
        functools.partial(on_device, wide=mesh.shape["wide"], narrow=mesh.shape["narrow"]),
        mesh=mesh,
        in_specs=placed,
        out_specs=(
            P(("wide", "narrow"), None),
            P(("wide", "narrow"), None),
            P(),
            P(),
            P("narrow", None),
            P("narrow", None),
            P("narrow", None),
            P("narrow", None),
            P(),
            P(),
            P(None, "narrow"),
            P("narrow", None),
            P(None, "narrow"),
        ),
        check_vma=False,
    )
```

```python
import functools
import math

import jax
import jax.numpy as jnp
from jax import lax
from jax.experimental import pallas as pl
from jax.experimental.pallas import tpu as pltpu
from jax.sharding import PartitionSpec as P

HD = 64
PAIR = 128
REACH = 1024
EPSILON = 1e-05
MASKED_SCORE = -1e30
ROOT = (2.0 / 3.141592653589793) ** 0.5
VMEM = 60 * 1024 * 1024
ATTEND_VMEM = 44 * 1024 * 1024
LIGHT = pl.CostEstimate(flops=1, bytes_accessed=1, transcendentals=0)
NT = (((1,), (1,)), ((), ()))
TN = (((0,), (0,)), ((), ()))


def row_norm(values):
    mean = jnp.mean(values, axis=1, keepdims=True)
    centred = values - mean
    spread = jnp.mean(centred * centred, axis=1, keepdims=True)
    inverse = lax.rsqrt(spread + EPSILON)
    return (centred * inverse, inverse)


def norm_backward(upstream, normed, inverse, gain):
    scaled = upstream * gain
    mean_plain = jnp.mean(scaled, axis=1, keepdims=True)
    mean_cross = jnp.mean(scaled * normed, axis=1, keepdims=True)
    result = inverse * (scaled - mean_plain - normed * mean_cross)
    return (result, jnp.sum(upstream * normed, axis=0), jnp.sum(upstream, axis=0))


def dot_nt(left, right):
    return lax.dot_general(left, right, NT, preferred_element_type=jnp.float32)


def dot_nn(left, right):
    return jnp.dot(left, right, preferred_element_type=jnp.float32)


def dot_tn(left, right):
    return lax.dot_general(left, right, TN, preferred_element_type=jnp.float32)


def make_strip(line_ref, strips, begin=0):
    for h in range(strips.shape[0]):
        spread = jnp.broadcast_to(line_ref[begin + h : begin + h + 1, :], strips.shape[1:])
        strips[h] = pltpu.roll(spread, 0, 1, stride=1, stride_axis=0)


def strip_line(strip):
    rows, span = strip.shape
    while rows > 1:
        rows //= 2
        strip = strip[:rows] + pltpu.roll(strip[rows : 2 * rows], span - rows, 1)
    return strip


def strip_at(t, u, rows, block):
    return pl.ds(pl.multiple_of(t * block + (block - u * rows), rows), block)


def strip_tile(strips, h, t, block):
    rows = strips.shape[1]
    parts = [strips[h, :, strip_at(t, u, rows, block)] for u in range(block // rows)]
    return jnp.concatenate(parts, axis=0)


def add_to_strip(strips, h, t, tile):
    rows, block = strips.shape[1], tile.shape[0]
    for u in range(block // rows):
        strips[h, :, strip_at(t, u, rows, block)] += tile[u * rows : (u + 1) * rows]


def place_of(index, me, per_slot):
    return ((index // per_slot) ^ me) * per_slot + index % per_slot


def head_lanes(block, h):
    lanes = lax.broadcasted_iota(jnp.int32, block.shape, 1)
    return jnp.where((lanes // HD) == h, block, jnp.zeros_like(block))


def columns_of(p, kind):
    return slice((3 * p + kind) * PAIR, (3 * p + kind + 1) * PAIR)


def attend_kernel(scalars, x_ref, first_ref, line_ref, out_ref, lse_ref, strips, v_t, kept, *, block, per_slot):
    i = pl.program_id(0)
    me = scalars[0]
    low = scalars[1 + i]
    heads = strips.shape[0]
    pairs = heads // 2

    @pl.when(i == 0)
    def _():
        make_strip(line_ref, strips)
        for p in range(pairs):
            v_t[p * PAIR : (p + 1) * PAIR] = x_ref[:, columns_of(p, 2)].T

    rows = pl.ds(pl.multiple_of(place_of(i, me, per_slot) * block, block), block)
    own = [head_lanes(x_ref[rows, columns_of(h // 2, 0)], h % 2) for h in range(heads)]
    first = first_ref[pl.ds(i, 1), :]
    key_index = lax.broadcasted_iota(jnp.int32, (block, block), 0)

    def rows_of(t):
        return pl.ds(pl.multiple_of(place_of(i - t, me, per_slot) * block, block), block)

    def fold(value):
        return value.reshape(block // 8, 8, block)

    def score_step(t, tops):
        here = rows_of(t)
        allowed = key_index >= (first - (i - t) * block)
        result = []
        for h in range(heads):
            scores = dot_nt(x_ref[here, columns_of(h // 2, 1)], own[h]) + strip_tile(strips, h, t, block)
            scores = jnp.where(allowed, scores, MASKED_SCORE)
            kept[h, t] = scores
            result.append(jnp.maximum(tops[h], jnp.max(fold(scores), axis=0)))
        return tuple(result)

    def value_step(t, carry):
        here = rows_of(t)
        result = []
        for h in range(heads):
            total, acc = carry[h]
            expo = jnp.exp(kept[h, t] - tops[h])
            total = total + jnp.sum(fold(expo), axis=0)
            acc = acc + dot_nn(v_t[h * HD : (h + 1) * HD, here], expo.astype(jnp.bfloat16))
            result.append((total, acc))
        return tuple(result)

    tops = lax.fori_loop(
        0, i - low + 1, score_step, (jnp.full((8, block), MASKED_SCORE, jnp.float32),) * heads
    )
    tops = [jnp.max(top, axis=0, keepdims=True) for top in tops]
    zero = (jnp.zeros((8, block), jnp.float32), jnp.zeros((HD, block), jnp.float32))
    done = lax.fori_loop(0, i - low + 1, value_step, (zero,) * heads)
    totals = [jnp.sum(total, axis=0, keepdims=True) for total, _ in done]
    for p in range(pairs):
        both = jnp.concatenate([done[h][1] / totals[h] for h in (2 * p, 2 * p + 1)], axis=0)
        out_ref[rows, p * PAIR : (p + 1) * PAIR] = both.T.astype(jnp.bfloat16)
    lse_ref[pl.ds(i, 1)] = jnp.concatenate([tops[h] + jnp.log(totals[h]) for h in range(heads)], axis=0)[None]


def attend_back_kernel(
    scalars,
    x_ref,
    mixed_ref,
    up_ref,
    first_ref,
    line_ref,
    lse_ref,
    grad_ref,
    sums_ref,
    strips,
    sums,
    k_t,
    dk,
    dv,
    *,
    block,
    per_slot,
    begin,
):
    i = pl.program_id(0)
    me = scalars[0]
    low = scalars[1 + i]
    heads = strips.shape[0]
    pairs = heads // 2

    columns = columns_of

    def wide_columns(p):
        return slice(p * PAIR, (p + 1) * PAIR)

    @pl.when(i == 0)
    def _():
        make_strip(line_ref, strips, 2 * begin)
        for p in range(pairs):
            k_t[p * PAIR : (p + 1) * PAIR] = x_ref[:, columns(p, 1)].T
        dk[...] = jnp.zeros_like(dk)
        dv[...] = jnp.zeros_like(dv)
        sums[...] = jnp.zeros_like(sums)

    rows = pl.ds(pl.multiple_of(place_of(i, me, per_slot) * block, block), block)
    own_q = [head_lanes(x_ref[rows, columns(h // 2, 0)], h % 2) for h in range(heads)]
    own_up = [head_lanes(up_ref[rows, wide_columns(h // 2)], h % 2) for h in range(heads)]
    picks = lax.broadcasted_iota(jnp.int32, (8, PAIR), 1) // HD == lax.broadcasted_iota(jnp.int32, (8, PAIR), 0)
    picks = picks.astype(jnp.bfloat16)
    deltas = []
    for p in range(pairs):
        span = wide_columns(p)
        product = up_ref[rows, span].astype(jnp.float32) * mixed_ref[rows, span].astype(jnp.float32)
        high = product.astype(jnp.bfloat16)
        rest = (product - high.astype(jnp.float32)).astype(jnp.bfloat16)
        both = dot_nt(picks, high) + dot_nt(picks, rest)
        deltas += [both[0:1], both[1:2]]
    first = first_ref[pl.ds(i, 1), :]
    key_index = lax.broadcasted_iota(jnp.int32, (block, block), 0)

    def step(t, carry):
        here = pl.ds(pl.multiple_of(place_of(i - t, me, per_slot) * block, block), block)
        allowed = key_index >= (first - (i - t) * block)
        dq = []
        for p in range(pairs):
            span = slice(p * PAIR, (p + 1) * PAIR)
            keys = x_ref[here, columns(p, 1)]
            values = x_ref[here, columns(p, 2)]
            dk_new = dk[here, span]
            dv_new = dv[here, span]
            both_scores = dot_nt(keys, jnp.concatenate(own_q[2 * p : 2 * p + 2], axis=0))
            both_grads = dot_nt(values, jnp.concatenate(own_up[2 * p : 2 * p + 2], axis=0))
            for h in (2 * p, 2 * p + 1):
                half = slice((h - 2 * p) * block, (h - 2 * p + 1) * block)
                scores = both_scores[:, half] + strip_tile(strips, h, t, block)
                scores = jnp.where(allowed, scores, MASKED_SCORE)
                probs = jnp.exp(scores - lse_ref[i, 2 * begin + h : 2 * begin + h + 1, :])
                score_grad = probs * (both_grads[:, half] - deltas[h])
                add_to_strip(sums, h, t, score_grad)
                low_grad = score_grad.astype(jnp.bfloat16)
                dv_new = dv_new + dot_nn(probs.astype(jnp.bfloat16), own_up[h])
                dk_new = dk_new + dot_nn(low_grad, own_q[h])
                dq.append(carry[h] + dot_nn(k_t[h * HD : (h + 1) * HD, here], low_grad))
            dk[here, span] = dk_new
            dv[here, span] = dv_new
        return tuple(dq)

    dq = lax.fori_loop(0, i - low + 1, step, (jnp.zeros((HD, block), jnp.float32),) * heads)
    for p in range(pairs):
        both = jnp.concatenate(dq[2 * p : 2 * p + 2], axis=0).T * (HD ** (-0.5))
        grad_ref[rows, columns_of(p, 0)] = both.astype(jnp.bfloat16)

    @pl.when(i == pl.num_programs(0) - 1)
    def _():
        for p in range(pairs):
            span = slice(p * PAIR, (p + 1) * PAIR)
            grad_ref[:, columns_of(p, 1)] = dk[:, span].astype(jnp.bfloat16)
            grad_ref[:, columns_of(p, 2)] = dv[:, span].astype(jnp.bfloat16)
        for h in range(heads):
            sums_ref[h : h + 1, :] = strip_line(sums[h])


WHOLE = pl.BlockSpec(memory_space=pltpu.VMEM)
ANYWHERE = pl.BlockSpec(memory_space=pl.ANY)


def ignoring(kernel, first, count):
    def body(*refs):
        kernel(*refs[:first], *refs[first + count :])

    return body


def attend(joined, first, lines, scalars, block, per_slot, waits):
    length = joined.shape[0]
    heads, span = lines.shape
    blocks = length // block
    strip = pltpu.VMEM((heads, min(128, block), span), jnp.float32)
    grid_spec = pltpu.PrefetchScalarGridSpec(
        num_scalar_prefetch=1,
        grid=(blocks,),
        in_specs=[WHOLE] * 3 + [ANYWHERE] * len(waits),
        out_specs=[WHOLE] * 2,
        scratch_shapes=[
            strip,
            pltpu.VMEM((heads * HD, length), jnp.bfloat16),
            pltpu.VMEM((heads, span // block - 1, block, block), jnp.float32),
        ],
    )
    return pl.pallas_call(
        ignoring(functools.partial(attend_kernel, block=block, per_slot=per_slot), 4, len(waits)),
        grid_spec=grid_spec,
        out_shape=[
            jax.ShapeDtypeStruct((length, heads * HD), jnp.bfloat16),
            jax.ShapeDtypeStruct((blocks, heads, block), jnp.float32),
        ],
        compiler_params=pltpu.CompilerParams(vmem_limit_bytes=ATTEND_VMEM),
        cost_estimate=LIGHT,
    )(scalars, joined, first, lines, *waits)


def attend_back(joined, mixed, upstream, first, lines, lse, scalars, block, per_slot, begin, end, waits):
    length = joined.shape[0]
    span = lines.shape[1]
    heads = 2 * (end - begin)
    part = begin // (end - begin)
    blocks = length // block
    strip = pltpu.VMEM((heads, min(128, block), span), jnp.float32)
    grid_spec = pltpu.PrefetchScalarGridSpec(
        num_scalar_prefetch=1,
        grid=(blocks,),
        in_specs=[
            pl.BlockSpec((length, 3 * heads * HD), lambda i, s: (0, part)),
            pl.BlockSpec((length, heads * HD), lambda i, s: (0, part)),
            pl.BlockSpec((length, heads * HD), lambda i, s: (0, part)),
        ]
        + [WHOLE] * 3
        + [ANYWHERE] * len(waits),
        out_specs=[WHOLE] * 2,
        scratch_shapes=[
            strip,
            strip,
            pltpu.VMEM((heads * HD, length), jnp.bfloat16),
            pltpu.VMEM((length, heads * HD), jnp.float32),
            pltpu.VMEM((length, heads * HD), jnp.float32),
        ],
    )
    return pl.pallas_call(
        ignoring(
            functools.partial(attend_back_kernel, block=block, per_slot=per_slot, begin=begin), 7, len(waits)
        ),
        grid_spec=grid_spec,
        out_shape=[
            jax.ShapeDtypeStruct((length, 3 * heads * HD), jnp.bfloat16),
            jax.ShapeDtypeStruct((heads, span), jnp.float32),
        ],
        compiler_params=pltpu.CompilerParams(vmem_limit_bytes=VMEM),
        cost_estimate=LIGHT,
    )(scalars, joined, mixed, upstream, first, lines, lse, *waits)


def hidden_kernel(*refs, slots, blocks, wide, chunk):
    a2_refs, dy_refs = refs[:slots], refs[slots : 2 * slots]
    at = 2 * slots
    up_parts, down_parts = refs[at : at + wide], refs[at + wide : at + 2 * wide]
    act_ref, up_grad_ref = refs[at + 2 * wide : at + 2 * wide + 2]
    back_refs = refs[at + 2 * wide + 2 : -2]
    up_ref, down_ref = refs[-2:]

    @pl.when(pl.program_id(0) == 0)
    def _():
        each = up_ref.shape[0] // wide
        for s in range(wide):
            up_ref[s * each : (s + 1) * each, :] = up_parts[s][...].reshape(each, up_ref.shape[1])
            down_ref[s * each : (s + 1) * each, :] = down_parts[s][...].reshape(each, up_ref.shape[1])

    for s in range(slots):

        @pl.when(pl.program_id(0) // blocks == s)
        def _(s=s):
            tokens = a2_refs[s][...]
            grads = dy_refs[s][...]
            total = jnp.zeros(tokens.shape, jnp.float32)
            for begin in range(0, up_ref.shape[0], chunk):
                rows = slice(begin, begin + chunk)
                x = dot_nt(tokens, up_ref[rows, :])
                square = x * x
                bend = jnp.tanh(x * (ROOT + ROOT * 0.044715 * square))
                half = 0.5 + 0.5 * bend
                act_ref[:, rows] = (x * half).astype(jnp.bfloat16)
                slope = half + 0.5 * x * (1.0 - bend * bend) * (ROOT + 3.0 * ROOT * 0.044715 * square)
                up_grad = (dot_nt(grads, down_ref[rows, :]) * slope).astype(jnp.bfloat16)
                up_grad_ref[:, rows] = up_grad
                total = total + dot_nn(up_grad, up_ref[rows, :])
            back_refs[s][...] = total.astype(jnp.bfloat16)


def hidden_units(a2, dy, up_parts, down_parts):
    tokens, width = a2[0].shape
    slots, wide = len(a2), len(up_parts)
    units = wide * up_parts[0].shape[0] * up_parts[0].shape[1]
    block = min(256, tokens)
    blocks = tokens // block
    unit_block = pl.BlockSpec((block, units), lambda i: (i, 0))
    by_slot = [
        pl.BlockSpec((block, width), functools.partial(lambda i, s: (spot_in(i, s, blocks), 0), s=s))
        for s in range(slots)
    ]
    return pl.pallas_call(
        functools.partial(hidden_kernel, slots=slots, blocks=blocks, wide=wide, chunk=min(1024, units)),
        grid=(slots * blocks,),
        in_specs=by_slot + by_slot + [WHOLE] * (2 * wide),
        out_specs=[unit_block, unit_block] + by_slot,
        out_shape=[jax.ShapeDtypeStruct((slots * tokens, units), jnp.bfloat16)] * 2
        + [jax.ShapeDtypeStruct((tokens, width), jnp.bfloat16)] * slots,
        scratch_shapes=[pltpu.VMEM((units, width), jnp.bfloat16)] * 2,
        compiler_params=pltpu.CompilerParams(vmem_limit_bytes=VMEM),
        cost_estimate=LIGHT,
    )(*a2, *dy, *up_parts, *down_parts)


def norm_back_kernel(*refs, parts):
    values_ref, add_ref, gain_ref = refs[:3]
    part_refs = refs[3 : 3 + parts]
    out_ref, low_ref, sums_ref = refs[3 + parts :]
    values = values_ref[...].astype(jnp.float32)
    normed, inverse = row_norm(values)
    upstream = part_refs[0][...].astype(jnp.float32)
    for ref in part_refs[1:]:
        upstream = upstream + ref[...].astype(jnp.float32)
    result, gain_grad, shift_grad = norm_backward(upstream, normed, inverse, gain_ref[...])
    result = result + add_ref[...].astype(jnp.float32)
    out_ref[...] = result
    low_ref[...] = result.astype(jnp.bfloat16)

    @pl.when(pl.program_id(0) == 0)
    def _():
        sums_ref[...] = jnp.zeros_like(sums_ref)

    sums_ref[0:1, :] += gain_grad[None]
    sums_ref[1:2, :] += shift_grad[None]


def norm_back(values, add, gain, parts, waits=()):
    tokens, width = values.shape
    block = min(512, tokens)
    rows = pl.BlockSpec((block, width), lambda i: (i, 0))
    result, low, sums = pl.pallas_call(
        ignoring(functools.partial(norm_back_kernel, parts=len(parts)), 3 + len(parts), len(waits)),
        grid=(tokens // block,),
        in_specs=[rows, rows, pl.BlockSpec((1, width), lambda i: (0, 0))]
        + [rows] * len(parts)
        + [ANYWHERE] * len(waits),
        out_specs=[rows, rows, pl.BlockSpec((8, width), lambda i: (0, 0))],
        out_shape=[
            jax.ShapeDtypeStruct((tokens, width), jnp.float32),
            jax.ShapeDtypeStruct((tokens, width), jnp.bfloat16),
            jax.ShapeDtypeStruct((8, width), jnp.float32),
        ],
        compiler_params=pltpu.CompilerParams(vmem_limit_bytes=VMEM),
        cost_estimate=LIGHT,
    )(values, add, gain[None], *parts, *waits)
    return result, low, sums[0], sums[1]


def spot_in(i, slot, blocks):
    return jnp.clip(i - slot * blocks, 0, blocks - 1)


def project_kernel(*refs, blocks):
    weight_ref, scale_ref, out_ref = refs[-3:]
    for s, ref in enumerate(refs[:-3]):

        @pl.when(pl.program_id(0) // blocks == s)
        def _(ref=ref):
            out_ref[...] = (dot_nt(ref[...], weight_ref[...]) * scale_ref[...]).astype(jnp.bfloat16)


def project(slots, weight, scale):
    tokens, width = slots[0].shape
    rows = min(512, tokens)
    blocks = tokens // rows
    units = weight.shape[0]
    return pl.pallas_call(
        functools.partial(project_kernel, blocks=blocks),
        grid=(len(slots) * blocks,),
        in_specs=[
            pl.BlockSpec((rows, width), functools.partial(lambda i, s: (spot_in(i, s, blocks), 0), s=s))
            for s in range(len(slots))
        ]
        + [WHOLE, WHOLE],
        out_specs=pl.BlockSpec((rows, units), lambda i: (i, 0)),
        out_shape=jax.ShapeDtypeStruct((len(slots) * tokens, units), jnp.bfloat16),
        compiler_params=pltpu.CompilerParams(vmem_limit_bytes=VMEM),
        cost_estimate=LIGHT,
    )(*slots, weight, scale)


def product_kernel(*refs, parts, weights, added):
    sides = refs[:parts]
    weight_refs = refs[parts : parts + weights]
    out_ref = refs[-1]
    depth = min([ref.shape[1] for ref in sides] + [math.prod(ref.shape[:-1]) for ref in weight_refs])
    total = None
    for at in range(0, sum(ref.shape[1] for ref in sides), depth):
        ref, here = sides[at // sides[0].shape[1]], at % sides[0].shape[1]
        rows = math.prod(weight_refs[0].shape[:-1])
        weight_ref, there = weight_refs[at // rows], at % rows
        if len(weight_ref.shape) == 2:
            weight = weight_ref[there : there + depth, :]
        else:
            weight = weight_ref[...].reshape(rows, weight_ref.shape[-1])
        part = dot_nn(ref[:, here : here + depth], weight)
        total = part if total is None else total + part
    for ref in refs[parts + weights : parts + weights + added]:
        total = total + ref[...].astype(jnp.float32)
    out_ref[...] = total.astype(out_ref.dtype)


def product(parts, slot, tokens, weights, addends, dtype, waits=()):
    rows = min(256, tokens)
    blocks = tokens // rows
    width = weights[0].shape[-1]
    own = pl.BlockSpec((rows, width), lambda i: (i, 0))
    return pl.pallas_call(
        ignoring(
            functools.partial(product_kernel, parts=len(parts), weights=len(weights), added=len(addends)),
            len(parts) + len(weights) + len(addends),
            len(waits),
        ),
        grid=(blocks,),
        in_specs=[pl.BlockSpec((rows, part.shape[1]), lambda i: (slot * blocks + i, 0)) for part in parts]
        + [WHOLE] * len(weights)
        + [own] * len(addends)
        + [ANYWHERE] * len(waits),
        out_specs=own,
        out_shape=jax.ShapeDtypeStruct((tokens, width), dtype),
        compiler_params=pltpu.CompilerParams(vmem_limit_bytes=VMEM),
        cost_estimate=LIGHT,
    )(*parts, *weights, *addends, *waits)


def unit_grads_kernel(me_ref, x_ref, *refs, slots, runs):
    outs = refs[slots:]
    tokens = refs[0].shape[0]
    total = None
    for k, ref in enumerate(refs[:slots]):
        part = dot_tn(x_ref[k * tokens : (k + 1) * tokens, :], ref[...])
        total = part if total is None else total + part
    low = total.astype(jnp.bfloat16)
    if len(outs) == 1:
        outs[0][...] = low
        return
    for s, ref in enumerate(outs):

        @pl.when(pl.program_id(0) // runs == s)
        def _(ref=ref):
            ref[...] = low


def unit_grads(x, slots, me, wide, split, waits=()):
    tokens, units = x.shape
    width = slots[0].shape[1]
    each = units // wide
    rows = min(512, each)
    runs = each // rows
    if split:
        out_specs = [
            pl.BlockSpec((rows, width), functools.partial(lambda i, m, s: (spot_in(i, s, runs), 0), s=s))
            for s in range(wide)
        ]
        out_shape = [jax.ShapeDtypeStruct((each, width), jnp.bfloat16)] * wide
    else:
        out_specs = pl.BlockSpec((rows, width), lambda i, m: (i, 0))
        out_shape = jax.ShapeDtypeStruct((units, width), jnp.bfloat16)
    grid_spec = pltpu.PrefetchScalarGridSpec(
        num_scalar_prefetch=1,
        grid=(units // rows,),
        in_specs=[pl.BlockSpec((tokens, rows), lambda i, m: (0, ((i // runs) ^ m[0]) * runs + i % runs))]
        + [WHOLE] * len(slots)
        + [ANYWHERE] * len(waits),
        out_specs=out_specs,
    )
    return pl.pallas_call(
        ignoring(
            functools.partial(unit_grads_kernel, slots=len(slots), runs=runs), 2 + len(slots), len(waits)
        ),
        grid_spec=grid_spec,
        out_shape=out_shape,
        compiler_params=pltpu.CompilerParams(vmem_limit_bytes=VMEM),
        cost_estimate=LIGHT,
    )(me, x, *slots, *waits)


def head_grads_kernel(me_ref, grads_ref, mixed_ref, *refs, group, wide):
    outs, low = refs[2 * group : 2 * group + wide], refs[-1]

    def give(left_ref, slots):
        tokens = slots[0].shape[0]
        total = None
        for k, ref in enumerate(slots):
            part = dot_tn(left_ref[k * tokens : (k + 1) * tokens, :], ref[...])
            total = part if total is None else total + part
        return total.astype(jnp.bfloat16)

    low[: 3 * PAIR] = give(grads_ref, refs[:group])
    low[3 * PAIR :] = give(mixed_ref, refs[group : 2 * group])
    rows = PAIR // wide
    for t in range(4):
        for s, ref in enumerate(outs):
            begin = pl.multiple_of(t * PAIR + (me_ref[0] ^ s) * rows, rows)
            ref[0, t] = low[pl.ds(begin, rows), :]


def head_grads(grads, mixed, a1, states, me, begin, wide):
    length = grads.shape[0]
    width = a1[0].shape[1]
    pairs = grads.shape[1] // (3 * PAIR)
    rows = PAIR // wide
    grid_spec = pltpu.PrefetchScalarGridSpec(
        num_scalar_prefetch=1,
        grid=(pairs,),
        in_specs=[
            pl.BlockSpec((length, 3 * PAIR), lambda p, m: (0, p)),
            pl.BlockSpec((length, PAIR), lambda p, m: (0, begin + p)),
        ]
        + [WHOLE] * (2 * len(states)),
        out_specs=[pl.BlockSpec((1, 4, rows, width), lambda p, m: (p, 0, 0, 0))] * wide,
        scratch_shapes=[pltpu.VMEM((4 * PAIR, width), jnp.bfloat16)],
    )
    return pl.pallas_call(
        functools.partial(head_grads_kernel, group=len(states), wide=wide),
        grid_spec=grid_spec,
        out_shape=[jax.ShapeDtypeStruct((pairs, 4, rows, width), jnp.bfloat16)] * wide,
        compiler_params=pltpu.CompilerParams(vmem_limit_bytes=VMEM),
        cost_estimate=LIGHT,
    )(me, grads, mixed, *a1, *states)


class Net:
    def __init__(self, wide, narrow, group):
        self.wide, self.narrow, self.group = wide, narrow, group
        self.ring = narrow // group

    def from_group(self, value, s):
        return lax.ppermute(value, "narrow", [(i, i ^ s) for i in range(self.narrow)])

    def from_ring(self, value, r):
        return self.from_group(value, r * self.group)

    def from_wide(self, value, s):
        return lax.ppermute(value, "wide", [(i, i ^ s) for i in range(self.wide)])

    def bit_order(self, turn):
        bits = self.wide.bit_length() - 1
        return [1 << ((b + turn) % bits) for b in range(bits)]

    def hops(self, unit, turn):
        return {bit: self.from_wide(unit, bit) for bit in self.bit_order(turn)}

    def spread(self, unit, turn, hops):
        pieces = {0: unit}
        for bit in self.bit_order(turn):
            more = {s ^ bit: self.from_wide(piece, bit) for s, piece in pieces.items() if s}
            pieces.update(more)
            pieces[bit] = hops[bit]
        return [pieces[s] for s in range(self.wide)]

    def scatter_wide(self, parts):
        return [parts[0]] + [self.from_wide(parts[s], s) for s in range(1, self.wide)]

    def spread_doubling(self, unit, turn):
        order, pieces = [0], [(unit[None], 0)]
        for bit in self.bit_order(turn):
            stacked = []
            for array, _ in pieces:
                if not any(array is other for other in stacked):
                    stacked.append(array)
            stacked = stacked[0] if len(stacked) == 1 else jnp.concatenate(stacked, axis=0)
            away = self.from_wide(stacked, bit)
            order = order + [s ^ bit for s in order]
            pieces = [(stacked, k) for k in range(len(pieces))] + [(away, k) for k in range(len(pieces))]
        return [pieces[order.index(s)] for s in range(self.wide)]

    def swap_wide(self, parts):
        return lax.all_to_all(parts, "wide", 0, 0, tiled=True)

    def gather_wide(self, own):
        return self.swap_wide(jnp.broadcast_to(own[None], (self.wide,) + own.shape))

    def ring_slots(self, own):
        return [own] + [self.from_ring(own, r) for r in range(1, self.ring)]

    def total(self, value):
        value = value + sum(self.from_group(value, s) for s in range(1, self.group))
        value = value + sum(self.from_ring(value, r) for r in range(1, self.ring))
        return value + sum(self.from_wide(value, s) for s in range(1, self.wide))


def by_xor(parts, me):
    bit = 1
    while bit < len(parts):
        swap = me & bit != 0
        parts = [jnp.where(swap, parts[k ^ bit], part) for k, part in enumerate(parts)]
        bit *= 2
    return parts


def hold_kernel(*refs):
    pass


def after(value, *others):
    values, tree = jax.tree.flatten(value)
    waits = jax.tree.leaves(others)
    if len(values) + len(waits) < 2 or not values:
        return value
    held = pl.pallas_call(
        hold_kernel,
        in_specs=[ANYWHERE] * (len(values) + len(waits)),
        out_specs=[ANYWHERE] * len(values),
        out_shape=[jax.ShapeDtypeStruct(one.shape, one.dtype) for one in values],
        input_output_aliases={k: k for k in range(len(values))},
        cost_estimate=LIGHT,
    )(*values, *waits)
    return jax.tree.unflatten(tree, held)


def sum_low(parts):
    return jnp.sum(parts.astype(jnp.float32), axis=0).astype(jnp.bfloat16)


class RingSum:
    def __init__(self, net, parts):
        self.net, self.parts = net, list(parts)

    def send(self):
        keep = len(self.parts) // 2
        self.gone = jnp.stack(self.parts[keep:], axis=0)
        self.arrived = self.net.from_ring(self.gone, keep)
        return self

    def add(self):
        keep = len(self.parts) // 2
        self.parts = [sum_low(jnp.stack([part, self.arrived[k]])) for k, part in enumerate(self.parts[:keep])]
        return self


def place_rows_kernel(me_ref, *refs, order, rows, wide, spots):
    out_ref = refs[-1]
    sources = [refs[k].at[at] for k, at in spots]
    places = {}
    for at, (r, t, w) in enumerate(order):
        places[r, t, w] = at
    half = sources[0].shape[0]
    for r, t, w in order:
        ref = sources[(r // half) * wide + w]
        at = jnp.int32(0)
        true_r, true_w = me_ref[0] ^ r, me_ref[1] ^ w
        first_r = {k: places[k, t, 0] for k in {key[0] for key in places}}
        for k, begin in first_r.items():
            at = jnp.where(true_r == k, begin, at)
        begin = pl.multiple_of((at + true_w) * rows, rows)
        out_ref[pl.ds(begin, rows), :] = ref[r % half, t * rows : (t + 1) * rows]


def place_rows(me, sources, order, rows, wide, waits=()):
    arrays, spots = [], []
    for array, at in sources:
        known = [k for k, other in enumerate(arrays) if other is array]
        if not known:
            arrays.append(array)
        spots.append((known[0] if known else len(arrays) - 1, at))
    return pl.pallas_call(
        ignoring(
            functools.partial(place_rows_kernel, order=order, rows=rows, wide=wide, spots=spots),
            1 + len(arrays),
            len(waits),
        ),
        in_specs=[pl.BlockSpec(memory_space=pltpu.SMEM)] + [WHOLE] * len(arrays) + [ANYWHERE] * len(waits),
        out_specs=WHOLE,
        out_shape=jax.ShapeDtypeStruct((len(order) * rows, arrays[0].shape[-1]), arrays[0].dtype),
        compiler_params=pltpu.CompilerParams(vmem_limit_bytes=VMEM),
        cost_estimate=LIGHT,
    )(me, *arrays, *waits)


def on_device(
    inputs,
    seg_ids,
    buckets,
    norm1_gain,
    norm1_shift,
    w_query,
    w_key,
    w_value,
    w_out,
    norm2_gain,
    norm2_shift,
    w_up,
    w_down,
    rel_table,
    out_grad,
    *,
    wide,
    narrow,
):
    bf16, f32 = jnp.bfloat16, jnp.float32
    tokens, width = inputs.shape
    length = seg_ids.shape[1]
    group = length // tokens
    net = Net(wide, narrow, group)
    ring = net.ring
    head_rows = w_query.shape[0]
    heads_here = rel_table.shape[1]
    piece_rows = head_rows // wide
    scale = HD ** (-0.5)
    block = min(256, tokens)
    per_slot = tokens // block
    blocks = length // block
    reach_blocks = min(blocks, -(-REACH // block) + 1)
    me_wide = lax.axis_index("wide")
    me_narrow = lax.axis_index("narrow")
    me_group = me_narrow % group
    me_ring = me_narrow // group

    def my_part(shard, axis=0):
        size = shard.shape[axis] // wide
        return lax.dynamic_slice_in_dim(shard, me_wide * size, size, axis)

    def slot(value, s):
        return value[s * tokens : (s + 1) * tokens]

    table_low = []
    left = rel_table
    for _ in range(3):
        table_low.append(lax.reduce_precision(left, 8, 7))
        left = left - table_low[-1]
    table_flat = jnp.stack(table_low, axis=0).astype(bf16).reshape(-1)
    table_row = jnp.pad(table_flat, (0, 16 * width - table_flat.size)).reshape(16, width)
    attention_quarter = my_part(jnp.stack([w_query, w_key, w_value, w_out], axis=0), 1).reshape(-1, width)
    attention_rows = attention_quarter.shape[0]
    first_parts = net.ring_slots(jnp.concatenate([attention_quarter, table_row], axis=0))
    tables = [
        jnp.sum(part[attention_rows, : table_flat.size].reshape((3,) + rel_table.shape).astype(f32), axis=0)
        for part in first_parts
    ]
    tables = by_xor(tables, me_ring)
    cut_ring = ring // 2
    attention_pieces = [
        net.spread_doubling(jnp.stack([part[:attention_rows] for part in half], axis=0), turn)
        for turn, half in enumerate([first_parts[:cut_ring], first_parts[cut_ring:]])
    ]
    ffn_own = jnp.concatenate([my_part(w_up, 1).T, my_part(w_down)], axis=0)
    unit = ffn_own.shape[0] // 2

    values_in = inputs.astype(f32)
    normed1, inverse1 = row_norm(values_in)
    a1_own = (normed1 * norm1_gain + norm1_shift).astype(bf16)
    a1_away = [net.from_group(a1_own, s) for s in range(1, group)]
    a1 = [a1_own] + a1_away
    dy_away = [net.from_group(out_grad, s) for s in range(1, group)]
    dy = [out_grad] + dy_away
    ffn_slots = net.ring_slots(after(ffn_own, first_parts[1:]))
    ffn_units = [jnp.stack([rows[k * unit : (k + 1) * unit] for rows in ffn_slots], axis=0) for k in range(2)]
    ffn_hops = [net.hops(units, k) for k, units in enumerate(ffn_units)]

    per_pair = PAIR // head_rows
    pairs = ring // per_pair
    order = [
        (p * per_pair + r, t, w)
        for p in range(pairs)
        for t in range(3)
        for r in range(per_pair)
        for w in range(wide)
    ] + [(r, 3, w) for r in range(ring) for w in range(wide)]
    cut_at = 3 * ring * wide

    me = jnp.stack([me_ring, me_wide]).astype(jnp.int32)
    sources = attention_pieces[0] + attention_pieces[1]
    w_joined = place_rows(me, sources, order[:cut_at], piece_rows, wide, dy_away + ffn_units)
    w_out_full = place_rows(me, sources, order[cut_at:], piece_rows, wide)
    column_kind = (jnp.arange(w_joined.shape[0]) // PAIR) % 3
    column_scale = jnp.where(column_kind == 0, jnp.asarray(scale, f32), jnp.asarray(1.0, f32))
    joined = project(a1, w_joined, column_scale[None])

    reach = reach_blocks * block
    one_hot = (buckets[:reach, None] == jnp.arange(rel_table.shape[0])[None, :]).astype(f32)

    table_here = jnp.concatenate([tables[r] for r in range(ring)], axis=1)
    line = jnp.dot(one_hot, table_here, precision=lax.Precision.HIGHEST, preferred_element_type=f32).T
    lines = jnp.concatenate([jnp.full((line.shape[0], block), MASKED_SCORE, f32), line], axis=1)

    segments = lax.dynamic_slice_in_dim(seg_ids, me_ring, 1, 0)[0]
    first = jnp.sum((segments[None, :] < segments[:, None]).astype(jnp.int32), axis=1)
    scalars = jnp.concatenate([me_group[None], first[::block] // block]).astype(jnp.int32)
    first = first.reshape(blocks, block)

    mixed, lse = attend(joined, first, lines, scalars, block, per_slot, ffn_units)
    mixed, ffn_hops = after((mixed, ffn_hops))
    ffn_pieces = [net.spread(units, k, ffn_hops[k]) for k, units in enumerate(ffn_units)]

    attended_part = [product([mixed], s, tokens, [w_out_full], [], bf16) for s in range(1, group)]
    attended_away = [net.from_group(part, s + 1) for s, part in enumerate(attended_part)]
    hidden_state = product([mixed], 0, tokens, [w_out_full], [inputs] + attended_away, f32)
    normed2, inverse2 = row_norm(hidden_state)
    a2_own = (normed2 * norm2_gain + norm2_shift).astype(bf16)
    a2_own, ffn_pieces = after((a2_own, ffn_pieces))
    a2 = [a2_own] + [net.from_group(a2_own, s) for s in range(1, group)]

    w_down = ffn_pieces[1]
    active, up_grad, *normed2_part = hidden_units(a2, dy, ffn_pieces[0], ffn_pieces[1])
    normed2_away = [net.from_group(normed2_part[s], s) for s in range(1, group)]
    here = jnp.zeros((1,), jnp.int32)
    down_grads = unit_grads(active, dy, me[1:], wide, False).reshape(wide, -1, width)
    down_parts = net.swap_wide(down_grads)
    state_grad, state_low, grad_gain2, grad_shift2 = norm_back(
        hidden_state, out_grad, norm2_gain, [normed2_part[0]] + normed2_away, [down_grads]
    )
    state_away = [net.from_group(state_low, s) for s in range(1, group)]
    up_grads = unit_grads(up_grad, a2, here, wide, True, [state_low])
    states = [state_low] + after(state_away, up_grads)
    mixed_grad = project(states, w_out_full, jnp.ones((1, w_out_full.shape[0]), f32))
    feed_part = [product([active], s, tokens, w_down, [], bf16, [mixed_grad]) for s in range(1, group)]
    feed_away = [net.from_group(rows, s + 1) for s, rows in enumerate(feed_part)]

    def grads_of(begin, end, waits):
        return attend_back(
            joined, mixed, mixed_grad, first, lines, lse, scalars, block, per_slot, begin, end, waits
        )

    def attention_grads(grads, begin, end, place):
        if per_pair == 1 and piece_rows % 16 == 0:
            return head_grads(grads, mixed, a1, states, place, begin, wide)
        grad_part = sum(dot_tn(slot(grads, s), rows) for s, rows in enumerate(a1)).astype(bf16).reshape(end - begin, 3, per_pair, wide, piece_rows, width)
        grad_part = jnp.transpose(grad_part, (3, 0, 2, 1, 4, 5)).reshape(wide, -1, 3, piece_rows, width)
        columns = slice(begin * PAIR, end * PAIR)
        grad_out = sum(dot_tn(slot(mixed, s)[:, columns], state) for s, state in enumerate(states)).astype(bf16)
        grad_out = jnp.moveaxis(grad_out.reshape(-1, wide, 1, piece_rows, width), 1, 0)
        whole = jnp.concatenate([grad_part, grad_out], axis=2)
        return by_xor([whole[w] for w in range(wide)], place[0])

    cut = pairs // 2
    up_parts = net.scatter_wide(up_grads)
    grads_a, lines_a = grads_of(0, cut, list(up_grads) + feed_part)
    grads_a, down_parts = after((grads_a, down_parts))
    head_a = attention_grads(grads_a, 0, cut, me[1:])
    head_a, up_parts = after((head_a, up_parts))
    parts_a = net.scatter_wide(head_a)
    down_low = sum_low(down_parts).reshape(ring, -1, width)
    up_low = sum_low(jnp.stack(up_parts)).reshape(ring, -1, width)
    ffn_low = jnp.concatenate([down_low, up_low], axis=1)
    ffn_ring = RingSum(net, [ffn_low[r] for r in range(ring)]).send()
    grads_b, lines_b = grads_of(cut, pairs, list(head_a) + [ffn_ring.gone])
    grads_b, ffn_ring.arrived, parts_a = after((grads_b, ffn_ring.arrived, parts_a))
    ffn_ring.add().send()
    head_b = attention_grads(grads_b, cut, pairs, me[1:])
    parts_b = net.scatter_wide(head_b)
    all_grads, all_lines = [grads_a, grads_b], [lines_a, lines_b]

    w_late = after(w_joined, head_b, ffn_ring.gone)

    normed1_part = [product(all_grads, s, tokens, [w_late], [], bf16) for s in range(1, group)]
    normed1_away = [net.from_group(part, s + 1) for s, part in enumerate(normed1_part)]
    w_late, ffn_ring.arrived = after((w_late, ffn_ring.arrived), normed1_part)
    normed1_own = product(all_grads, 0, tokens, [w_late], [], bf16)
    parts_b = after(parts_b, normed1_own)
    head_low = jnp.concatenate([sum_low(jnp.stack(parts_a)), sum_low(jnp.stack(parts_b))], axis=0)
    head_ring = RingSum(net, by_xor([head_low[z] for z in range(ring)], me_ring)).send()
    ffn_part = after(ffn_ring.add().parts[0], head_ring.gone)
    ffn_pieces = [net.from_wide(ffn_part, s) for s in range(1, wide)]
    out = product(
        [active], 0, tokens, w_down, [hidden_state] + feed_away, bf16, [head_ring.gone, ffn_part]
    )
    input_grad, _, grad_gain1, grad_shift1 = norm_back(
        inputs, state_grad, norm1_gain, [normed1_own] + normed1_away, [out] + ffn_pieces
    )

    line_grad = jnp.concatenate(all_lines, axis=0)[:, block:]
    table_grad = jnp.dot(line_grad, one_hot, precision=lax.Precision.HIGHEST, preferred_element_type=f32)
    all_heads = heads_here * narrow
    head_ids = jnp.stack([(r * group + me_group) * heads_here + h for r in range(ring) for h in range(heads_here)])
    placed = (jnp.arange(all_heads)[:, None] == head_ids[None, :]).astype(f32)
    table_all = jnp.dot(placed, table_grad, precision=lax.Precision.HIGHEST, preferred_element_type=f32)

    small = jnp.concatenate([grad_gain1, grad_shift1, grad_gain2, grad_shift2, table_all.reshape(-1)])
    pad = -small.shape[0] % 1024
    small_own = small
    small = jnp.pad(small, (0, pad)).reshape(-1, 128)
    small = small + sum(net.from_group(small, s) for s in range(1, group))
    small_away = [net.from_wide(small, s) for s in range(1, wide)]
    head_ring.arrived = after(head_ring.arrived, small_own)
    head_ring.add().send()
    attention_part = head_ring.add().parts[0]
    attention_part = jnp.broadcast_to(attention_part[None], (wide,) + attention_part.shape)
    small = small + sum(after(small_away, attention_part))
    small = small + sum(net.from_ring(small, r) for r in range(1, ring))
    small = small.reshape(-1)
    gain1, shift1, gain2, shift2 = (small[k * width : (k + 1) * width] for k in range(4))
    table_sum = small[4 * width : 4 * width + table_all.size].reshape(table_all.shape)
    table_out = lax.dynamic_slice_in_dim(table_sum, me_narrow * heads_here, heads_here, 0).T

    ffn_pieces = after(ffn_pieces, attention_part)
    ffn_all = jnp.stack(by_xor([ffn_part] + ffn_pieces, me_wide), axis=0)
    down_all = ffn_all[:, :unit].reshape(-1, width).astype(f32)
    up_all = ffn_all[:, unit:].reshape(-1, width).T.astype(f32)
    attention_all = net.swap_wide(attention_part)
    attention_all = jnp.moveaxis(attention_all, 1, 0).reshape(4, head_rows, width).astype(f32)
    return (
        out,
        input_grad,
        gain1,
        shift1,
        attention_all[0],
        attention_all[1],
        attention_all[2],
        attention_all[3],
        gain2,
        shift2,
        up_all,
        down_all,
        table_out,
    )


def solution(mesh):
    placed = (
        P(("wide", "narrow"), None),
        P("wide", None),
        P(),
        P(),
        P(),
        P("narrow", None),
        P("narrow", None),
        P("narrow", None),
        P("narrow", None),
        P(),
        P(),
        P(None, "narrow"),
        P("narrow", None),
        P(None, "narrow"),
        P(("wide", "narrow"), None),
    )
    return jax.shard_map(
        functools.partial(on_device, wide=mesh.shape["wide"], narrow=mesh.shape["narrow"]),
        mesh=mesh,
        in_specs=placed,
        out_specs=(
            P(("wide", "narrow"), None),
            P(("wide", "narrow"), None),
            P(),
            P(),
            P("narrow", None),
            P("narrow", None),
            P("narrow", None),
            P("narrow", None),
            P(),
            P(),
            P(None, "narrow"),
            P("narrow", None),
            P(None, "narrow"),
        ),
        check_vma=False,
    )
```
